128 devices in a mesh: exp: 32 (over x, z, core), ws: 4 (over y).
Axes of the slice: x: 4, y: 4, z: 4, core: 2. Of those that a mesh axis runs over, the one named last changes fastest.
Arguments:
- tokens: bfloat16 [16384, 1536], P(('exp', 'ws')), may hold values from -6 to 6
- cotangent: bfloat16 [16384, 1536], P(('exp', 'ws')), may hold values from -6 to 6
- seg_lengths: int32 [32, 13], P('exp'), may hold values from 1 to 256, 512 in all within a row
- parents: int32 [32, 13], P('exp'), may hold values from 0 to 11, as said below
- routes: int32 [16384, 8], P(('exp', 'ws')), may hold values from 0 to 31, all different within a row; in each aligned block of 128 rows (0 to 127, 128 to 255, ...) at most 48 rows name the same one
- norm_attn: bfloat16 [1536], P('ws'), may hold values from 0.5 to 1.5
- w_query: bfloat16 [1536, 1536], P('ws'), may hold values from -0.15625 to 0.15625
- w_key: bfloat16 [1536, 512], P('ws'), may hold values from -0.15625 to 0.15625
- w_value: bfloat16 [1536, 512], P('ws'), may hold values from -0.15625 to 0.15625
- w_out: bfloat16 [1536, 1536], P('ws'), may hold values from -1.25 to 1.25
- norm_moe: bfloat16 [1536], P('ws'), may hold values from 0.5 to 1.5
- w_router: bfloat16 [1536, 32], P('ws'), may hold values from -0.078125 to 0.078125
- w_gate: bfloat16 [32, 1536, 512], P('exp', None, 'ws'), may hold values from -0.15625 to 0.15625
- w_up: bfloat16 [32, 1536, 512], P('exp', None, 'ws'), may hold values from -0.15625 to 0.15625
- w_down: bfloat16 [32, 512, 1536], P('exp', 'ws'), may hold values from -1 to 1
Outputs:
- layer_out: bfloat16 [16384, 1536], P(('exp', 'ws'))
- grad_tokens: float32 [16384, 1536], P(('exp', 'ws'))
- grad_norm_attn: float32 [1536], P('ws')
- grad_w_query: float32 [1536, 1536], P('ws')
- grad_w_key: float32 [1536, 512], P('ws')
- grad_w_value: float32 [1536, 512], P('ws')
- grad_w_out: float32 [1536, 1536], P('ws')
- grad_norm_moe: float32 [1536], P('ws')
- grad_w_router: float32 [1536, 32], P('ws')
- grad_w_gate: float32 [32, 1536, 512], P('exp', None, 'ws')
- grad_w_up: float32 [32, 1536, 512], P('exp', None, 'ws')
- grad_w_down: float32 [32, 512, 1536], P('exp', 'ws')
The draws below stay inside these ranges and needn't reach their ends.
Inputs may be any that keep to these rules, and one draw needn't show every extreme that they name: parents[t, 0] is 0; for every other segment s, parents[t, s] is a segment before s; the parent of the last segment is segment 13 - 2. `seg_lengths`: each tree's lengths sum to 512, and the longest is 256. `routes`: each row names 8 different experts; among the 128 rows of one device no expert is named more than 48 times, and on some device one expert is named exactly 48 times.
All inputs are finite; a program needn't handle non-finite values.
Results may differ from the reference program's by a relative error of at most 0.025.
Values may be sent and summed in bfloat16 or wider, within the bound.
No kernel may reach another device: no remote copies, remote signals or barrier semaphores. Data moves between devices by JAX's collectives and lax.ppermute only.
A program may use at most 192 MiB of HBM per device.

```python
import math
import jax
import jax.numpy as jnp
import numpy as np
from jax import lax

D = 1536
HEADS = 24
KV_HEADS = 8
HEAD = 64
FF = 512
TOP = 8
NSEG = 13
TOK_DEV = 128
EXPERTS = 32
TREES = 32
TREE = 512
SEG_MOST = 256
CAP = 48
TOKENS = 16384


def draw_parents(key, part):
    limits = jnp.maximum(jnp.arange(NSEG, dtype=jnp.int32), 1)
    links = jax.random.randint(key, (TREES, NSEG), 0, limits[None, :], dtype=jnp.int32)
    links = links.at[:, NSEG - 1].set(NSEG - 2)
    return links


def shard_levels(rng, shape, cuts, least, largest):
    def one(dim, blocks):
        steps = jax.random.uniform(jax.random.fold_in(jax.random.fold_in(rng, 6), dim), (blocks,), jnp.float32, least / len(cuts), largest / len(cuts))
        return jnp.repeat(jnp.exp(steps), shape[dim] // blocks).reshape((-1,) + (1,) * (len(shape) - dim - 1))

    level = one(*cuts[0])
    for cut in cuts[1:]:
        level = level * one(*cut)
    return level


def split_up(number_of, total, limit, slope):
    weights = [(1 << 20) // math.isqrt(grade ** slope) + 1 for grade in range(2, number_of + 1)]
    surplus, holding = total - limit - (number_of - 1), [1] * (number_of - 1)
    while surplus > 0:
        movable = [i for i in range(number_of - 1) if holding[i] < limit]
        whole, remaining = sum([weights[i] for i in movable]), surplus
        for i in movable:
            extra = min(limit - holding[i], max(1, remaining * weights[i] // whole), surplus)
            holding[i] = holding[i] + extra
            surplus = surplus - extra
    return np.array([limit] + holding)


def uneven_parts(stream_key, number_of, total, bound, slope):
    if number_of == 2:
        one = jax.random.randint(stream_key, (), max(1, total - bound), min(bound, total - 1) + 1)
        return jnp.stack([one, total - one])
    tallies = jnp.asarray(split_up(number_of, total, bound, slope), jnp.int32)
    twos = (number_of - 1) // 2
    giver, sink = tallies[1:1 + 2 * twos:2], tallies[2:2 + 2 * twos:2]
    margin = jnp.minimum(giver - 1, bound - sink)
    passed = jax.random.randint(jax.random.fold_in(stream_key, 1), (twos,), 0, 1 << 20) % (margin + 1)
    tallies = tallies.at[1:1 + 2 * twos:2].set(giver - passed).at[2:2 + 2 * twos:2].set(sink + passed)
    return tallies[jax.random.permutation(jax.random.fold_in(stream_key, 2), number_of)]


def routed_block(stream_key, own, number, rows, amount, top, most, slope):
    sequence = jax.random.permutation(stream_key, amount)
    heavy_load, ordinary = portions_of(amount, rows * top, most, slope, True), portions_of(amount, rows * top, most, slope, False)
    places = jnp.arange(amount)

    def named(tallies, rotation):
        used = int((tallies > 0).sum())
        fixed = max(1, used // 4)
        moved = fixed + (places - fixed + rotation * (used - fixed)) % max(1, amount - fixed)
        return jnp.zeros((amount,), jnp.int32).at[sequence[jnp.where(places < fixed, places, moved)]].set(jnp.asarray(tallies, jnp.int32))

    tallies = jnp.where(number % 4 == 0, named(heavy_load, number // 4), named(ordinary, number - number // 4 - 1))
    mixed = jax.random.permutation(jax.random.fold_in(own, 3), amount)
    donor, taker = mixed[0:amount // 2 * 2:2], mixed[1:amount // 2 * 2:2]
    margin = jnp.minimum(tallies[donor] - 1, most - tallies[taker]) // 2
    margin = jnp.where((donor == sequence[0]) | (taker == sequence[0]) | (tallies[taker] == 0), 0, jnp.maximum(margin, 0))
    moved = jax.random.randint(jax.random.fold_in(own, 4), (amount // 2,), 0, 1 << 20) % (margin + 1)
    tallies = tallies.at[donor].add(-moved).at[taker].add(moved)
    items = jnp.searchsorted(jnp.cumsum(tallies), jnp.arange(rows * top), side="right").astype(jnp.int32)
    grid = items.reshape(top, rows).T
    grid = grid[jax.random.permutation(jax.random.fold_in(own, 1), rows)]
    rotation = jax.random.randint(jax.random.fold_in(own, 2), (rows, 1), 0, top)
    return jnp.take_along_axis(grid, (jnp.arange(top)[None, :] + rotation) % top, axis=1)


def portions_of(count, total, reach, lean, full):
    portions = [(1 << 20) // math.isqrt(standing ** lean) + 1 for standing in range(1, count + 1)]
    largest = reach if full else min(reach, max(-(-total // count), total * portions[0] // sum(portions)))
    least = 1 if total - largest >= count - 1 else 0
    given, spare = [largest] + [least] * (count - 1), total - largest - least * (count - 1)
    while spare > 0:
        free = [i for i in range(1, count) if given[i] < largest] or [i for i in range(1, count) if given[i] < reach]
        mass, budget = sum([portions[i] for i in free]), spare
        for i in free:
            addition = min(reach - given[i], max(1, budget * portions[i] // mass), spare)
            given[i] = given[i] + addition
            spare = spare - addition
    return np.array(given)


def centred(stream_key, shape, width, most, shards=(), kind=jnp.bfloat16):
    values = jax.random.normal(stream_key, shape, jnp.float32) * width
    if len(shards) > 0:
        values = shard_levels(stream_key, shape, shards, -0.22, 0.18) * values
    return jnp.clip(values, min=-most, max=most).astype(kind)


def setup_inputs(seed: int = 0) -> dict:
    seeds = jax.random.split(jax.random.key(seed), 16)
    tokens = centred(seeds[0], (TOKENS, D), 1.0, 6.0, ((0, 128),))
    cotangent = centred(seeds[1], (TOKENS, D), 1.0, 6.0, ((0, 128),))
    seg_lengths = jax.vmap(lambda own: uneven_parts(own, NSEG, TREE, SEG_MOST, 1))(jax.random.split(seeds[2], TREES)).reshape((TREES, NSEG)).astype(jnp.int32)
    parents = draw_parents(jax.random.fold_in(seeds[15], 71), 0)
    routes_keys = jax.random.split(jax.random.fold_in(seeds[4], 1), TOKENS // TOK_DEV)
    routes_turns = jax.random.permutation(jax.random.fold_in(seeds[4], 3), TOKENS // TOK_DEV)
    routes = jax.vmap(lambda own, number: routed_block(jax.random.fold_in(seeds[4], 2), own, number, TOK_DEV, EXPERTS, TOP, CAP, 2))(routes_keys, routes_turns).reshape((TOKENS, TOP))
    norm_attn = jnp.clip(1.0 + 0.1 * jax.random.normal(seeds[5], (D,), jnp.float32), 0.5, 1.5).astype(jnp.bfloat16)
    w_query = centred(seeds[6], (D, HEADS * HEAD), D ** -0.5, 0.15625, ((0, 4),))
    w_key = centred(seeds[7], (D, KV_HEADS * HEAD), D ** -0.5, 0.15625, ((0, 4),))
    w_value = centred(seeds[8], (D, KV_HEADS * HEAD), D ** -0.5, 0.15625, ((0, 4),))
    w_out = centred(seeds[9], (HEADS * HEAD, D), (max(HEADS * HEAD // 64, 4)) ** -0.5, 1.25, ((0, 4),))
    norm_moe = jnp.clip(1.0 + 0.1 * jax.random.normal(seeds[10], (D,), jnp.float32), 0.5, 1.5).astype(jnp.bfloat16)
    w_router = centred(seeds[11], (D, EXPERTS), (4 * D) ** -0.5, 0.078125, ((0, 4),))
    w_gate = centred(seeds[12], (EXPERTS, D, FF), D ** -0.5, 0.15625, ((0, 32), (2, 4)))
    w_up = centred(seeds[13], (EXPERTS, D, FF), D ** -0.5, 0.15625, ((0, 32), (2, 4)))
    w_down = centred(seeds[14], (EXPERTS, FF, D), (FF // 16) ** -0.5, 1.0, ((0, 32), (1, 4)))
    return {"tokens": tokens, "cotangent": cotangent, "seg_lengths": seg_lengths, "parents": parents, "routes": routes, "norm_attn": norm_attn, "w_query": w_query, "w_key": w_key, "w_value": w_value, "w_out": w_out, "norm_moe": norm_moe, "w_router": w_router, "w_gate": w_gate, "w_up": w_up, "w_down": w_down}


EPS = 1e-06
THETA = 10000.0
MASKED = -1e+30

@jax.custom_vjp
def low(v):
    return lax.optimization_barrier(v.astype(jnp.bfloat16)).astype(jnp.float32)

@jax.custom_vjp
def low_back(v):
    return v

def low_keep(v):
    return (low(v), None)

def low_pass(kept, grad):
    return (grad,)

def back_keep(v):
    return (v, None)

def back_low(kept, grad):
    return (low(grad),)
low.defvjp(low_keep, low_pass)
low_back.defvjp(back_keep, back_low)

def tree_layout(lengths, parents, tree_size):
    seg_count = lengths.shape[0]
    labels = jnp.arange(seg_count, dtype=jnp.int32)
    segment_end = jnp.cumsum(lengths, dtype=jnp.int32)
    starts = segment_end - lengths
    token_index = jnp.arange(tree_size, dtype=jnp.int32)
    segment = lax.optimization_barrier(jnp.sum((token_index[:, None] >= segment_end[None, :]).astype(jnp.int32), axis=1, dtype=jnp.int32))
    current = labels
    ancestry = (current[:, None] == labels[None, :]).astype(jnp.int32)
    for repeat in range(seg_count - 1):
        current = lax.optimization_barrier(jnp.sum(jnp.where(current[:, None] == labels[None, :], parents[None, :], 0), axis=1, dtype=jnp.int32))
        ancestry = jnp.maximum(ancestry, (current[:, None] == labels[None, :]).astype(jnp.int32))
    above_count = lax.optimization_barrier(jnp.sum(ancestry * lengths[None, :], axis=1, dtype=jnp.int32)) - lengths
    members = (segment[:, None] == labels[None, :]).astype(jnp.int32)
    position = lax.optimization_barrier(jnp.sum(members * (above_count - starts)[None, :], axis=1, dtype=jnp.int32)) + token_index
    reaches = ancestry[segment]
    return (members, reaches, position)

def angles_for(position, head_size):
    middle = head_size // 2
    inverse = THETA ** (-jnp.arange(middle, dtype=jnp.float32) * 2.0 / head_size)
    angles = position.astype(jnp.float32)[:, None] * inverse[None, :]
    return (jnp.cos(angles), jnp.sin(angles))

def turn_forward(vectors, cosines, sines):
    middle = vectors.shape[-1] // 2
    first_half = vectors[..., :middle]
    second_half = vectors[..., middle:]
    cosines = cosines[:, None, :]
    sines = sines[:, None, :]
    return jnp.concatenate([first_half * cosines - second_half * sines, second_half * cosines + first_half * sines], axis=-1)

def root_norm(values, gain):
    scale = lax.rsqrt(lax.optimization_barrier(jnp.mean(values * values, axis=-1, keepdims=True)) + EPS)
    return values * scale * gain

def expert_block(block_items, gate_w, up_w, down_w):
    normed, route_rows, gate_rows = block_items
    flat_routes = route_rows.reshape(-1)
    pair_count = flat_routes.shape[0]
    labels = jnp.arange(EXPERTS, dtype=jnp.int32)
    onehot = (flat_routes[:, None] == labels[None, :]).astype(jnp.int32)
    slot_rank = lax.optimization_barrier(jnp.sum((jnp.cumsum(onehot, axis=0, dtype=jnp.int32) - onehot) * onehot, axis=1, dtype=jnp.int32))
    target = flat_routes * CAP + slot_rank
    source = jnp.full((EXPERTS * CAP,), pair_count, jnp.int32).at[target].set(jnp.arange(pair_count, dtype=jnp.int32))
    filled = source < pair_count
    token_of = jnp.minimum(source // TOP, TOK_DEV - 1)
    rows_in = jnp.where(filled[:, None], normed[token_of], 0.0)
    rows_in = low_back(rows_in).reshape(EXPERTS, CAP, D)
    gate_pre = low_back(jnp.einsum('ecd,edf->ecf', rows_in, gate_w, precision=lax.Precision.HIGHEST))
    up_pre = low_back(jnp.einsum('ecd,edf->ecf', rows_in, up_w, precision=lax.Precision.HIGHEST))
    hidden = low(jax.nn.silu(gate_pre) * up_pre)
    result = low_back(low(jnp.einsum('ecf,efd->ecd', hidden, down_w, precision=lax.Precision.HIGHEST)))
    pair_rows = result.reshape(EXPERTS * CAP, D)[target].reshape(TOK_DEV, TOP, D)
    return lax.optimization_barrier(jnp.sum(gate_rows[:, :, None] * pair_rows, axis=1))

def reference(tokens, cotangent, seg_lengths, parents, routes, norm_attn, w_query, w_key, w_value, w_out, norm_moe, w_router, w_gate, w_up, w_down):
    tree_count = seg_lengths.shape[0]
    seg_count = seg_lengths.shape[1]
    total_rows = tokens.shape[0]
    tree_size = total_rows // tree_count
    members, reaches, positions = jax.vmap(lambda lengths, links: tree_layout(lengths, links, tree_size))(seg_lengths, parents)
    cosines, sines = angles_for(positions.reshape(-1), HEAD)
    group_size = HEADS // KV_HEADS
    score_scale = HEAD ** (-0.5)
    token_index = jnp.arange(tree_size, dtype=jnp.int32)
    seg_labels = jnp.arange(seg_count, dtype=jnp.int32)
    block_count = total_rows // TOK_DEV

    def tree_attention(tree_items):
        queries, key_rows, value_rows, member_rows, reach_rows = tree_items
        key_segment = lax.optimization_barrier(jnp.sum(member_rows * seg_labels[None, :], axis=1, dtype=jnp.int32))
        visible = (reach_rows[:, key_segment] > 0) & (token_index[None, :] <= token_index[:, None])
        grouped = queries.reshape(tree_size, KV_HEADS, group_size, HEAD)
        scores = jnp.einsum('tkgd,skd->kgts', grouped, key_rows, precision=lax.Precision.HIGHEST) * score_scale
        scores = low_back(jnp.where(visible[None, None], scores, MASKED))
        attention = low(jax.nn.softmax(scores, axis=-1))
        mixed_heads = jnp.einsum('kgts,skd->tkgd', attention, value_rows, precision=lax.Precision.HIGHEST)
        return mixed_heads.reshape(tree_size, HEADS * HEAD)

    def layer(resid, gain_attn, wq_full, wk_full, wv_full, wo_full, gain_moe, wr_full, wg_full, wu_full, wd_full):
        normed_one = low(root_norm(resid, gain_attn))
        query_pre = low_back(jnp.dot(normed_one, wq_full, precision=lax.Precision.HIGHEST))
        key_pre = low_back(jnp.dot(normed_one, wk_full, precision=lax.Precision.HIGHEST))
        value_rows = low_back(low(jnp.dot(normed_one, wv_full, precision=lax.Precision.HIGHEST)))
        queries = low(turn_forward(query_pre.reshape(total_rows, HEADS, HEAD), cosines, sines))
        key_rows = low(turn_forward(key_pre.reshape(total_rows, KV_HEADS, HEAD), cosines, sines))
        mixed_heads = lax.map(jax.checkpoint(tree_attention), (queries.reshape(tree_count, tree_size, HEADS, HEAD), key_rows.reshape(tree_count, tree_size, KV_HEADS, HEAD), value_rows.reshape(tree_count, tree_size, KV_HEADS, HEAD), members, reaches))
        mixed_heads = low_back(low(mixed_heads.reshape(total_rows, HEADS * HEAD)))
        resid_two = resid + low_back(jnp.dot(mixed_heads, wo_full, precision=lax.Precision.HIGHEST))
        normed_two = low(root_norm(resid_two, gain_moe))
        logits = jnp.dot(normed_two, wr_full, precision=lax.Precision.HIGHEST)
        gates = jax.nn.softmax(jnp.take_along_axis(logits, routes, axis=1), axis=-1)

        def run_block(block_items):
            return jax.checkpoint(expert_block)(block_items, wg_full, wu_full, wd_full)
        expert_sum = lax.map(run_block, (normed_two.reshape(block_count, TOK_DEV, D), routes.reshape(block_count, TOK_DEV, TOP), gates.reshape(block_count, TOK_DEV, TOP)))
        return resid_two + expert_sum.reshape(total_rows, D)
    final, pullback = jax.vjp(layer, tokens.astype(jnp.float32), norm_attn.astype(jnp.float32), w_query.astype(jnp.float32), w_key.astype(jnp.float32), w_value.astype(jnp.float32), w_out.astype(jnp.float32), norm_moe.astype(jnp.float32), w_router.astype(jnp.float32), w_gate.astype(jnp.float32), w_up.astype(jnp.float32), w_down.astype(jnp.float32))
    grad_tokens, grad_norm_attn, grad_w_query, grad_w_key, grad_w_value, grad_w_out, grad_norm_moe, grad_w_router, grad_w_gate, grad_w_up, grad_w_down = pullback(cotangent.astype(jnp.float32))
    return (final.astype(jnp.bfloat16), grad_tokens, grad_norm_attn, grad_w_query, grad_w_key, grad_w_value, grad_w_out, grad_norm_moe, grad_w_router, grad_w_gate, grad_w_up, grad_w_down)
```

```python
import jax
import jax.numpy as jnp
from jax import lax
from jax.sharding import PartitionSpec as P

HEADS = 24
KV_HEADS = 8
HEAD = 64
EPS = 1e-06
THETA = 10000.0
MASKED = -1e30
BF = jnp.bfloat16
F32 = jnp.float32
WS = 4
CHIPS = 16
CAP = 48


def dot(a, b):
    return jnp.dot(a, b, preferred_element_type=F32)


def dot_t(a, b):
    return lax.dot_general(a, b, (((1,), (1,)), ((), ())), preferred_element_type=F32)


def tdot(a, b):
    return lax.dot_general(a, b, (((0,), (0,)), ((), ())), preferred_element_type=F32)


def split(v):
    hi = v.astype(BF)
    return hi, (v - hi.astype(F32)).astype(BF)


def from_peer(v, k):
    return lax.ppermute(v, "ws", [(s, (s - k) % WS) for s in range(WS)])


def to_peer(v, k):
    return lax.ppermute(v, "ws", [(s, (s + k) % WS) for s in range(WS)])


def other_core(v):
    return lax.ppermute(v, "exp", [(s, s ^ 1) for s in range(2 * CHIPS)])


def same_core(v):
    groups = [[2 * chip + core for chip in range(CHIPS)] for core in range(2)]
    return lax.all_to_all(v, "exp", 0, 0, tiled=True, axis_index_groups=groups)


def tree_layout(lengths, parents, token_index):
    seg = lengths.shape[0]
    labels = jnp.arange(seg, dtype=jnp.int32)
    segment_end = jnp.cumsum(lengths, dtype=jnp.int32)
    starts = segment_end - lengths
    segment = jnp.sum((token_index[:, None] >= segment_end[None, :]).astype(jnp.int32), axis=1)
    reach = ((parents[:, None] == labels[None, :]) | (labels[:, None] == labels[None, :])).astype(
        BF
    )
    for _ in range(4):
        reach = (dot(reach, reach) > 0.5).astype(BF)
    above = jnp.sum(reach.astype(jnp.int32) * lengths[None, :], axis=1) - lengths
    members = segment[:, None] == labels[None, :]
    position = jnp.sum(jnp.where(members, (above - starts)[None, :], 0), axis=1) + token_index
    members = members.astype(BF)
    reaches = dot(members, reach).astype(BF)
    visible = (dot_t(reaches, members) > 0.5) & (token_index[None, :] <= token_index[:, None])
    return visible, position


def rope(vectors, cosines, sines, sign):
    rows, width = vectors.shape
    v = vectors.reshape(rows, width // HEAD, HEAD)
    a, b = v[..., : HEAD // 2], v[..., HEAD // 2 :]
    c, s = cosines[:, None, :], sines[:, None, :] * sign
    return jnp.concatenate([a * c - b * s, b * c + a * s], axis=-1).reshape(rows, width)


def norm_back(resid, scale, gain, slope):
    gain_slope = jnp.sum(slope * resid * scale, axis=0)
    inner = jnp.mean(gain * slope * resid, axis=-1, keepdims=True)
    return scale * gain * slope - resid * scale * scale * scale * inner, gain_slope


def masked_softmax(logits, mask):
    top = jnp.max(jnp.where(mask, logits, MASKED), axis=-1, keepdims=True)
    lifted = jnp.where(mask, jnp.exp(jnp.where(mask, logits, MASKED) - top), 0.0)
    return lifted / jnp.maximum(jnp.sum(lifted, axis=-1, keepdims=True), 1e-30)


def shards(
    tokens,
    cotangent,
    seg_lengths,
    parents,
    routes,
    norm_attn,
    w_query,
    w_key,
    w_value,
    w_out,
    norm_moe,
    w_router,
    w_gate,
    w_up,
    w_down,
):
    me = lax.axis_index("ws")
    expert = lax.axis_index("exp")
    core = expert % 2
    rows, width = tokens.shape
    tree = rows * WS
    shard = width // WS
    experts = 2 * CHIPS
    group = HEADS // KV_HEADS
    my_heads = HEADS // WS
    my_kv = KV_HEADS // WS
    q_w, kv_w = my_heads * HEAD, my_kv * HEAD
    slots = experts * CAP

    def gathered(v):
        return [v] + [from_peer(v, k) for k in (1, 2, 3)]

    def absolute(parts):
        out = jnp.zeros((WS,) + parts[0].shape, parts[0].dtype)
        for r, part in enumerate(parts):
            out = lax.dynamic_update_index_in_dim(out, part, (me + r) % WS, 0)
        return out.reshape((WS * parts[0].shape[0],) + parts[0].shape[1:])

    x_all16 = jnp.concatenate(gathered(tokens), axis=0)
    small = jnp.concatenate(
        [
            w_router,
            norm_attn[:, None],
            norm_moe[:, None],
            jnp.zeros((shard, 128 - experts - 2), BF),
        ],
        axis=1,
    )
    small_full = absolute(gathered(small))
    router = small_full[:, :experts]
    gain_one = small_full[:, experts].astype(F32)
    gain_two = small_full[:, experts + 1].astype(F32)

    def piece(d):
        return jnp.concatenate(
            [
                lax.dynamic_slice_in_dim(w_query, d * q_w, q_w, 1),
                lax.dynamic_slice_in_dim(w_key, d * kv_w, kv_w, 1),
                lax.dynamic_slice_in_dim(w_value, d * kv_w, kv_w, 1),
            ],
            axis=1,
        )

    qkv_parts = [piece(me)] + [from_peer(piece((me - k) % WS), k) for k in (1, 2, 3)]
    w_qkv = absolute(qkv_parts)

    labels = jnp.arange(experts, dtype=jnp.int32)
    chosen = jnp.any(routes[:, :, None] == labels[None, None, :], axis=1)
    row_id = jnp.arange(rows, dtype=jnp.int32)
    before = (row_id[None, :] < row_id[:, None]).astype(BF)
    rank = dot(before, chosen.astype(BF))
    col = jnp.arange(slots, dtype=jnp.int32)
    spread = (col[None, :] // CAP == labels[:, None]).astype(BF)
    place = dot(jnp.where(chosen, rank + 1.0, 0.0).astype(BF), spread)
    taken = place == (col % CAP + 1).astype(F32)[None, :]
    to_slot = taken.astype(BF)
    extra = jnp.concatenate(
        [cotangent, chosen.astype(BF), jnp.zeros((rows, 128 - experts), BF)], axis=1
    )
    dy_send = tdot(to_slot, extra).astype(BF).reshape(experts, CAP, width + 128)
    dy_slots = lax.all_to_all(dy_send, "exp", 0, 0, tiled=True).reshape(slots, width + 128)

    order = (
        ((me + jnp.arange(WS, dtype=jnp.int32)) % WS)[:, None] * rows + row_id[None, :]
    ).reshape(-1)
    visible, position = tree_layout(seg_lengths[0], parents[0], order)
    inverse = THETA ** (-jnp.arange(HEAD // 2, dtype=F32) * 2.0 / HEAD)
    angles = position.astype(F32)[:, None] * inverse[None, :]
    cosines, sines = jnp.cos(angles), jnp.sin(angles)
    x_all = x_all16.astype(F32)
    scale_one = lax.rsqrt(jnp.mean(x_all * x_all, axis=-1, keepdims=True) + EPS)
    h1 = (x_all * scale_one * gain_one).astype(BF)
    qkv = dot(h1, w_qkv)
    q = rope(qkv[:, :q_w], cosines, sines, 1.0).astype(BF).reshape(tree, my_kv, group, HEAD)
    k = rope(qkv[:, q_w : q_w + kv_w], cosines, sines, 1.0).astype(BF).reshape(tree, my_kv, HEAD)
    v = qkv[:, q_w + kv_w :].astype(BF).reshape(tree, my_kv, HEAD)
    score_scale = HEAD ** (-0.5)

    def score_rows():
        raw = jnp.einsum("tkgd,skd->kgts", q, k, preferred_element_type=F32) * score_scale
        return jnp.where(visible[None, None], raw, MASKED)

    scores = score_rows()
    row_peak = jnp.max(scores, axis=-1, keepdims=True)
    lifted = jnp.exp(scores - row_peak)
    row_total = jnp.sum(lifted, axis=-1, keepdims=True)
    logsum = row_peak + jnp.log(row_total)
    attention = (lifted / row_total).astype(BF)
    o = (
        jnp.einsum("kgts,skd->tkgd", attention, v, preferred_element_type=F32)
        .reshape(tree, q_w)
        .astype(BF)
    )

    def to_owners(partial):
        blocks = partial.reshape(WS, rows, width)
        total = blocks[0]
        for k in (1, 2, 3):
            total = total + to_peer(blocks[k].astype(BF), k).astype(F32)
        return total

    x2 = tokens.astype(F32) + to_owners(dot(o, w_out))
    scale_two = lax.rsqrt(jnp.mean(x2 * x2, axis=-1, keepdims=True) + EPS)
    h2 = (x2 * scale_two * gain_two).astype(BF)
    x_send = tdot(to_slot, h2).astype(BF).reshape(experts, CAP, width)
    x_send, wg_own, wu_own, wd_own = lax.optimization_barrier(
        (x_send, w_gate[0], w_up[0], w_down[0])
    )
    x_slots = lax.all_to_all(x_send, "exp", 0, 0, tiled=True).reshape(slots, width)
    gates = masked_softmax(dot(h2, router), chosen)

    wg = jnp.concatenate(gathered(wg_own), axis=1)
    wu = jnp.concatenate(gathered(wu_own), axis=1)
    wd = jnp.concatenate(gathered(wd_own), axis=0)
    g_pre = dot(x_slots, wg)
    u_pre = dot(x_slots, wu)
    sig = jax.nn.sigmoid(g_pre)
    hidden = (g_pre * sig * u_pre).astype(BF)
    y = dot(hidden, wd).astype(BF)
    dy = dy_slots[:, :width].astype(F32)
    slot_mask = dy_slots[:, width : width + experts] > 0.5
    slot_gates = masked_softmax(dot(x_slots, router), slot_mask)
    mine = (labels == expert)[None, :]
    gate_here = jnp.sum(jnp.where(mine, slot_gates, 0.0), axis=1, keepdims=True)
    dgate = jnp.sum(dy * y.astype(F32), axis=1, keepdims=True)
    d_y = (gate_here * dy).astype(BF)
    d_h = dot_t(d_y, wd)
    d_g = (d_h * u_pre * sig * (1.0 + g_pre * (1.0 - sig))).astype(BF)
    d_u = (d_h * g_pre * sig).astype(BF)
    d_x = (dot_t(d_g, wg) + dot_t(d_u, wu)).astype(BF)
    hi, lo = split(dgate)
    none = jnp.zeros((), BF)
    tail = jnp.concatenate(
        [
            jnp.where(mine, hi, none),
            jnp.where(mine, lo, none),
            jnp.zeros((slots, 128 - 2 * experts), BF),
        ],
        axis=1,
    )
    dx_send = jnp.concatenate([d_x, tail], axis=1).reshape(experts, CAP, width + 128)
    dx_back = lax.all_to_all(dx_send, "exp", 0, 0, tiled=True).reshape(slots, width + 128)
    y, dx_back = lax.optimization_barrier((y, dx_back))
    y_back = lax.all_to_all(y.reshape(experts, CAP, width), "exp", 0, 0, tiled=True).reshape(
        slots, width
    )

    part = w_gate.shape[2]

    def shard_sum(blocks):
        total = blocks[0]
        for k in (1, 2, 3):
            total = total + to_peer(blocks[k].astype(BF), k).astype(F32)
        return total

    grad_wg = shard_sum(
        [tdot(x_slots, d_g[:, r * part : (r + 1) * part]) for r in range(WS)]
    )[None]
    grad_wu = shard_sum(
        [tdot(x_slots, d_u[:, r * part : (r + 1) * part]) for r in range(WS)]
    )[None]
    grad_wd = shard_sum(
        [tdot(hidden[:, r * part : (r + 1) * part], d_y) for r in range(WS)]
    )[None]

    back = dot(to_slot, dx_back)
    dgate_dense = back[:, width : width + experts] + back[:, width + experts : width + 2 * experts]
    dlogits = gates * (dgate_dense - jnp.sum(gates * dgate_dense, axis=-1, keepdims=True))
    dl_hi, dl_lo = split(dlogits)
    dh2 = back[:, :width] + dot_t(dl_hi, router) + dot_t(dl_lo, router)
    grad_router = tdot(h2, dl_hi) + tdot(h2, dl_lo)
    dres, grad_gain_two = norm_back(x2, scale_two, gain_two, dh2)
    dx2 = cotangent.astype(F32) + dres
    d_a = jnp.concatenate(gathered(dx2.astype(BF)), axis=0)
    grad_wout = tdot(o, d_a)
    d_o = dot_t(d_a, w_out).astype(BF).reshape(tree, my_kv, group, HEAD)
    probs = jnp.exp(score_rows() - logsum)
    d_p = jnp.einsum("tkgd,skd->kgts", d_o, v, preferred_element_type=F32)
    delta = jnp.sum(probs * d_p, axis=-1, keepdims=True)
    d_s = (probs * (d_p - delta)).astype(BF)
    d_q = jnp.einsum("kgts,skd->tkgd", d_s, k, preferred_element_type=F32) * score_scale
    d_k = jnp.einsum("kgts,tkgd->skd", d_s, q, preferred_element_type=F32) * score_scale
    d_v = jnp.einsum("kgts,tkgd->skd", probs.astype(BF), d_o, preferred_element_type=F32)
    d_qkv = jnp.concatenate(
        [
            rope(d_q.reshape(tree, q_w), cosines, sines, -1.0).astype(BF),
            rope(d_k.reshape(tree, kv_w), cosines, sines, -1.0).astype(BF),
            d_v.reshape(tree, kv_w).astype(BF),
        ],
        axis=1,
    )
    dh1_part = dot_t(d_qkv, w_qkv)
    grad_gain_one = jnp.sum(dh1_part * x_all * scale_one, axis=0)
    dh1 = to_owners(dh1_part)
    dres_one, _ = norm_back(tokens.astype(F32), scale_one[:rows], gain_one, dh1)
    grad_tokens = dx2 + dres_one
    grad_wqkv = tdot(h1, d_qkv)

    half = (q_w + 2 * kv_w + 128) // 2
    load = jnp.concatenate(
        [
            grad_wqkv,
            grad_router,
            grad_gain_two[:, None],
            grad_gain_one[:, None],
            jnp.zeros((width, 128 - experts - 2), F32),
        ],
        axis=1,
    )
    load_o = jnp.concatenate([grad_wout[:, i * half : (i + 1) * half] for i in range(WS)], axis=0)
    load_o = jnp.concatenate([load_o[: 2 * shard], load_o[2 * shard :]], axis=1)
    load = jnp.concatenate([load, load_o], axis=0)
    keep = jnp.where(core == 0, load[:, :half], load[:, half:])
    give = jnp.where(core == 0, load[:, half:], load[:, :half]).astype(BF)
    chip_sum = (keep + other_core(give).astype(F32)).astype(BF)
    step = shard // CHIPS
    sets = chip_sum.shape[0] // shard
    sent = chip_sum.reshape(sets, CHIPS, step, half).transpose(1, 0, 2, 3)
    got = same_core(sent)
    total = jnp.sum(got.astype(F32), axis=0).astype(BF)
    turned = absolute(
        [lax.dynamic_index_in_dim(total, me, 0, False)]
        + [
            from_peer(lax.dynamic_index_in_dim(total, (me - k) % WS, 0, False), k)
            for k in (1, 2, 3)
        ]
    ).reshape(WS, step, half)
    final = jnp.concatenate([turned, total[WS:]], axis=0)
    spread_out = same_core(jnp.broadcast_to(final, (CHIPS,) + final.shape))
    twin = other_core(spread_out)
    first = jnp.where(core == 0, spread_out, twin).transpose(1, 0, 2, 3).reshape(sets, shard, half)
    second = jnp.where(core == 0, twin, spread_out).transpose(1, 0, 2, 3).reshape(sets, shard, half)
    first, second = first.astype(F32), second.astype(F32)
    sum_query = jnp.concatenate([first[i] for i in range(WS)], axis=1)
    sum_key = jnp.concatenate([second[i][:, :kv_w] for i in range(WS)], axis=1)
    sum_value = jnp.concatenate([second[i][:, kv_w : 2 * kv_w] for i in range(WS)], axis=1)
    sum_small = sum(second[i][:, 2 * kv_w :] for i in range(WS))
    sum_out = jnp.concatenate([first[WS], first[WS + 1], second[WS], second[WS + 1]], axis=1)

    gates_slot = jnp.where(taken, dot(split(gates)[0], spread) + dot(split(gates)[1], spread), 0.0)
    gs_hi, gs_lo = split(gates_slot)
    layer_out = (x2 + dot(gs_hi, y_back) + dot(gs_lo, y_back)).astype(BF)
    return (
        layer_out,
        grad_tokens,
        sum_small[:, experts + 1],
        sum_query,
        sum_key,
        sum_value,
        sum_out,
        sum_small[:, experts],
        sum_small[:, :experts],
        grad_wg,
        grad_wu,
        grad_wd,
    )


def solution(mesh):
    rows = P(("exp", "ws"), None)
    placed = (
        rows,
        rows,
        P("exp", None),
        P("exp", None),
        rows,
        P("ws"),
        P("ws", None),
        P("ws", None),
        P("ws", None),
        P("ws", None),
        P("ws"),
        P("ws", None),
        P("exp", None, "ws"),
        P("exp", None, "ws"),
        P("exp", "ws", None),
    )
    return jax.shard_map(
        shards,
        mesh=mesh,
        in_specs=placed,
        out_specs=(
            rows,
            rows,
            P("ws"),
            P("ws", None),
            P("ws", None),
            P("ws", None),
            P("ws", None),
            P("ws"),
            P("ws", None),
            P("exp", None, "ws"),
            P("exp", None, "ws"),
            P("exp", "ws", None),
        ),
        check_vma=False,
    )
```

```python
import functools

import jax
import jax.numpy as jnp
from jax import lax
from jax.experimental import pallas as pl
from jax.experimental.pallas import tpu as pltpu
from jax.sharding import PartitionSpec as P

HEADS = 24
KV_HEADS = 8
HEAD = 64
EPS = 1e-06
THETA = 10000.0
MASKED = -1e30
BF = jnp.bfloat16
F32 = jnp.float32
WS = 4
CHIPS = 16
CAP = 48
VM = 60 * 1024 * 1024


def dot(a, b):
    return jnp.dot(a, b, preferred_element_type=F32)


def dot_t(a, b):
    return lax.dot_general(a, b, (((1,), (1,)), ((), ())), preferred_element_type=F32)


def tdot(a, b):
    return lax.dot_general(a, b, (((0,), (0,)), ((), ())), preferred_element_type=F32)


def split(v):
    hi = v.astype(BF)
    return hi, (v - hi.astype(F32)).astype(BF)


def from_peer(v, k):
    return lax.ppermute(v, "ws", [(s, (s - k) % WS) for s in range(WS)])


def to_peer(v, k):
    return lax.ppermute(v, "ws", [(s, (s + k) % WS) for s in range(WS)])


def other_core(v):
    return lax.ppermute(v, "exp", [(s, s ^ 1) for s in range(2 * CHIPS)])


def same_core(v):
    groups = [[2 * chip + core for chip in range(CHIPS)] for core in range(2)]
    return lax.all_to_all(v, "exp", 0, 0, tiled=True, axis_index_groups=groups)


def tree_layout(lengths, parents, token_index):
    seg = lengths.shape[0]
    labels = jnp.arange(seg, dtype=jnp.int32)
    segment_end = jnp.cumsum(lengths, dtype=jnp.int32)
    starts = segment_end - lengths
    segment = jnp.sum((token_index[:, None] >= segment_end[None, :]).astype(jnp.int32), axis=1)
    reach = ((parents[:, None] == labels[None, :]) | (labels[:, None] == labels[None, :])).astype(
        BF
    )
    for _ in range(4):
        reach = (dot(reach, reach) > 0.5).astype(BF)
    above = jnp.sum(reach.astype(jnp.int32) * lengths[None, :], axis=1) - lengths
    members = segment[:, None] == labels[None, :]
    position = jnp.sum(jnp.where(members, (above - starts)[None, :], 0), axis=1) + token_index
    members = members.astype(BF)
    reaches = dot(members, reach).astype(BF)
    visible = (dot_t(reaches, members) > 0.5) & (token_index[None, :] <= token_index[:, None])
    return visible, position


def rope(vectors, cosines, sines, sign):
    rows, width = vectors.shape
    v = vectors.reshape(rows, width // HEAD, HEAD)
    a, b = v[..., : HEAD // 2], v[..., HEAD // 2 :]
    c, s = cosines[:, None, :], sines[:, None, :] * sign
    return jnp.concatenate([a * c - b * s, b * c + a * s], axis=-1).reshape(rows, width)


def norm_back(resid, scale, gain, slope):
    gain_slope = jnp.sum(slope * resid * scale, axis=0)
    inner = jnp.mean(gain * slope * resid, axis=-1, keepdims=True)
    return scale * gain * slope - resid * scale * scale * scale * inner, gain_slope


def masked_softmax(logits, mask):
    top = jnp.max(jnp.where(mask, logits, MASKED), axis=-1, keepdims=True)
    lifted = jnp.where(mask, jnp.exp(jnp.where(mask, logits, MASKED) - top), 0.0)
    return lifted / jnp.maximum(jnp.sum(lifted, axis=-1, keepdims=True), 1e-30)


def expert_body(width, ff, x_ref, dy_ref, sel_ref, wr_ref, *rest):
    wg, wu, wd = rest[0:4], rest[4:8], rest[8:12]
    y_ref, dx_ref, h_ref, dgu_ref, dyo_ref = rest[12:17]
    wgu, wdn = rest[17:]
    part = wg[0].shape[1]

    @pl.when(pl.program_id(0) == 0)
    def _():
        for r in range(4):
            wgu[:, r * part : (r + 1) * part] = wg[r][...]
            wgu[:, ff + r * part : ff + (r + 1) * part] = wu[r][...]
            wdn[r * part : (r + 1) * part, :] = wd[r][...]
        wgu[:, 2 * ff :] = wr_ref[...]

    x = x_ref[...]
    pre = dot(x, wgu[...])
    g, u, logits = pre[:, :ff], pre[:, ff : 2 * ff], pre[:, 2 * ff :]
    mask = dy_ref[:, width:].astype(F32) > 0.5
    logits = jnp.where(mask, logits, MASKED)
    lifted = jnp.where(mask, jnp.exp(logits - jnp.max(logits, axis=1, keepdims=True)), 0.0)
    total = jnp.maximum(jnp.sum(lifted, axis=1, keepdims=True), 1e-30)
    gate = jnp.sum(lifted * sel_ref[0:1, :], axis=1, keepdims=True) / total
    sig = 1.0 / (1.0 + jnp.exp(-g))
    silu = g * sig
    h = (silu * u).astype(BF)
    h_ref[...] = h
    y = dot(h, wdn[...]).astype(BF)
    y_ref[...] = y
    dy = dy_ref[:, :width].astype(F32)
    dgate = jnp.sum(dy * y.astype(F32), axis=1, keepdims=True)
    d_y = (gate * dy).astype(BF)
    dyo_ref[...] = d_y
    dh = dot_t(d_y, wdn[...])
    dgu_ref[:, :ff] = (dh * u * sig * (1.0 + g * (1.0 - sig))).astype(BF)
    dgu_ref[:, ff:] = (dh * silu).astype(BF)
    dx_ref[:, :width] = dot_t(dgu_ref[...], wgu[:, : 2 * ff]).astype(BF)
    hi = dgate.astype(BF).astype(F32)
    dx_ref[:, width:] = (hi * sel_ref[0:1, :] + (dgate - hi) * sel_ref[1:2, :]).astype(BF)

def expert_pass(x, dy, sel, wr, wg, wu, wd, tile):
    slots, width = x.shape
    part = wg[0].shape[1]; ff = 4 * part
    row = lambda w: pl.BlockSpec((tile, w), lambda i: (i, 0))
    whole = lambda a: pl.BlockSpec(a.shape, lambda i: (0, 0))
    return pl.pallas_call(
        functools.partial(expert_body, width, ff),
        grid=(slots // tile,),
        in_specs=[row(width), row(width + 128), whole(sel), whole(wr)] + [whole(a) for a in (*wg, *wu, *wd)],
        out_specs=[row(width), row(width + 128), row(ff), row(2 * ff), row(width)],
        out_shape=[jax.ShapeDtypeStruct((slots, w), BF) for w in (width, width + 128, ff, 2 * ff, width)],
        scratch_shapes=[pltpu.VMEM((width, 2 * ff + 128), BF), pltpu.VMEM((ff, width), BF)],
        compiler_params=pltpu.CompilerParams(vmem_limit_bytes=VM),
        cost_estimate=pl.CostEstimate(flops=12*slots*width*ff, bytes_accessed=12*slots*width, transcendentals=slots*ff),
        name="expert_pass",
    )(x, dy, sel, wr, *wg, *wu, *wd)

def slope_body(x_ref, dgu_ref, h_ref, dy_ref, own_g, own_u, own_d, *peers):
    part = own_g.shape[1]
    ff = h_ref.shape[1]
    gu = tdot(x_ref[...], dgu_ref[...])
    dn = tdot(h_ref[...], dy_ref[...])
    own_g[...] = gu[:, :part]
    own_u[...] = gu[:, ff : ff + part]
    own_d[...] = dn[:part]
    for k in (1, 2, 3):
        peers[2 * k - 2][0] = gu[:, k * part : (k + 1) * part].astype(BF)
        peers[2 * k - 2][1] = gu[:, ff + k * part : ff + (k + 1) * part].astype(BF)
        peers[2 * k - 1][...] = dn[k * part : (k + 1) * part].astype(BF)

def expert_slopes(x, dgu, h, dy, tile=256):
    slots, width = x.shape
    ff = h.shape[1]; part = ff // 4
    col = pl.BlockSpec((slots, tile), lambda i: (0, i))
    whole = lambda a: pl.BlockSpec(a.shape, lambda i: (0, 0))
    tall = pl.BlockSpec((tile, part), lambda i: (i, 0))
    wide = pl.BlockSpec((part, tile), lambda i: (0, i))
    pair = pl.BlockSpec((2, tile, part), lambda i: (0, i, 0))
    S = jax.ShapeDtypeStruct
    return pl.pallas_call(
        slope_body,
        grid=(width // tile,),
        in_specs=[col, whole(dgu), whole(h), col],
        out_specs=[tall, tall, wide] + [pair, wide] * 3,
        out_shape=[S((width, part), F32)] * 2 + [S((part, width), F32)] + [S((2, width, part), BF), S((part, width), BF)] * 3,
        compiler_params=pltpu.CompilerParams(vmem_limit_bytes=VM),
        cost_estimate=pl.CostEstimate(flops=6*slots*width*ff, bytes_accessed=8*slots*width, transcendentals=0),
        name="expert_slopes",
    )(x, dgu, h, dy)


def load_body(h_ref, dqkv_ref, o_ref, da_ref, small_ref, flag_ref, keep_ref, give_ref):
    step = pl.program_id(0)
    half = keep_ref.shape[3]
    count = keep_ref.shape[0] * keep_ref.shape[2]
    shape = (keep_ref.shape[0], keep_ref.shape[2], half)

    def put(kept, given):
        keep_ref[:, 0] = kept.reshape(shape)
        give_ref[:, 0] = given.reshape(shape).astype(BF)

    @pl.when(step < WS)
    def _():
        both = tdot(h_ref[...], dqkv_ref[...])
        none = jnp.zeros((count, half - 128), F32)
        small = jnp.concatenate([none, small_ref[...]], axis=1)
        put(both[:, :half] + small * flag_ref[0:1, 0:1], both[:, half:] + small * flag_ref[1:2, 0:1])

    for i in range(2):

        @pl.when(step == WS + i)
        def _():
            kept = tdot(o_ref[...], da_ref[:, i * half : (i + 1) * half])
            given = tdot(o_ref[...], da_ref[:, (2 + i) * half : (3 + i) * half])
            put(kept, given)


def load_terms(h1, dqkv, o, da, small, flag):
    tree, width = h1.shape
    half = dqkv.shape[1] // 2
    sets, step = WS + 2, width // WS // CHIPS
    whole = lambda a: pl.BlockSpec(a.shape, lambda i: (0, 0))
    out = pl.BlockSpec((CHIPS, 1, step, half), lambda i: (0, i, 0, 0))
    return pl.pallas_call(
        load_body,
        grid=(sets,),
        in_specs=[
            pl.BlockSpec((tree, width // WS), lambda i: (0, jnp.minimum(i, WS - 1))),
            whole(dqkv),
            whole(o),
            whole(da),
            pl.BlockSpec((width // WS, 128), lambda i: (jnp.minimum(i, WS - 1), 0)),
            whole(flag),
        ],
        out_specs=[out, out],
        out_shape=[
            jax.ShapeDtypeStruct((CHIPS, sets, step, half), F32),
            jax.ShapeDtypeStruct((CHIPS, sets, step, half), BF),
        ],
        compiler_params=pltpu.CompilerParams(vmem_limit_bytes=VM),
        cost_estimate=pl.CostEstimate(
            flops=4 * tree * sets * (width // WS) * half,
            bytes_accessed=6 * sets * width * half,
            transcendentals=0,
        ),
        name="load_terms",
    )(h1, dqkv, o, da, small, flag)


def finish_body(a_ref, b_ref, ao_ref, bo_ref, flag_ref, q_ref, k_ref, v_ref, s_ref, o_ref):
    turn = pl.program_id(0)
    second = flag_ref[0:1, 0:1]
    rows = q_ref.shape[0]
    half = a_ref.shape[3]
    kv = k_ref.shape[1]
    mine = a_ref[:, 0].astype(F32).reshape(rows, half)
    twin = b_ref[:, 0].astype(F32).reshape(rows, half)
    q_ref[...] = jnp.where(second > 0.5, twin, mine)
    rest = jnp.where(second > 0.5, mine, twin)
    k_ref[...] = rest[:, :kv]
    v_ref[...] = rest[:, kv : 2 * kv]

    @pl.when(turn == 0)
    def _():
        s_ref[...] = rest[:, 2 * kv :]

    @pl.when(turn > 0)
    def _():
        s_ref[...] += rest[:, 2 * kv :]

    mine = ao_ref[:, 0].astype(F32).reshape(rows, half)
    twin = bo_ref[:, 0].astype(F32).reshape(rows, half)
    use_twin = jnp.where(turn < 2, second, 1.0 - second)
    o_ref[...] = jnp.where(use_twin > 0.5, twin, mine)


def finish(mine, twin, flag):
    chips, sets, step, half = mine.shape
    rows = chips * step
    first = pl.BlockSpec((chips, 1, step, half), lambda i: (0, i, 0, 0))
    later = pl.BlockSpec((chips, 1, step, half), lambda i: (0, WS + i % 2, 0, 0))
    kv = (half - 128) // 2
    S = jax.ShapeDtypeStruct
    return pl.pallas_call(
        finish_body,
        grid=(WS,),
        in_specs=[first, first, later, later, pl.BlockSpec(flag.shape, lambda i: (0, 0))],
        out_specs=[
            pl.BlockSpec((rows, half), lambda i: (0, i)),
            pl.BlockSpec((rows, kv), lambda i: (0, i)),
            pl.BlockSpec((rows, kv), lambda i: (0, i)),
            pl.BlockSpec((rows, 128), lambda i: (0, 0)),
            pl.BlockSpec((rows, half), lambda i: (0, i)),
        ],
        out_shape=[
            S((rows, WS * half), F32),
            S((rows, WS * kv), F32),
            S((rows, WS * kv), F32),
            S((rows, 128), F32),
            S((rows, WS * half), F32),
        ],
        compiler_params=pltpu.CompilerParams(vmem_limit_bytes=VM),
        cost_estimate=pl.CostEstimate(flops=0, bytes_accessed=16 * rows * WS * half, transcendentals=0),
        name="finish",
    )(mine, twin, mine, twin, flag)


def shards(
    tokens,
    cotangent,
    seg_lengths,
    parents,
    routes,
    norm_attn,
    w_query,
    w_key,
    w_value,
    w_out,
    norm_moe,
    w_router,
    w_gate,
    w_up,
    w_down,
):
    me = lax.axis_index("ws")
    expert = lax.axis_index("exp")
    core = expert % 2
    rows, width = tokens.shape
    tree = rows * WS
    shard = width // WS
    experts = 2 * CHIPS
    group = HEADS // KV_HEADS
    my_heads = HEADS // WS
    my_kv = KV_HEADS // WS
    q_w, kv_w = my_heads * HEAD, my_kv * HEAD
    slots = experts * CAP

    def gathered(v):
        return [v] + [from_peer(v, k) for k in (1, 2, 3)]

    def absolute(parts):
        out = jnp.zeros((WS,) + parts[0].shape, parts[0].dtype)
        for r, part in enumerate(parts):
            out = lax.dynamic_update_index_in_dim(out, part, (me + r) % WS, 0)
        return out.reshape((WS * parts[0].shape[0],) + parts[0].shape[1:])

    def piece(d):
        return jnp.concatenate(
            [
                lax.dynamic_slice_in_dim(w_query, d * q_w, q_w, 1),
                lax.dynamic_slice_in_dim(w_key, d * kv_w, kv_w, 1),
                lax.dynamic_slice_in_dim(w_value, d * kv_w, kv_w, 1),
            ],
            axis=1,
        )

    small = jnp.concatenate(
        [
            w_router,
            norm_attn[:, None],
            norm_moe[:, None],
            jnp.zeros((shard, 128 - experts - 2), BF),
        ],
        axis=1,
    )
    pieces = [piece((me - k) % WS) for k in range(WS)]
    pieces, small, routes = lax.optimization_barrier((pieces, small, routes))
    w_qkv = absolute([pieces[0]] + [from_peer(pieces[k], k) for k in (1, 2, 3)])
    x_all16 = jnp.concatenate(gathered(tokens), axis=0)
    small_full = absolute(gathered(small))
    router = small_full[:, :experts]
    gain_one = small_full[:, experts].astype(F32)
    gain_two = small_full[:, experts + 1].astype(F32)

    labels = jnp.arange(experts, dtype=jnp.int32)
    chosen = jnp.any(routes[:, :, None] == labels[None, None, :], axis=1)
    row_id = jnp.arange(rows, dtype=jnp.int32)
    before = (row_id[None, :] < row_id[:, None]).astype(BF)
    rank = dot(before, chosen.astype(BF))
    col = jnp.arange(slots, dtype=jnp.int32)
    spread = (col[None, :] // CAP == labels[:, None]).astype(BF)
    place = dot(jnp.where(chosen, rank + 1.0, 0.0).astype(BF), spread)
    taken = place == (col % CAP + 1).astype(F32)[None, :]
    to_slot = taken.astype(BF)
    extra = jnp.concatenate(
        [cotangent, chosen.astype(BF), jnp.zeros((rows, 128 - experts), BF)], axis=1
    )
    dy_send = tdot(to_slot, extra).astype(BF).reshape(experts, CAP, width + 128)
    dy_slots = lax.all_to_all(dy_send, "exp", 0, 0, tiled=True).reshape(slots, width + 128)

    order = (
        ((me + jnp.arange(WS, dtype=jnp.int32)) % WS)[:, None] * rows + row_id[None, :]
    ).reshape(-1)
    visible, position = tree_layout(seg_lengths[0], parents[0], order)
    inverse = THETA ** (-jnp.arange(HEAD // 2, dtype=F32) * 2.0 / HEAD)
    angles = position.astype(F32)[:, None] * inverse[None, :]
    cosines, sines = jnp.cos(angles), jnp.sin(angles)
    x_all = x_all16.astype(F32)
    scale_one = lax.rsqrt(jnp.mean(x_all * x_all, axis=-1, keepdims=True) + EPS)
    h1 = (x_all * scale_one * gain_one).astype(BF)
    qkv = dot(h1, w_qkv)
    q = rope(qkv[:, :q_w], cosines, sines, 1.0).astype(BF).reshape(tree, my_kv, group, HEAD)
    k = rope(qkv[:, q_w : q_w + kv_w], cosines, sines, 1.0).astype(BF).reshape(tree, my_kv, HEAD)
    v = qkv[:, q_w + kv_w :].astype(BF).reshape(tree, my_kv, HEAD)
    score_scale = HEAD ** (-0.5)

    def score_rows():
        raw = jnp.einsum("tkgd,skd->kgts", q, k, preferred_element_type=F32) * score_scale
        return jnp.where(visible[None, None], raw, MASKED)

    scores = score_rows()
    row_peak = jnp.max(scores, axis=-1, keepdims=True)
    lifted = jnp.exp(scores - row_peak)
    row_total = jnp.sum(lifted, axis=-1, keepdims=True)
    logsum = row_peak + jnp.log(row_total)
    attention = (lifted / row_total).astype(BF)
    o = (
        jnp.einsum("kgts,skd->tkgd", attention, v, preferred_element_type=F32)
        .reshape(tree, q_w)
        .astype(BF)
    )

    def to_owners(partial):
        blocks = partial.reshape(WS, rows, width)
        total = blocks[0]
        for k in (1, 2, 3):
            total = total + to_peer(blocks[k].astype(BF), k).astype(F32)
        return total

    x2 = tokens.astype(F32) + to_owners(dot(o, w_out))
    scale_two = lax.rsqrt(jnp.mean(x2 * x2, axis=-1, keepdims=True) + EPS)
    h2 = (x2 * scale_two * gain_two).astype(BF)
    x_send = tdot(to_slot, h2).astype(BF).reshape(experts, CAP, width)
    x_send, wg_own, wu_own, wd_own = lax.optimization_barrier(
        (x_send, w_gate[0], w_up[0], w_down[0])
    )
    x_slots = lax.all_to_all(x_send, "exp", 0, 0, tiled=True).reshape(slots, width)
    gates = masked_softmax(dot(h2, router), chosen)

    lane = jnp.arange(128, dtype=jnp.int32)
    sel = jnp.concatenate(
        [
            (lane == expert).astype(F32)[None],
            (lane == expert + experts).astype(F32)[None],
            jnp.zeros((6, 128), F32),
        ],
        axis=0,
    )
    y, dx_send, hidden, d_gu, d_y = expert_pass(
        x_slots, dy_slots, sel, small_full, gathered(wg_own), gathered(wu_own), gathered(wd_own), 512
    )
    dx_back = lax.all_to_all(
        dx_send.reshape(experts, CAP, width + 128), "exp", 0, 0, tiled=True
    ).reshape(slots, width + 128)

    own_g, own_u, own_d, gu1, dn1, gu2, dn2, gu3, dn3 = expert_slopes(x_slots, d_gu, hidden, d_y)
    gu1, dn1 = to_peer(gu1, 1), to_peer(dn1, 1)
    gu3, dn3 = to_peer(gu3, 3), to_peer(dn3, 3)
    dx_back, y, gu1, dn1, gu3, dn3 = lax.optimization_barrier((dx_back, y, gu1, dn1, gu3, dn3))
    y_back = lax.all_to_all(y.reshape(experts, CAP, width), "exp", 0, 0, tiled=True).reshape(
        slots, width
    )

    back = dot(to_slot, dx_back)
    dgate_dense = back[:, width : width + experts] + back[:, width + experts : width + 2 * experts]
    dlogits = gates * (dgate_dense - jnp.sum(gates * dgate_dense, axis=-1, keepdims=True))
    dl_hi, dl_lo = split(dlogits)
    dh2 = back[:, :width] + dot_t(dl_hi, router) + dot_t(dl_lo, router)
    grad_router = tdot(h2, dl_hi) + tdot(h2, dl_lo)
    dres, grad_gain_two = norm_back(x2, scale_two, gain_two, dh2)
    dx2 = cotangent.astype(F32) + dres
    d_a = jnp.concatenate(gathered(dx2.astype(BF)), axis=0)
    d_a, gu2, dn2 = lax.optimization_barrier((d_a, gu2, dn2))
    gu2, dn2 = to_peer(gu2, 2), to_peer(dn2, 2)
    grad_gu = jnp.stack([own_g, own_u]) + gu1.astype(F32) + gu2.astype(F32) + gu3.astype(F32)
    grad_wg, grad_wu = grad_gu[0][None], grad_gu[1][None]
    grad_wd = (own_d + dn1.astype(F32) + dn2.astype(F32) + dn3.astype(F32))[None]
    d_o = dot_t(d_a, w_out).astype(BF).reshape(tree, my_kv, group, HEAD)
    probs = jnp.exp(score_rows() - logsum)
    d_p = jnp.einsum("tkgd,skd->kgts", d_o, v, preferred_element_type=F32)
    delta = jnp.sum(probs * d_p, axis=-1, keepdims=True)
    d_s = (probs * (d_p - delta)).astype(BF)
    d_q = jnp.einsum("kgts,skd->tkgd", d_s, k, preferred_element_type=F32) * score_scale
    d_k = jnp.einsum("kgts,tkgd->skd", d_s, q, preferred_element_type=F32) * score_scale
    d_v = jnp.einsum("kgts,tkgd->skd", probs.astype(BF), d_o, preferred_element_type=F32)
    d_qkv = jnp.concatenate(
        [
            rope(d_q.reshape(tree, q_w), cosines, sines, -1.0).astype(BF),
            rope(d_k.reshape(tree, kv_w), cosines, sines, -1.0).astype(BF),
            d_v.reshape(tree, kv_w).astype(BF),
        ],
        axis=1,
    )
    dh1_part = dot_t(d_qkv, w_qkv)
    grad_gain_one = jnp.sum(dh1_part * x_all * scale_one, axis=0)
    dh1 = to_owners(dh1_part)
    dres_one, _ = norm_back(tokens.astype(F32), scale_one[:rows], gain_one, dh1)
    grad_tokens = dx2 + dres_one
    half = (q_w + 2 * kv_w + 128) // 2
    flag = jnp.broadcast_to(jnp.stack([core, 1 - core]).astype(F32)[:, None], (2, 128))
    flag = jnp.concatenate([flag, jnp.zeros((6, 128), F32)], axis=0)
    small_terms = jnp.concatenate(
        [
            grad_router,
            grad_gain_two[:, None],
            grad_gain_one[:, None],
            jnp.zeros((width, 128 - experts - 2), F32),
        ],
        axis=1,
    )
    d_kv = jnp.concatenate([d_qkv[:, q_w:], jnp.zeros((tree, 128), BF)], axis=1)
    d_turned = jnp.where(
        core == 0,
        jnp.concatenate([d_qkv[:, :q_w], d_kv], axis=1),
        jnp.concatenate([d_kv, d_qkv[:, :q_w]], axis=1),
    )
    da_turned = jnp.where(
        core == 0, d_a, jnp.concatenate([d_a[:, width // 2 :], d_a[:, : width // 2]], axis=1)
    )
    keep, give = load_terms(h1, d_turned, o, da_turned, small_terms, flag)
    give, y_back = lax.optimization_barrier((give, y_back))
    sent = (keep + other_core(give).astype(F32)).astype(BF)
    step = shard // CHIPS
    got = same_core(sent)
    total = jnp.sum(got.astype(F32), axis=0).astype(BF)
    turned = absolute(
        [lax.dynamic_index_in_dim(total, me, 0, False)]
        + [
            from_peer(lax.dynamic_index_in_dim(total, (me - k) % WS, 0, False), k)
            for k in (1, 2, 3)
        ]
    ).reshape(WS, step, half)
    final = jnp.concatenate([turned, total[WS:]], axis=0)
    spread_out = same_core(jnp.broadcast_to(final, (CHIPS,) + final.shape))
    twin = other_core(spread_out)
    sum_query, sum_key, sum_value, sum_small, sum_out = finish(spread_out, twin, flag)

    gates_slot = jnp.where(taken, dot(split(gates)[0], spread) + dot(split(gates)[1], spread), 0.0)
    gs_hi, gs_lo = split(gates_slot)
    layer_out = (x2 + dot(gs_hi, y_back) + dot(gs_lo, y_back)).astype(BF)
    return (
        layer_out,
        grad_tokens,
        sum_small[:, experts + 1],
        sum_query,
        sum_key,
        sum_value,
        sum_out,
        sum_small[:, experts],
        sum_small[:, :experts],
        grad_wg,
        grad_wu,
        grad_wd,
    )


def solution(mesh):
    rows = P(("exp", "ws"), None)
    placed = (
        rows,
        rows,
        P("exp", None),
        P("exp", None),
        rows,
        P("ws"),
        P("ws", None),
        P("ws", None),
        P("ws", None),
        P("ws", None),
        P("ws"),
        P("ws", None),
        P("exp", None, "ws"),
        P("exp", None, "ws"),
        P("exp", "ws", None),
    )
    return jax.shard_map(
        shards,
        mesh=mesh,
        in_specs=placed,
        out_specs=(
            rows,
            rows,
            P("ws"),
            P("ws", None),
            P("ws", None),
            P("ws", None),
            P("ws", None),
            P("ws"),
            P("ws", None),
            P("exp", None, "ws"),
            P("exp", None, "ws"),
            P("exp", "ws", None),
        ),
        check_vma=False,
    )
```

```python
import functools

import jax
import jax.numpy as jnp
from jax import lax
from jax.experimental import pallas as pl
from jax.experimental.pallas import tpu as pltpu
from jax.sharding import PartitionSpec as P

HEADS = 24
KV_HEADS = 8
HEAD = 64
EPS = 1e-06
THETA = 10000.0
MASKED = -1e30
BF = jnp.bfloat16
F32 = jnp.float32
WS = 4
CHIPS = 16
CAP = 48
VM = 60 * 1024 * 1024


def dot(a, b):
    return jnp.dot(a, b, preferred_element_type=F32)


def dot_t(a, b):
    return lax.dot_general(a, b, (((1,), (1,)), ((), ())), preferred_element_type=F32)


def tdot(a, b):
    return lax.dot_general(a, b, (((0,), (0,)), ((), ())), preferred_element_type=F32)


def split(v):
    hi = v.astype(BF)
    return hi, (v - hi.astype(F32)).astype(BF)


def from_peer(v, k):
    return lax.ppermute(v, "ws", [(s, (s - k) % WS) for s in range(WS)])


def to_peer(v, k):
    return lax.ppermute(v, "ws", [(s, (s + k) % WS) for s in range(WS)])


def other_core(v):
    return lax.ppermute(v, "exp", [(s, s ^ 1) for s in range(2 * CHIPS)])


def same_core(v):
    groups = [[2 * chip + core for chip in range(CHIPS)] for core in range(2)]
    return lax.all_to_all(v, "exp", 0, 0, tiled=True, axis_index_groups=groups)


def tree_layout(lengths, parents, token_index):
    seg = lengths.shape[0]
    labels = jnp.arange(seg, dtype=jnp.int32)
    segment_end = jnp.cumsum(lengths, dtype=jnp.int32)
    starts = segment_end - lengths
    segment = jnp.sum((token_index[:, None] >= segment_end[None, :]).astype(jnp.int32), axis=1)
    reach = ((parents[:, None] == labels[None, :]) | (labels[:, None] == labels[None, :])).astype(
        BF
    )
    for _ in range(4):
        reach = (dot(reach, reach) > 0.5).astype(BF)
    above = jnp.sum(reach.astype(jnp.int32) * lengths[None, :], axis=1) - lengths
    members = segment[:, None] == labels[None, :]
    position = jnp.sum(jnp.where(members, (above - starts)[None, :], 0), axis=1) + token_index
    members = members.astype(BF)
    reaches = dot(members, reach).astype(BF)
    visible = (dot_t(reaches, members) > 0.5) & (token_index[None, :] <= token_index[:, None])
    return visible, position


def expert_body(width, ff, x_ref, dy_ref, sel_ref, wr_ref, *rest):
    wg, wu, wd = rest[0:4], rest[4:8], rest[8:12]
    y_ref, dx_ref, h_ref, dgu_ref, dyo_ref = rest[12:17]
    wgu, wdn = rest[17:]
    part = wg[0].shape[1]

    @pl.when(pl.program_id(0) == 0)
    def _():
        for r in range(4):
            wgu[:, r * part : (r + 1) * part] = wg[r][...]
            wgu[:, ff + r * part : ff + (r + 1) * part] = wu[r][...]
            wdn[r * part : (r + 1) * part, :] = wd[r][...]
        wgu[:, 2 * ff :] = wr_ref[...]

    x = x_ref[...]
    pre = dot(x, wgu[...])
    g, u, logits = pre[:, :ff], pre[:, ff : 2 * ff], pre[:, 2 * ff :]
    mask = dy_ref[:, width:].astype(F32) > 0.5
    logits = jnp.where(mask, logits, MASKED)
    lifted = jnp.where(mask, jnp.exp(logits - jnp.max(logits, axis=1, keepdims=True)), 0.0)
    total = jnp.maximum(jnp.sum(lifted, axis=1, keepdims=True), 1e-30)
    gate = jnp.sum(lifted * sel_ref[0:1, :], axis=1, keepdims=True) / total
    sig = 1.0 / (1.0 + jnp.exp(-g))
    silu = g * sig
    h = (silu * u).astype(BF)
    h_ref[...] = h
    y = dot(h, wdn[...]).astype(BF)
    y_ref[...] = y
    dy = dy_ref[:, :width].astype(F32)
    dgate = jnp.sum(dy * y.astype(F32), axis=1, keepdims=True)
    d_y = (gate * dy).astype(BF)
    dyo_ref[...] = d_y
    dh = dot_t(d_y, wdn[...])
    dgu_ref[:, :ff] = (dh * u * sig * (1.0 + g * (1.0 - sig))).astype(BF)
    dgu_ref[:, ff:] = (dh * silu).astype(BF)
    dx_ref[:, :width] = dot_t(dgu_ref[...], wgu[:, : 2 * ff]).astype(BF)
    hi = dgate.astype(BF).astype(F32)
    dx_ref[:, width:] = (hi * sel_ref[0:1, :] + (dgate - hi) * sel_ref[1:2, :]).astype(BF)

def expert_pass(x, dy, sel, wr, wg, wu, wd, tile):
    slots, width = x.shape
    part = wg[0].shape[1]; ff = 4 * part
    row = lambda w: pl.BlockSpec((tile, w), lambda i: (i, 0))
    whole = lambda a: pl.BlockSpec(a.shape, lambda i: (0, 0))
    return pl.pallas_call(
        functools.partial(expert_body, width, ff),
        grid=(slots // tile,),
        in_specs=[row(width), row(width + 128), whole(sel), whole(wr)] + [whole(a) for a in (*wg, *wu, *wd)],
        out_specs=[row(width), row(width + 128), row(ff), row(2 * ff), row(width)],
        out_shape=[jax.ShapeDtypeStruct((slots, w), BF) for w in (width, width + 128, ff, 2 * ff, width)],
        scratch_shapes=[pltpu.VMEM((width, 2 * ff + 128), BF), pltpu.VMEM((ff, width), BF)],
        compiler_params=pltpu.CompilerParams(vmem_limit_bytes=VM),
        cost_estimate=pl.CostEstimate(flops=12*slots*width*ff, bytes_accessed=12*slots*width, transcendentals=slots*ff),
        name="expert_pass",
    )(x, dy, sel, wr, *wg, *wu, *wd)

def slope_body(x_ref, dgu_ref, h_ref, dy_ref, own_g, own_u, own_d, *peers):
    part = own_g.shape[1]
    ff = h_ref.shape[1]
    gu = tdot(x_ref[...], dgu_ref[...])
    dn = tdot(h_ref[...], dy_ref[...])
    own_g[...] = gu[:, :part]
    own_u[...] = gu[:, ff : ff + part]
    own_d[...] = dn[:part]
    for k in (1, 2, 3):
        peers[2 * k - 2][0] = gu[:, k * part : (k + 1) * part].astype(BF)
        peers[2 * k - 2][1] = gu[:, ff + k * part : ff + (k + 1) * part].astype(BF)
        peers[2 * k - 1][...] = dn[k * part : (k + 1) * part].astype(BF)

def expert_slopes(x, dgu, h, dy, tile=256):
    slots, width = x.shape
    ff = h.shape[1]; part = ff // 4
    col = pl.BlockSpec((slots, tile), lambda i: (0, i))
    whole = lambda a: pl.BlockSpec(a.shape, lambda i: (0, 0))
    tall = pl.BlockSpec((tile, part), lambda i: (i, 0))
    wide = pl.BlockSpec((part, tile), lambda i: (0, i))
    pair = pl.BlockSpec((2, tile, part), lambda i: (0, i, 0))
    S = jax.ShapeDtypeStruct
    return pl.pallas_call(
        slope_body,
        grid=(width // tile,),
        in_specs=[col, whole(dgu), whole(h), col],
        out_specs=[tall, tall, wide] + [pair, wide] * 3,
        out_shape=[S((width, part), F32)] * 2 + [S((part, width), F32)] + [S((2, width, part), BF), S((part, width), BF)] * 3,
        compiler_params=pltpu.CompilerParams(vmem_limit_bytes=VM),
        cost_estimate=pl.CostEstimate(flops=6*slots*width*ff, bytes_accessed=8*slots*width, transcendentals=0),
        name="expert_slopes",
    )(x, dgu, h, dy)


def finish_body(experts, a_ref, b_ref, ao_ref, bo_ref, flag_ref, *refs):
    q_ref, k_ref, v_ref, r_ref, g_ref, o_ref, s_ref = refs
    turn = pl.program_id(0)
    second = flag_ref[0:1, 0:1]
    rows = q_ref.shape[0]
    half = a_ref.shape[3]
    kv = k_ref.shape[1]
    mine = a_ref[:, 0].astype(F32).reshape(rows, half)
    twin = b_ref[:, 0].astype(F32).reshape(rows, half)
    q_ref[...] = jnp.where(second > 0.5, twin, mine)
    rest = jnp.where(second > 0.5, mine, twin)
    k_ref[...] = rest[:, :kv]
    v_ref[...] = rest[:, kv : 2 * kv]

    @pl.when(turn == 0)
    def _():
        s_ref[...] = rest[:, 2 * kv :]

    @pl.when(turn > 0)
    def _():
        s_ref[...] += rest[:, 2 * kv :]

    @pl.when(turn == WS - 1)
    def _():
        turned = s_ref[...].T
        r_ref[...] = turned[:experts]
        g_ref[...] = turned[experts : experts + 8]

    mine = ao_ref[:, 0].astype(F32).reshape(rows, half)
    twin = bo_ref[:, 0].astype(F32).reshape(rows, half)
    use_twin = jnp.where(turn < 2, second, 1.0 - second)
    o_ref[...] = jnp.where(use_twin > 0.5, twin, mine)


def finish(experts, mine, twin, flag):
    chips, sets, step, half = mine.shape
    rows = chips * step
    first = pl.BlockSpec((chips, 1, step, half), lambda i: (0, i, 0, 0))
    later = pl.BlockSpec((chips, 1, step, half), lambda i: (0, WS + i % 2, 0, 0))
    kv = (half - 128) // 2
    S = jax.ShapeDtypeStruct
    return pl.pallas_call(
        functools.partial(finish_body, experts),
        grid=(WS,),
        in_specs=[first, first, later, later, pl.BlockSpec(flag.shape, lambda i: (0, 0))],
        out_specs=[
            pl.BlockSpec((rows, half), lambda i: (0, i)),
            pl.BlockSpec((rows, kv), lambda i: (0, i)),
            pl.BlockSpec((rows, kv), lambda i: (0, i)),
            pl.BlockSpec((experts, rows), lambda i: (0, 0)),
            pl.BlockSpec((8, rows), lambda i: (0, 0)),
            pl.BlockSpec((rows, half), lambda i: (0, i)),
        ],
        scratch_shapes=[pltpu.VMEM((rows, 128), F32)],
        out_shape=[
            S((rows, WS * half), F32),
            S((rows, WS * kv), F32),
            S((rows, WS * kv), F32),
            S((experts, rows), F32),
            S((8, rows), F32),
            S((rows, WS * half), F32),
        ],
        compiler_params=pltpu.CompilerParams(vmem_limit_bytes=VM),
        cost_estimate=pl.CostEstimate(flops=0, bytes_accessed=16 * rows * WS * half, transcendentals=0),
        name="finish",
    )(mine, twin, mine, twin, flag)


def whole(shape):
    return pl.BlockSpec(shape, lambda *_: (0,) * len(shape))


def sds(shape, kind):
    return jax.ShapeDtypeStruct(shape, kind)


def one_step(body, name, scalars, arrays, outs, scratch, flops):
    moved = sum(a.size * a.dtype.itemsize for a in arrays)
    return pl.pallas_call(
        body,
        in_specs=[pl.BlockSpec(memory_space=pltpu.SMEM)] * len(scalars)
        + [pl.BlockSpec(memory_space=pltpu.VMEM)] * len(arrays),
        out_specs=[pl.BlockSpec(memory_space=pltpu.VMEM)] * len(outs),
        out_shape=outs,
        scratch_shapes=scratch,
        compiler_params=pltpu.CompilerParams(vmem_limit_bytes=VM),
        cost_estimate=pl.CostEstimate(flops=flops, bytes_accessed=moved, transcendentals=0),
        name=name,
    )(*scalars, *arrays)


def other_half(v):
    lanes = v.shape[1]
    low = lax.broadcasted_iota(jnp.int32, v.shape, 1) % HEAD < HEAD // 2
    ahead = pltpu.roll(v, lanes - HEAD // 2, 1)
    behind = pltpu.roll(v, HEAD // 2, 1)
    return jnp.where(low, ahead, behind)


def wide(ref, times):
    return jnp.concatenate([ref[...]] * times, axis=1)


def rms(x):
    return lax.rsqrt(jnp.mean(x * x, axis=1, keepdims=True) + EPS)


def column_sum(m, lane):
    hi, lo = split(m)
    pick = (lax.broadcasted_iota(jnp.int32, (m.shape[0], 128), 1) == lane).astype(F32).astype(BF)
    return tdot(hi, pick) + tdot(lo, pick)


def pack_body(experts, place_ref, wq, wk, wv, wr, na, nm, *outs):
    small = outs[WS + 1]
    me, core = place_ref[0], place_ref[1]
    strip = wq.shape[0] // 2
    q_w, kv_w = wq.shape[1] // WS, wk.shape[1] // WS
    shard = wq.shape[0]
    gains = jnp.concatenate(
        [na[...].astype(F32), nm[...].astype(F32), jnp.zeros((6, shard), F32)], axis=0
    ).T
    small[...] = jnp.concatenate(
        [wr[...].astype(F32), gains, jnp.zeros((shard, 128 - experts - 8), F32)], axis=1
    ).astype(BF)
    for r in range(WS + 1):
        side = core if r < WS else 1 - core
        d = lax.rem(me + WS - r % WS, WS)
        part = pl.ds(pl.multiple_of(side * strip, 64), strip)
        outs[r][:, :q_w] = wq[part, pl.ds(pl.multiple_of(d * q_w, 128), q_w)]
        spot = pl.ds(pl.multiple_of(d * kv_w, 128), kv_w)
        outs[r][:, q_w : q_w + kv_w] = wk[part, spot]
        outs[r][:, q_w + kv_w : q_w + 2 * kv_w] = wv[part, spot]
        outs[r][:, q_w + 2 * kv_w :] = small[part, :]


def pack(experts, place, wq, wk, wv, wr, na, nm):
    shard = wq.shape[0]
    wide_w = (wq.shape[1] + 2 * wk.shape[1]) // WS + 128
    return one_step(
        functools.partial(pack_body, experts),
        "pack",
        [place],
        [wq, wk, wv, wr, na[None], nm[None]],
        [sds((shard // 2, wide_w), BF)] * (WS + 1),
        [pltpu.VMEM((shard, 128), BF)],
        0,
    )


def attend_body(experts, place_ref, *refs):
    xs, own, twin = refs[0:4], refs[4:8], refs[8:12]
    cos_ref, sin_ref, bias_ref, wo_ref = refs[12:16]
    h1_ref, qkv_ref, o_ref, lse_ref, w_ref, small_ref, rows_ref = refs[16:23]
    parts = refs[23:27]
    me, core = place_ref[0], place_ref[1]
    rows = xs[0].shape[0]
    strip = own[0].shape[0]
    heads = o_ref.shape[1] // HEAD
    q_w = heads * HEAD
    qkv_w = qkv_ref.shape[1]
    kv_w = (qkv_w - q_w) // 2
    group = q_w // kv_w
    for r in range(WS):
        base = lax.rem(me + r, WS) * (2 * strip)
        for source, side in ((own[r], core), (twin[r], 1 - core)):
            spot = pl.ds(pl.multiple_of(base + side * strip, 64), strip)
            w_ref[spot, :] = source[:, :qkv_w]
            small_ref[spot, :] = source[:, qkv_w:]
    turned = small_ref[...].astype(F32).T
    rows_ref[...] = jnp.concatenate(
        [turned[experts : experts + 2], jnp.zeros((6, turned.shape[1]), F32)], axis=0
    )
    gain = turned[experts : experts + 1]
    for r in range(WS):
        x = xs[r][...].astype(F32)
        h1_ref[r * rows : (r + 1) * rows, :] = (x * rms(x) * gain).astype(BF)
    qkv = dot(h1_ref[...], w_ref[...])
    qk = qkv[:, : q_w + kv_w]
    times = (q_w + kv_w) // 128
    qk = qk * wide(cos_ref, times) + other_half(qk) * wide(sin_ref, times)
    qkv_ref[:, : q_w + kv_w] = qk.astype(BF)
    qkv_ref[:, q_w + kv_w :] = qkv[:, q_w + kv_w :].astype(BF)
    for h in range(heads):
        at = h // group * HEAD
        q = qkv_ref[:, h * HEAD : (h + 1) * HEAD]
        k = qkv_ref[:, q_w + at : q_w + at + HEAD]
        v = qkv_ref[:, q_w + kv_w + at : q_w + kv_w + at + HEAD]
        s = dot_t(q, k) * HEAD ** (-0.5) + bias_ref[...]
        peak = jnp.max(s, axis=1, keepdims=True)
        p = jnp.exp(s - peak)
        total = jnp.sum(p, axis=1, keepdims=True)
        lse_ref[:, h : h + 1] = peak + jnp.log(total)
        o_ref[:, h * HEAD : (h + 1) * HEAD] = dot((p / total).astype(BF), v).astype(BF)
    for r in range(WS):
        part = dot(o_ref[r * rows : (r + 1) * rows, :], wo_ref[...])
        parts[r][...] = part.astype(parts[r].dtype)


def attend(experts, place, xs, own, twin, cos, sin, bias, wo):
    rows, width = xs[0].shape
    tree = rows * WS
    q_w, qkv_w = wo.shape[0], own[0].shape[1] - 128
    outs = [
        sds((tree, width), BF),
        sds((tree, qkv_w), BF),
        sds((tree, q_w), BF),
        sds((tree, 128), F32),
        sds((width, qkv_w), BF),
        sds((width, 128), BF),
        sds((8, width), F32),
        sds((rows, width), F32),
    ] + [sds((rows, width), BF)] * 3
    flops = 2 * tree * width * (qkv_w + q_w) + 4 * tree * tree * q_w
    return one_step(
        functools.partial(attend_body, experts),
        "attend",
        [place],
        [*xs, *own, *twin, cos, sin, bias, wo],
        outs,
        [],
        flops,
    )


def enter_body(x_ref, p0, p1, p2, p3, rows_ref, router_ref, slot_ref, chosen_ref, spread_ref, *outs):
    x2_ref, h2_ref, send_ref, gates_ref, gs_ref = outs
    x2 = x_ref[...].astype(F32) + p0[...]
    for p in (p1, p2, p3):
        x2 = x2 + p[...].astype(F32)
    x2_ref[...] = x2
    h2 = (x2 * rms(x2) * rows_ref[1:2, :]).astype(BF)
    h2_ref[...] = h2
    send_ref[...] = tdot(slot_ref[...], h2).astype(BF)
    logits = dot(h2, router_ref[...])
    mask = chosen_ref[...].astype(F32) > 0.5
    logits = jnp.where(mask, logits, MASKED)
    lifted = jnp.where(mask, jnp.exp(logits - jnp.max(logits, axis=1, keepdims=True)), 0.0)
    gates = lifted / jnp.maximum(jnp.sum(lifted, axis=1, keepdims=True), 1e-30)
    gates_ref[...] = gates
    hi, lo = split(gates)
    on_slots = dot(hi, spread_ref[...]) + dot(lo, spread_ref[...])
    hi, lo = split(on_slots * slot_ref[...].astype(F32))
    rows = x2.shape[0]
    gs_ref[:rows, :] = hi
    gs_ref[rows:, :] = lo


def enter(x, parts, rows, router, to_slot, chosen, spread):
    n, width = x.shape
    slots = to_slot.shape[1]
    outs = [
        sds((n, width), F32),
        sds((n, width), BF),
        sds((slots, width), BF),
        sds((n, 128), F32),
        sds((2 * n, slots), BF),
    ]
    return one_step(
        enter_body,
        "enter",
        [],
        [x, *parts, rows, router, to_slot, chosen, spread],
        outs,
        [],
        2 * n * width * slots,
    )


def leave_body(experts, back_ref, slot_ref, gates_ref, router_ref, x2_ref, h2_ref, rows_ref, cot_ref, *outs):
    dx2_ref, da_ref, small_ref = outs
    width = x2_ref.shape[1]
    back = dot(slot_ref[...], back_ref[...])
    tail = back[:, width:]
    dgate = tail + pltpu.roll(tail, 128 - experts, 1)
    gates = gates_ref[...]
    dl = gates * (dgate - jnp.sum(gates * dgate, axis=1, keepdims=True))
    hi, lo = split(dl)
    dh2 = back[:, :width] + dot_t(hi, router_ref[...]) + dot_t(lo, router_ref[...])
    x2 = x2_ref[...]
    scale, gain = rms(x2), rows_ref[1:2, :]
    inner = jnp.mean(gain * dh2 * x2, axis=1, keepdims=True)
    dx2 = cot_ref[...].astype(F32) + scale * gain * dh2 - x2 * scale * scale * scale * inner
    dx2_ref[...] = dx2
    da_ref[...] = dx2.astype(BF)
    h2 = h2_ref[...]
    small_ref[...] = tdot(h2, hi) + tdot(h2, lo) + column_sum(dh2 * x2 * scale, experts)


def leave(experts, back, to_slot, gates, router, x2, h2, rows, cot):
    n, width = x2.shape
    outs = [sds((n, width), F32), sds((n, width), BF), sds((width, 128), F32)]
    return one_step(
        functools.partial(leave_body, experts),
        "leave",
        [],
        [back, to_slot, gates, router, x2, h2, rows, cot],
        outs,
        [],
        2 * n * back.size,
    )


def attend_back_body(experts, place_ref, *refs):
    das, xs = refs[0:4], refs[4:8]
    wo_ref, qkv_ref, o_ref, lse_ref, h1_ref, w_ref = refs[8:14]
    cos_ref, sin_ref, bias_ref, small_ref = refs[14:18]
    keep_ref, give_ref = refs[18:20]
    parts = refs[20:24]
    da, do, dqk, dqkv = refs[24:28]
    core = place_ref[1]
    rows = xs[0].shape[0]
    q_w, qkv_w = o_ref.shape[1], qkv_ref.shape[1]
    kv_w = (qkv_w - q_w) // 2
    group = q_w // kv_w
    scale = HEAD ** (-0.5)
    for r in range(WS):
        da[r * rows : (r + 1) * rows, :] = das[r][...]
    do[...] = dot_t(da[...], wo_ref[...]).astype(BF)
    for n in range(kv_w // HEAD):
        at = n * HEAD
        k = qkv_ref[:, q_w + at : q_w + at + HEAD]
        v = qkv_ref[:, q_w + kv_w + at : q_w + kv_w + at + HEAD]
        dk, dv = None, None
        for h in range(n * group, (n + 1) * group):
            q = qkv_ref[:, h * HEAD : (h + 1) * HEAD]
            doh = do[:, h * HEAD : (h + 1) * HEAD]
            p = jnp.exp(dot_t(q, k) * scale + bias_ref[...] - lse_ref[:, h : h + 1])
            dp = dot_t(doh, v)
            delta = jnp.sum(p * dp, axis=1, keepdims=True)
            ds = (p * (dp - delta)).astype(BF)
            dqk[:, h * HEAD : (h + 1) * HEAD] = dot(ds, k) * scale
            more_k, more_v = tdot(ds, q), tdot(p.astype(BF), doh)
            dk = more_k if dk is None else dk + more_k
            dv = more_v if dv is None else dv + more_v
        dqk[:, q_w + at : q_w + at + HEAD] = dk * scale
        dqkv[:, q_w + kv_w + at : q_w + kv_w + at + HEAD] = dv.astype(BF)
    dqkv[:, qkv_w:] = jnp.zeros((da.shape[0], 128), BF)
    d = dqk[...]
    times = (q_w + kv_w) // 128
    d = d * wide(cos_ref, times) - other_half(d) * wide(sin_ref, times)
    dqkv[:, : q_w + kv_w] = d.astype(BF)
    small = small_ref[...]
    for r in range(WS):
        dh1 = dot_t(dqkv[r * rows : (r + 1) * rows, :qkv_w], w_ref[...])
        parts[r][...] = dh1.astype(parts[r].dtype)
        x = xs[r][...].astype(F32)
        small = small + column_sum(dh1 * x * rms(x), experts + 1)
    half = keep_ref.shape[3]
    chips, step = keep_ref.shape[0], keep_ref.shape[2]
    count = chips * step

    def put(i, first, second):
        kept = jnp.where(core == 0, first, second)
        given = jnp.where(core == 0, second, first)
        keep_ref[:, i] = kept.reshape(chips, step, half)
        give_ref[:, i] = given.reshape(chips, step, half).astype(BF)

    for i in range(WS):
        both = tdot(h1_ref[:, i * count : (i + 1) * count], dqkv[...])
        mine = small[i * count : (i + 1) * count]
        second = jnp.concatenate([both[:, half : 2 * half - 128], both[:, 2 * half - 128 :] + mine], axis=1)
        put(i, both[:, :half], second)
    slope = tdot(o_ref[...], da[...])
    for i in range(2):
        put(WS + i, slope[:, i * half : (i + 1) * half], slope[:, (2 + i) * half : (3 + i) * half])


def attend_back(experts, place, das, xs, wo, qkv, o, lse, h1, w, cos, sin, bias, small):
    rows, width = xs[0].shape
    tree = rows * WS
    q_w, qkv_w = wo.shape[0], qkv.shape[1]
    half = (qkv_w + 128) // 2
    load = (CHIPS, WS + 2, width // WS // CHIPS, half)
    outs = [sds(load, F32), sds(load, BF), sds((rows, width), F32)] + [sds((rows, width), BF)] * 3
    scratch = [
        pltpu.VMEM((tree, width), BF),
        pltpu.VMEM((tree, q_w), BF),
        pltpu.VMEM((tree, (q_w + qkv_w) // 2), F32),
        pltpu.VMEM((tree, qkv_w + 128), BF),
    ]
    flops = 4 * tree * width * (qkv_w + q_w) + 10 * tree * tree * q_w
    return one_step(
        functools.partial(attend_back_body, experts),
        "attend_back",
        [place],
        [*das, *xs, wo, qkv, o, lse, h1, w, cos, sin, bias, small],
        outs,
        scratch,
        flops,
    )


def shards(
    tokens,
    cotangent,
    seg_lengths,
    parents,
    routes,
    norm_attn,
    w_query,
    w_key,
    w_value,
    w_out,
    norm_moe,
    w_router,
    w_gate,
    w_up,
    w_down,
):
    me = lax.axis_index("ws")
    expert = lax.axis_index("exp")
    core = expert % 2
    place = jnp.stack([me, core]).astype(jnp.int32)
    rows, width = tokens.shape
    shard = width // WS
    strip = shard // 2
    experts = 2 * CHIPS
    q_w, kv_w = HEADS // WS * HEAD, KV_HEADS // WS * HEAD
    slots = experts * CAP

    def gathered(v):
        return [v] + [from_peer(v, k) for k in (1, 2, 3)]

    xs = gathered(tokens)

    pieces = pack(experts, place, w_query, w_key, w_value, w_router, norm_attn, norm_moe)
    pieces, routes = lax.optimization_barrier((pieces, routes))
    own = [pieces[0]] + [from_peer(pieces[k], k) for k in (1, 2, 3)]
    twin = [pieces[WS]] + [other_core(own[k]) for k in (1, 2, 3)]

    labels = jnp.arange(experts, dtype=jnp.int32)
    lane = jnp.arange(128, dtype=jnp.int32)
    chosen = jnp.any(routes[:, :, None] == lane[None, None, :], axis=1)
    row_id = jnp.arange(rows, dtype=jnp.int32)
    before = (row_id[None, :] < row_id[:, None]).astype(BF)
    rank = dot(before, chosen.astype(BF))
    col = jnp.arange(slots, dtype=jnp.int32)
    spread = (col[None, :] // CAP == lane[:, None]).astype(BF)
    spot = dot(jnp.where(chosen, rank + 1.0, 0.0).astype(BF), spread)
    nothing = (xs[1][:1, :1] + xs[3][:1, :1]).astype(F32) * 0.0
    to_slot = (spot == (col % CAP + 1).astype(F32)[None, :] + nothing).astype(BF)
    chosen = chosen.astype(BF)
    extra = jnp.concatenate([cotangent, chosen], axis=1)
    dy_send = tdot(to_slot, extra).astype(BF).reshape(experts, CAP, width + 128)
    dy_slots = lax.all_to_all(dy_send, "exp", 0, 0, tiled=True).reshape(slots, width + 128)

    order = (
        ((me + jnp.arange(WS, dtype=jnp.int32)) % WS)[:, None] * rows + row_id[None, :]
    ).reshape(-1)
    visible, position = tree_layout(seg_lengths[0], parents[0], order)
    bias = jnp.where(visible, 0.0, MASKED).astype(F32)
    inverse = THETA ** (-(lane % (HEAD // 2)).astype(F32) * 2.0 / HEAD)
    angles = position.astype(F32)[:, None] * inverse[None, :]
    cosines = jnp.cos(angles)
    sines = jnp.where((lane % HEAD < HEAD // 2)[None, :], -1.0, 1.0) * jnp.sin(angles)
    h1, qkv, o, lse, w_qkv, small_full, gains, *parts = attend(
        experts, place, xs, own, twin, cosines, sines, bias, w_out
    )
    sums = [parts[0]] + [to_peer(parts[k], k) for k in (1, 2, 3)]
    x2, h2, x_send, gates, gate_slots = enter(
        tokens, sums, gains, small_full, to_slot, chosen, spread
    )
    x_send, wg_own, wu_own, wd_own = lax.optimization_barrier(
        (x_send, w_gate[0], w_up[0], w_down[0])
    )
    x_slots = lax.all_to_all(
        x_send.reshape(experts, CAP, width), "exp", 0, 0, tiled=True
    ).reshape(slots, width)

    sel = jnp.concatenate(
        [
            (lane == expert).astype(F32)[None],
            (lane == expert + experts).astype(F32)[None],
            jnp.zeros((6, 128), F32),
        ],
        axis=0,
    )
    y, dx_send, hidden, d_gu, d_y = expert_pass(
        x_slots, dy_slots, sel, small_full, gathered(wg_own), gathered(wu_own), gathered(wd_own), 512
    )
    dx_back = lax.all_to_all(
        dx_send.reshape(experts, CAP, width + 128), "exp", 0, 0, tiled=True
    ).reshape(slots, width + 128)

    own_g, own_u, own_d, gu1, dn1, gu2, dn2, gu3, dn3 = expert_slopes(x_slots, d_gu, hidden, d_y)
    gu1, dn1 = to_peer(gu1, 1), to_peer(dn1, 1)
    gu3, dn3 = to_peer(gu3, 3), to_peer(dn3, 3)
    gu2, dn2 = to_peer(gu2, 2), to_peer(dn2, 2)
    dx_back, y, gu1, dn1, gu2, dn2, gu3, dn3 = lax.optimization_barrier(
        (dx_back, y, gu1, dn1, gu2, dn2, gu3, dn3)
    )
    y_back = lax.all_to_all(y.reshape(experts, CAP, width), "exp", 0, 0, tiled=True).reshape(
        slots, width
    )

    dx2, d_a, small_terms = leave(
        experts, dx_back, to_slot, gates, small_full, x2, h2, gains, cotangent
    )
    das = gathered(d_a)
    grad_gu = jnp.stack([own_g, own_u]) + gu1.astype(F32) + gu2.astype(F32) + gu3.astype(F32)
    grad_wg, grad_wu = grad_gu[0][None], grad_gu[1][None]
    grad_wd = (own_d + dn1.astype(F32) + dn2.astype(F32) + dn3.astype(F32))[None]
    keep, give, *slopes = attend_back(
        experts, place, das, xs, w_out, qkv, o, lse, h1, w_qkv, cosines, sines, bias, small_terms
    )
    dh1 = slopes[0]
    for k in (1, 2, 3):
        dh1 = dh1 + to_peer(slopes[k], k).astype(F32)
    resid = tokens.astype(F32)
    scale = lax.rsqrt(jnp.mean(resid * resid, axis=-1, keepdims=True) + EPS)
    inner = jnp.mean(gains[0:1] * dh1 * resid, axis=-1, keepdims=True)
    grad_tokens = dx2 + scale * gains[0:1] * dh1 - resid * scale * scale * scale * inner

    half = (q_w + 2 * kv_w + 128) // 2
    flag = jnp.broadcast_to(jnp.stack([core, 1 - core]).astype(F32)[:, None], (2, 128))
    flag = jnp.concatenate([flag, jnp.zeros((6, 128), F32)], axis=0)
    give, y_back = lax.optimization_barrier((give, y_back))
    sent = (keep + other_core(give).astype(F32)).astype(BF)
    step = shard // CHIPS
    both = dot(gate_slots, y_back)
    layer_out = (x2 + both[:rows] + both[rows:]).astype(BF)
    got = same_core(sent)
    got, layer_out, grad_tokens, grad_wg, grad_wu, grad_wd = lax.optimization_barrier(
        (got, layer_out, grad_tokens, grad_wg, grad_wu, grad_wd)
    )
    total = jnp.sum(got.astype(F32), axis=0).astype(BF)
    turned = jnp.stack(
        [lax.dynamic_index_in_dim(total, me, 0, False)]
        + [
            from_peer(lax.dynamic_index_in_dim(total, (me - k) % WS, 0, False), k)
            for k in (1, 2, 3)
        ]
    )
    turned = lax.dynamic_slice_in_dim(jnp.concatenate([turned, turned]), (WS - me) % WS, WS, 0)
    final = jnp.concatenate([turned, total[WS:]], axis=0)
    spread_out = same_core(jnp.broadcast_to(final, (CHIPS,) + final.shape))
    twin_out = other_core(spread_out)
    sum_query, sum_key, sum_value, sum_router, sum_gains, sum_out = finish(
        experts, spread_out, twin_out, flag
    )

    return (
        layer_out,
        grad_tokens,
        sum_gains[1],
        sum_query,
        sum_key,
        sum_value,
        sum_out,
        sum_gains[0],
        sum_router.T,
        grad_wg,
        grad_wu,
        grad_wd,
    )


def solution(mesh):
    rows = P(("exp", "ws"), None)
    placed = (
        rows,
        rows,
        P("exp", None),
        P("exp", None),
        rows,
        P("ws"),
        P("ws", None),
        P("ws", None),
        P("ws", None),
        P("ws", None),
        P("ws"),
        P("ws", None),
        P("exp", None, "ws"),
        P("exp", None, "ws"),
        P("exp", "ws", None),
    )
    return jax.shard_map(
        shards,
        mesh=mesh,
        in_specs=placed,
        out_specs=(
            rows,
            rows,
            P("ws"),
            P("ws", None),
            P("ws", None),
            P("ws", None),
            P("ws", None),
            P("ws"),
            P("ws", None),
            P("exp", None, "ws"),
            P("exp", None, "ws"),
            P("exp", "ws", None),
        ),
        check_vma=False,
    )
```

```python
import functools

import jax
import jax.numpy as jnp
from jax import lax
from jax.experimental import pallas as pl
from jax.experimental.pallas import tpu as pltpu
from jax.sharding import PartitionSpec as P

HEADS = 24
KV_HEADS = 8
HEAD = 64
EPS = 1e-06
THETA = 10000.0
MASKED = -1e30
BF = jnp.bfloat16
F32 = jnp.float32
WS = 4
CHIPS = 16
CAP = 48
VM = 60 * 1024 * 1024


def dot(a, b):
    return jnp.dot(a, b, preferred_element_type=F32)


def dot_t(a, b):
    return lax.dot_general(a, b, (((1,), (1,)), ((), ())), preferred_element_type=F32)


def tdot(a, b):
    return lax.dot_general(a, b, (((0,), (0,)), ((), ())), preferred_element_type=F32)


def split(v):
    hi = v.astype(BF)
    return hi, (v - hi.astype(F32)).astype(BF)


def from_peer(v, k):
    return lax.ppermute(v, "ws", [(s, (s - k) % WS) for s in range(WS)])


def to_peer(v, k):
    return lax.ppermute(v, "ws", [(s, (s + k) % WS) for s in range(WS)])


def other_core(v):
    return lax.ppermute(v, "exp", [(s, s ^ 1) for s in range(2 * CHIPS)])


def same_core(v):
    groups = [[2 * chip + core for chip in range(CHIPS)] for core in range(2)]
    return lax.all_to_all(v, "exp", 0, 0, tiled=True, axis_index_groups=groups)


def tree_layout(lengths, parents, token_index):
    seg = lengths.shape[0]
    labels = jnp.arange(seg, dtype=jnp.int32)
    segment_end = jnp.cumsum(lengths, dtype=jnp.int32)
    starts = segment_end - lengths
    segment = jnp.sum((token_index[:, None] >= segment_end[None, :]).astype(jnp.int32), axis=1)
    reach = ((parents[:, None] == labels[None, :]) | (labels[:, None] == labels[None, :])).astype(
        BF
    )
    for _ in range(4):
        reach = (dot(reach, reach) > 0.5).astype(BF)
    above = jnp.sum(reach.astype(jnp.int32) * lengths[None, :], axis=1) - lengths
    members = segment[:, None] == labels[None, :]
    position = jnp.sum(jnp.where(members, (above - starts)[None, :], 0), axis=1) + token_index
    members = members.astype(BF)
    reaches = dot(members, reach).astype(BF)
    visible = (dot_t(reaches, members) > 0.5) & (token_index[None, :] <= token_index[:, None])
    return visible, position


def expert_body(width, ff, x_ref, dy_ref, sel_ref, wr_ref, *rest):
    wg, wu, wd = rest[0:4], rest[4:8], rest[8:12]
    dx_ref, h_ref, dgu_ref, gate_ref = rest[12:16]
    wgu, wdn = rest[16:]
    part = wg[0].shape[1]

    @pl.when(pl.program_id(0) == 0)
    def _():
        for r in range(WS):
            wgu[:, r * part : (r + 1) * part] = wg[r][...]
            wgu[:, ff + r * part : ff + (r + 1) * part] = wu[r][...]
            wdn[r * part : (r + 1) * part, :] = wd[r][...]
        wgu[:, 2 * ff :] = wr_ref[...]

    pre = dot(x_ref[...], wgu[...])
    g, u, logits = pre[:, :ff], pre[:, ff : 2 * ff], pre[:, 2 * ff :]
    mask = dy_ref[:, width:].astype(F32) > 0.5
    logits = jnp.where(mask, logits, MASKED)
    lifted = jnp.where(mask, jnp.exp(logits - jnp.max(logits, axis=1, keepdims=True)), 0.0)
    total = jnp.maximum(jnp.sum(lifted, axis=1, keepdims=True), 1e-30)
    gate = jnp.sum(lifted * sel_ref[0:1, :], axis=1, keepdims=True) / total
    gate_ref[...] = jnp.broadcast_to(gate, gate_ref.shape)
    sig = 1.0 / (1.0 + jnp.exp(-g))
    silu = g * sig
    h = (silu * u).astype(BF)
    h_ref[...] = h
    raw = dot_t(dy_ref[:, :width], wdn[...])
    dgate = jnp.sum(raw * h.astype(F32), axis=1, keepdims=True)
    dh = raw * gate
    dgu_ref[:, :ff] = (dh * u * sig * (1.0 + g * (1.0 - sig))).astype(BF)
    dgu_ref[:, ff:] = (dh * silu).astype(BF)
    dx_ref[:, :width] = dot_t(dgu_ref[...], wgu[:, : 2 * ff]).astype(BF)
    hi = dgate.astype(BF).astype(F32)
    dx_ref[:, width:] = (hi * sel_ref[0:1, :] + (dgate - hi) * sel_ref[1:2, :]).astype(BF)


def expert_pass(x, dy, sel, wr, wg, wu, wd, tile):
    slots, width = x.shape
    part = wg[0].shape[1]
    ff = WS * part
    row = lambda w: pl.BlockSpec((tile, w), lambda i: (i, 0))
    once = lambda a: pl.BlockSpec(a.shape, lambda i: (0, 0))
    return pl.pallas_call(
        functools.partial(expert_body, width, ff),
        grid=(slots // tile,),
        in_specs=[row(width), row(width + 128), once(sel), once(wr)]
        + [once(a) for a in (*wg, *wu, *wd)],
        out_specs=[row(width + 128), row(ff), row(2 * ff), row(128)],
        out_shape=[
            jax.ShapeDtypeStruct((slots, width + 128), BF),
            jax.ShapeDtypeStruct((slots, ff), BF),
            jax.ShapeDtypeStruct((slots, 2 * ff), BF),
            jax.ShapeDtypeStruct((slots, 128), F32),
        ],
        scratch_shapes=[pltpu.VMEM((width, 2 * ff + 128), BF), pltpu.VMEM((ff, width), BF)],
        compiler_params=pltpu.CompilerParams(vmem_limit_bytes=VM),
        cost_estimate=pl.CostEstimate(
            flops=10 * slots * width * ff, bytes_accessed=9 * slots * width, transcendentals=0
        ),
        name="expert_pass",
    )(x, dy, sel, wr, *wg, *wu, *wd)


def slope_body(x_ref, dgu_ref, h_ref, dy_ref, gate_ref, *refs):
    wd = refs[0:4]
    y_ref, own_g, own_u, own_d = refs[4:8]
    peers = refs[8:]
    part = own_g.shape[1]
    ff = h_ref.shape[1]
    gu = tdot(x_ref[...], dgu_ref[...])
    d_y = (gate_ref[:, 0:1] * dy_ref[...].astype(F32)).astype(BF)
    dn = tdot(h_ref[...], d_y)
    y_ref[...] = dot(h_ref[...], jnp.concatenate([w[...] for w in wd], axis=0)).astype(BF)
    own_g[...] = gu[:, :part]
    own_u[...] = gu[:, ff : ff + part]
    own_d[...] = dn[:part]
    for k in (1, 2, 3):
        peers[2 * k - 2][0] = gu[:, k * part : (k + 1) * part].astype(BF)
        peers[2 * k - 2][1] = gu[:, ff + k * part : ff + (k + 1) * part].astype(BF)
        peers[2 * k - 1][...] = dn[k * part : (k + 1) * part].astype(BF)


def expert_slopes(x, dgu, h, dy, gate, wd, tile=256):
    slots, width = x.shape
    ff = h.shape[1]
    part = ff // WS
    col = pl.BlockSpec((slots, tile), lambda i: (0, i))
    once = lambda a: pl.BlockSpec(a.shape, lambda i: (0, 0))
    tall = pl.BlockSpec((tile, part), lambda i: (i, 0))
    flat = pl.BlockSpec((part, tile), lambda i: (0, i))
    pair = pl.BlockSpec((2, tile, part), lambda i: (0, i, 0))
    S = jax.ShapeDtypeStruct
    return pl.pallas_call(
        slope_body,
        grid=(width // tile,),
        in_specs=[col, once(dgu), once(h), col, once(gate)] + [flat] * WS,
        out_specs=[col, tall, tall, flat] + [pair, flat] * 3,
        out_shape=[S((slots, width), BF)]
        + [S((width, part), F32)] * 2
        + [S((part, width), F32)]
        + [S((2, width, part), BF), S((part, width), BF)] * 3,
        compiler_params=pltpu.CompilerParams(vmem_limit_bytes=VM),
        cost_estimate=pl.CostEstimate(
            flops=8 * slots * width * ff, bytes_accessed=8 * slots * width, transcendentals=0
        ),
        name="expert_slopes",
    )(x, dgu, h, dy, gate, *wd)


def finish_body(experts, place_ref, a_ref, b_ref, ao_ref, bo_ref, flag_ref, *refs):
    q_ref, k_ref, v_ref, r_ref, g_ref, o_ref, s_ref = refs
    turn = pl.program_id(0)
    second = flag_ref[0:1, 0:1]
    rows = q_ref.shape[0]
    half = a_ref.shape[3]
    kv = k_ref.shape[1]
    mine = a_ref[:, 0].astype(F32).reshape(rows, half)
    twin = b_ref[:, 0].astype(F32).reshape(rows, half)
    q_ref[...] = jnp.where(second > 0.5, twin, mine)
    rest = jnp.where(second > 0.5, mine, twin)
    k_ref[...] = rest[:, :kv]
    v_ref[...] = rest[:, kv : 2 * kv]

    @pl.when(turn == 0)
    def _():
        s_ref[...] = rest[:, 2 * kv :]

    @pl.when(turn > 0)
    def _():
        s_ref[...] += rest[:, 2 * kv :]

    @pl.when(turn == WS - 1)
    def _():
        turned = s_ref[...].T
        r_ref[...] = turned[:experts]
        g_ref[...] = turned[experts : experts + 8]

    mine = ao_ref[:, 0].astype(F32).reshape(rows, half)
    twin = bo_ref[:, 0].astype(F32).reshape(rows, half)
    use_twin = jnp.where(turn < 2, second, 1.0 - second)
    o_ref[...] = jnp.where(use_twin > 0.5, twin, mine)


def finish(experts, place, mine, twin, flag):
    chips, sets, step, half = mine.shape
    rows = chips * step
    first = pl.BlockSpec((chips, 1, step, half), lambda i, p: (0, i, 0, 0))
    later = pl.BlockSpec((chips, 1, step, half), lambda i, p: (0, WS + i % 2, 0, 0))
    turned = lambda i, p: (0, lax.rem(p[0] + i, WS))
    kv = (half - 128) // 2
    S = jax.ShapeDtypeStruct
    return pl.pallas_call(
        functools.partial(finish_body, experts),
        grid_spec=pltpu.PrefetchScalarGridSpec(
            num_scalar_prefetch=1,
            grid=(WS,),
            in_specs=[first, first, later, later, whole(flag.shape)],
            out_specs=[
                pl.BlockSpec((rows, half), turned),
                pl.BlockSpec((rows, kv), turned),
                pl.BlockSpec((rows, kv), turned),
                whole((experts, rows)),
                whole((8, rows)),
                pl.BlockSpec((rows, half), lambda i, p: (0, i)),
            ],
            scratch_shapes=[pltpu.VMEM((rows, 128), F32)],
        ),
        out_shape=[
            S((rows, WS * half), F32),
            S((rows, WS * kv), F32),
            S((rows, WS * kv), F32),
            S((experts, rows), F32),
            S((8, rows), F32),
            S((rows, WS * half), F32),
        ],
        compiler_params=pltpu.CompilerParams(vmem_limit_bytes=VM),
        cost_estimate=pl.CostEstimate(flops=0, bytes_accessed=16 * rows * WS * half, transcendentals=0),
        name="finish",
    )(place, mine, twin, mine, twin, flag)


def whole(shape):
    return pl.BlockSpec(shape, lambda *_: (0,) * len(shape))


def sds(shape, kind):
    return jax.ShapeDtypeStruct(shape, kind)


def one_step(body, name, scalars, arrays, outs, scratch, flops):
    moved = sum(a.size * a.dtype.itemsize for a in arrays)
    return pl.pallas_call(
        body,
        in_specs=[pl.BlockSpec(memory_space=pltpu.SMEM)] * len(scalars)
        + [pl.BlockSpec(memory_space=pltpu.VMEM)] * len(arrays),
        out_specs=[pl.BlockSpec(memory_space=pltpu.VMEM)] * len(outs),
        out_shape=outs,
        scratch_shapes=scratch,
        compiler_params=pltpu.CompilerParams(vmem_limit_bytes=VM),
        cost_estimate=pl.CostEstimate(flops=flops, bytes_accessed=moved, transcendentals=0),
        name=name,
    )(*scalars, *arrays)


def other_half(v):
    lanes = v.shape[1]
    low = lax.broadcasted_iota(jnp.int32, v.shape, 1) % HEAD < HEAD // 2
    ahead = pltpu.roll(v, lanes - HEAD // 2, 1)
    behind = pltpu.roll(v, HEAD // 2, 1)
    return jnp.where(low, ahead, behind)


def wide(ref, times):
    return jnp.concatenate([ref[...]] * times, axis=1)


def rms(x):
    return lax.rsqrt(jnp.mean(x * x, axis=1, keepdims=True) + EPS)


def column_sum(m, lane):
    hi, lo = split(m)
    pick = (lax.broadcasted_iota(jnp.int32, (m.shape[0], 128), 1) == lane).astype(F32).astype(BF)
    return tdot(hi, pick) + tdot(lo, pick)


def pack_body(experts, place_ref, wq, wk, wv, wr, na, nm, *outs):
    small = outs[WS + 1]
    me, core = place_ref[0], place_ref[1]
    strip = wq.shape[0] // 2
    q_w, kv_w = wq.shape[1] // WS, wk.shape[1] // WS
    shard = wq.shape[0]
    gains = jnp.concatenate(
        [na[...].astype(F32), nm[...].astype(F32), jnp.zeros((6, shard), F32)], axis=0
    ).T
    small[...] = jnp.concatenate(
        [wr[...].astype(F32), gains, jnp.zeros((shard, 128 - experts - 8), F32)], axis=1
    ).astype(BF)
    for r in range(WS + 1):
        side = core if r < WS else 1 - core
        d = lax.rem(me + WS - r % WS, WS)
        part = pl.ds(pl.multiple_of(side * strip, 64), strip)
        outs[r][:, :q_w] = wq[part, pl.ds(pl.multiple_of(d * q_w, 128), q_w)]
        spot = pl.ds(pl.multiple_of(d * kv_w, 128), kv_w)
        outs[r][:, q_w : q_w + kv_w] = wk[part, spot]
        outs[r][:, q_w + kv_w : q_w + 2 * kv_w] = wv[part, spot]
        outs[r][:, q_w + 2 * kv_w :] = small[part, :]


def pack(experts, place, wq, wk, wv, wr, na, nm):
    shard = wq.shape[0]
    wide_w = (wq.shape[1] + 2 * wk.shape[1]) // WS + 128
    return one_step(
        functools.partial(pack_body, experts),
        "pack",
        [place],
        [wq, wk, wv, wr, na[None], nm[None]],
        [sds((shard // 2, wide_w), BF)] * (WS + 1),
        [pltpu.VMEM((shard, 128), BF)],
        0,
    )


def attend_rows(qkv_ref, bias_ref, o_ref, lse_ref, start, q_w, kv_w):
    rows = o_ref.shape[0]
    group = q_w // kv_w
    here = slice(start, start + rows)
    for h in range(q_w // HEAD):
        at = h // group * HEAD
        q = qkv_ref[here, h * HEAD : (h + 1) * HEAD]
        k = qkv_ref[:, q_w + at : q_w + at + HEAD]
        v = qkv_ref[:, q_w + kv_w + at : q_w + kv_w + at + HEAD]
        s = dot_t(q, k) * HEAD ** (-0.5) + bias_ref[here, :]
        peak = jnp.max(s, axis=1, keepdims=True)
        p = jnp.exp(s - peak)
        total = jnp.sum(p, axis=1, keepdims=True)
        lse_ref[:, h : h + 1] = peak + jnp.log(total)
        o_ref[:, h * HEAD : (h + 1) * HEAD] = dot((p / total).astype(BF), v).astype(BF)


def attend_body(experts, place_ref, *refs):
    xs, own, twin = refs[0:4], refs[4:8], refs[8:12]
    cos_ref, sin_ref, bias_ref, wo_ref = refs[12:16]
    h1_ref, qkv_ref, o_ref, lse_ref, w_ref, small_ref, rows_ref = refs[16:23]
    parts = refs[23:26]
    me, core = place_ref[0], place_ref[1]
    rows = xs[0].shape[0]
    strip = own[0].shape[0]
    q_w = o_ref.shape[1]
    qkv_w = qkv_ref.shape[1]
    kv_w = (qkv_w - q_w) // 2
    for r in range(WS):
        base = lax.rem(me + r, WS) * (2 * strip)
        for source, side in ((own[r], core), (twin[r], 1 - core)):
            spot = pl.ds(pl.multiple_of(base + side * strip, 64), strip)
            w_ref[spot, :] = source[:, :qkv_w]
            small_ref[spot, :] = source[:, qkv_w:]
    turned = small_ref[...].astype(F32).T
    rows_ref[...] = jnp.concatenate(
        [turned[experts : experts + 2], jnp.zeros((6, turned.shape[1]), F32)], axis=0
    )
    gain = turned[experts : experts + 1]
    for r in range(WS):
        x = xs[r][...].astype(F32)
        h1_ref[r * rows : (r + 1) * rows, :] = (x * rms(x) * gain).astype(BF)
    qkv = dot(h1_ref[...], w_ref[...])
    qk = qkv[:, : q_w + kv_w]
    times = (q_w + kv_w) // 128
    qk = qk * wide(cos_ref, times) + other_half(qk) * wide(sin_ref, times)
    qkv_ref[:, : q_w + kv_w] = qk.astype(BF)
    qkv_ref[:, q_w + kv_w :] = qkv[:, q_w + kv_w :].astype(BF)
    attend_rows(qkv_ref, bias_ref, o_ref, lse_ref, rows, q_w, kv_w)
    for r in range(3):
        part = dot(o_ref[r * rows : (r + 1) * rows, :], wo_ref[...])
        parts[r][...] = part.astype(BF)


def attend(experts, place, xs, own, twin, cos, sin, bias, wo):
    rows, width = xs[0].shape
    tree = rows * WS
    q_w, qkv_w = wo.shape[0], own[0].shape[1] - 128
    outs = [
        sds((tree, width), BF),
        sds((tree, qkv_w), BF),
        sds((tree - rows, q_w), BF),
        sds((tree - rows, 128), F32),
        sds((width, qkv_w), BF),
        sds((width, 128), BF),
        sds((8, width), F32),
    ] + [sds((rows, width), BF)] * 3
    flops = 2 * tree * width * (qkv_w + q_w) + 4 * tree * tree * q_w
    return one_step(
        functools.partial(attend_body, experts),
        "attend",
        [place],
        [*xs, *own, *twin, cos, sin, bias, wo],
        outs,
        [],
        flops,
    )


def attend_own_body(qkv_ref, bias_ref, wo_ref, o_ref, lse_ref, part_ref):
    q_w = o_ref.shape[1]
    kv_w = (qkv_ref.shape[1] - q_w) // 2
    attend_rows(qkv_ref, bias_ref, o_ref, lse_ref, 0, q_w, kv_w)
    part_ref[...] = dot(o_ref[...], wo_ref[...])


def attend_own(rows, qkv, bias, wo):
    q_w, width = wo.shape
    outs = [sds((rows, q_w), BF), sds((rows, 128), F32), sds((rows, width), F32)]
    flops = 2 * rows * width * q_w + 4 * rows * qkv.shape[0] * q_w
    return one_step(attend_own_body, "attend_own", [], [qkv, bias, wo], outs, [], flops)


def enter_body(x_ref, p0, p1, p2, p3, rows_ref, slot_ref, x2_ref, h2_ref, send_ref):
    @pl.when(pl.program_id(0) == 0)
    def _():
        x2 = x_ref[...].astype(F32) + p0[...]
        for p in (p1, p2, p3):
            x2 = x2 + p[...].astype(F32)
        x2_ref[...] = x2
        h2_ref[...] = (x2 * rms(x2) * rows_ref[1:2, :]).astype(BF)

    send_ref[...] = tdot(slot_ref[...], h2_ref[...]).astype(BF)


def enter(x, parts, rows, to_slot, tile=512):
    n, width = x.shape
    slots = to_slot.shape[1]
    arrays = [x, *parts, rows]
    return pl.pallas_call(
        enter_body,
        grid=(slots // tile,),
        in_specs=[whole(a.shape) for a in arrays] + [pl.BlockSpec((n, tile), lambda i: (0, i))],
        out_specs=[
            whole((n, width)),
            whole((n, width)),
            pl.BlockSpec((tile, width), lambda i: (i, 0)),
        ],
        out_shape=[sds((n, width), F32), sds((n, width), BF), sds((slots, width), BF)],
        compiler_params=pltpu.CompilerParams(vmem_limit_bytes=VM),
        cost_estimate=pl.CostEstimate(
            flops=2 * n * width * slots, bytes_accessed=3 * slots * width, transcendentals=0
        ),
        name="enter",
    )(*arrays, to_slot)


def gate_body(h2_ref, router_ref, slot_ref, chosen_ref, spread_ref, gates_ref, gs_ref):
    logits = dot(h2_ref[...], router_ref[...])
    mask = chosen_ref[...].astype(F32) > 0.5
    logits = jnp.where(mask, logits, MASKED)
    lifted = jnp.where(mask, jnp.exp(logits - jnp.max(logits, axis=1, keepdims=True)), 0.0)
    gates = lifted / jnp.maximum(jnp.sum(lifted, axis=1, keepdims=True), 1e-30)
    gates_ref[...] = gates
    hi, lo = split(gates)
    on_slots = dot(hi, spread_ref[...]) + dot(lo, spread_ref[...])
    hi, lo = split(on_slots * slot_ref[...].astype(F32))
    rows = gates.shape[0]
    gs_ref[:rows, :] = hi
    gs_ref[rows:, :] = lo


def gate_terms(h2, router, to_slot, chosen, spread):
    n, slots = to_slot.shape
    outs = [sds((n, 128), F32), sds((2 * n, slots), BF)]
    arrays = [h2, router, to_slot, chosen, spread]
    return one_step(gate_body, "gate_terms", [], arrays, outs, [], 8 * n * 128 * slots)


def leave_body(experts, back_ref, slot_ref, gates_ref, router_ref, x2_ref, rows_ref, cot_ref, *outs):
    dx2_ref, da_ref, dh2_ref, dl_ref, sum_ref = outs
    width = x2_ref.shape[1]
    step = pl.program_id(0)
    more = dot(slot_ref[...], back_ref[...])

    @pl.when(step == 0)
    def _():
        sum_ref[...] = more

    @pl.when(step > 0)
    def _():
        sum_ref[...] += more

    @pl.when(step == pl.num_programs(0) - 1)
    def _():
        tail = sum_ref[:, width:]
        dgate = tail + pltpu.roll(tail, 128 - experts, 1)
        gates = gates_ref[...]
        dl = gates * (dgate - jnp.sum(gates * dgate, axis=1, keepdims=True))
        dl_ref[...] = dl
        hi, lo = split(dl)
        dh2 = sum_ref[:, :width] + dot_t(hi, router_ref[...]) + dot_t(lo, router_ref[...])
        dh2_ref[...] = dh2
        x2 = x2_ref[...]
        scale, gain = rms(x2), rows_ref[1:2, :]
        inner = jnp.mean(gain * dh2 * x2, axis=1, keepdims=True)
        dx2 = cot_ref[...].astype(F32) + scale * gain * dh2 - x2 * scale * scale * scale * inner
        dx2_ref[...] = dx2
        da_ref[...] = dx2.astype(BF)


def leave(experts, back, to_slot, gates, router, x2, rows, cot, tile=512):
    n, width = x2.shape
    slots = back.shape[0]
    outs = [sds((n, width), F32), sds((n, width), BF), sds((n, width), F32), sds((n, 128), F32)]
    rest = [gates, router, x2, rows, cot]
    return pl.pallas_call(
        functools.partial(leave_body, experts),
        grid=(slots // tile,),
        in_specs=[
            pl.BlockSpec((tile, width + 128), lambda i: (i, 0)),
            pl.BlockSpec((n, tile), lambda i: (0, i)),
        ]
        + [whole(a.shape) for a in rest],
        out_specs=[whole(o.shape) for o in outs],
        out_shape=outs,
        scratch_shapes=[pltpu.VMEM((n, width + 128), F32)],
        compiler_params=pltpu.CompilerParams(vmem_limit_bytes=VM),
        cost_estimate=pl.CostEstimate(
            flops=2 * n * width * slots, bytes_accessed=3 * slots * width, transcendentals=0
        ),
        name="leave",
    )(back, to_slot, *rest)


def small_body(experts, h2_ref, dl_ref, dh2_ref, x2_ref, out_ref):
    hi, lo = split(dl_ref[...])
    h2, x2 = h2_ref[...], x2_ref[...]
    out_ref[...] = tdot(h2, hi) + tdot(h2, lo) + column_sum(dh2_ref[...] * x2 * rms(x2), experts)


def small_slopes(experts, h2, dl, dh2, x2):
    n, width = x2.shape
    return one_step(
        functools.partial(small_body, experts),
        "small_slopes",
        [],
        [h2, dl, dh2, x2],
        [sds((width, 128), F32)],
        [],
        8 * n * width * 128,
    )[0]


def attend_back_body(experts, place_ref, *refs):
    das, xs = refs[0:4], refs[4:8]
    wo_ref, qkv_ref, o_own, o_far, lse_own, lse_far, h1_ref, w_ref = refs[8:16]
    cos_ref, sin_ref, bias_ref, small_ref = refs[16:20]
    keep_ref, give_ref = refs[20:22]
    parts = refs[22:26]
    da, do, dqk, dqkv, o_ref, lse_ref = refs[26:32]
    core = place_ref[1]
    rows = xs[0].shape[0]
    q_w, qkv_w = o_ref.shape[1], qkv_ref.shape[1]
    kv_w = (qkv_w - q_w) // 2
    group = q_w // kv_w
    scale = HEAD ** (-0.5)
    for r in range(WS):
        da[r * rows : (r + 1) * rows, :] = das[r][...]
    o_ref[:rows, :] = o_own[...]
    o_ref[rows:, :] = o_far[...]
    lse_ref[:rows, :] = lse_own[...]
    lse_ref[rows:, :] = lse_far[...]
    do[...] = dot_t(da[...], wo_ref[...]).astype(BF)
    for n in range(kv_w // HEAD):
        at = n * HEAD
        k = qkv_ref[:, q_w + at : q_w + at + HEAD]
        v = qkv_ref[:, q_w + kv_w + at : q_w + kv_w + at + HEAD]
        dk, dv = None, None
        for h in range(n * group, (n + 1) * group):
            q = qkv_ref[:, h * HEAD : (h + 1) * HEAD]
            doh = do[:, h * HEAD : (h + 1) * HEAD]
            p = jnp.exp(dot_t(q, k) * scale + bias_ref[...] - lse_ref[:, h : h + 1])
            dp = dot_t(doh, v)
            delta = jnp.sum(p * dp, axis=1, keepdims=True)
            ds = (p * (dp - delta)).astype(BF)
            dqk[:, h * HEAD : (h + 1) * HEAD] = dot(ds, k) * scale
            more_k, more_v = tdot(ds, q), tdot(p.astype(BF), doh)
            dk = more_k if dk is None else dk + more_k
            dv = more_v if dv is None else dv + more_v
        dqk[:, q_w + at : q_w + at + HEAD] = dk * scale
        dqkv[:, q_w + kv_w + at : q_w + kv_w + at + HEAD] = dv.astype(BF)
    dqkv[:, qkv_w:] = jnp.zeros((da.shape[0], 128), BF)
    d = dqk[...]
    times = (q_w + kv_w) // 128
    d = d * wide(cos_ref, times) - other_half(d) * wide(sin_ref, times)
    dqkv[:, : q_w + kv_w] = d.astype(BF)
    small = small_ref[...]
    for r in range(WS):
        dh1 = dot_t(dqkv[r * rows : (r + 1) * rows, :qkv_w], w_ref[...])
        parts[r][...] = dh1.astype(parts[r].dtype)
        x = xs[r][...].astype(F32)
        small = small + column_sum(dh1 * x * rms(x), experts + 1)
    half = keep_ref.shape[3]
    chips, step = keep_ref.shape[0], keep_ref.shape[2]
    count = chips * step

    def put(i, first, second):
        kept = jnp.where(core == 0, first, second)
        given = jnp.where(core == 0, second, first)
        keep_ref[:, i] = kept.reshape(chips, step, half)
        give_ref[:, i] = given.reshape(chips, step, half).astype(BF)

    for i in range(WS):
        both = tdot(h1_ref[:, i * count : (i + 1) * count], dqkv[...])
        mine = small[i * count : (i + 1) * count]
        second = jnp.concatenate([both[:, half : 2 * half - 128], both[:, 2 * half - 128 :] + mine], axis=1)
        put(i, both[:, :half], second)
    slope = tdot(o_ref[...], da[...])
    for i in range(2):
        put(WS + i, slope[:, i * half : (i + 1) * half], slope[:, (2 + i) * half : (3 + i) * half])


def attend_back(experts, place, das, xs, wo, qkv, os, lses, h1, w, cos, sin, bias, small):
    rows, width = xs[0].shape
    tree = rows * WS
    q_w, qkv_w = wo.shape[0], qkv.shape[1]
    half = (qkv_w + 128) // 2
    load = (CHIPS, WS + 2, width // WS // CHIPS, half)
    outs = [sds(load, F32), sds(load, BF), sds((rows, width), F32)] + [sds((rows, width), BF)] * 3
    scratch = [
        pltpu.VMEM((tree, width), BF),
        pltpu.VMEM((tree, q_w), BF),
        pltpu.VMEM((tree, (q_w + qkv_w) // 2), F32),
        pltpu.VMEM((tree, qkv_w + 128), BF),
        pltpu.VMEM((tree, q_w), BF),
        pltpu.VMEM((tree, 128), F32),
    ]
    flops = 4 * tree * width * (qkv_w + q_w) + 10 * tree * tree * q_w
    return one_step(
        functools.partial(attend_back_body, experts),
        "attend_back",
        [place],
        [*das, *xs, wo, qkv, *os, *lses, h1, w, cos, sin, bias, small],
        outs,
        scratch,
        flops,
    )


def shards(
    tokens,
    cotangent,
    seg_lengths,
    parents,
    routes,
    norm_attn,
    w_query,
    w_key,
    w_value,
    w_out,
    norm_moe,
    w_router,
    w_gate,
    w_up,
    w_down,
):
    me = lax.axis_index("ws")
    expert = lax.axis_index("exp")
    core = expert % 2
    place = jnp.stack([me, core]).astype(jnp.int32)
    rows, width = tokens.shape
    shard = width // WS
    strip = shard // 2
    experts = 2 * CHIPS
    q_w, kv_w = HEADS // WS * HEAD, KV_HEADS // WS * HEAD
    slots = experts * CAP

    def gathered(v):
        return [v] + [from_peer(v, k) for k in (1, 2, 3)]

    xs = gathered(tokens)

    pieces = pack(experts, place, w_query, w_key, w_value, w_router, norm_attn, norm_moe)
    pieces, routes = lax.optimization_barrier((pieces, routes))
    own = [pieces[0]] + [from_peer(pieces[k], k) for k in (1, 2, 3)]
    twin = [pieces[WS]] + [other_core(own[k]) for k in (1, 2, 3)]

    labels = jnp.arange(experts, dtype=jnp.int32)
    lane = jnp.arange(128, dtype=jnp.int32)
    chosen = jnp.any(routes[:, :, None] == lane[None, None, :], axis=1)
    row_id = jnp.arange(rows, dtype=jnp.int32)
    before = (row_id[None, :] < row_id[:, None]).astype(BF)
    rank = dot(before, chosen.astype(BF))
    col = jnp.arange(slots, dtype=jnp.int32)
    spread = (col[None, :] // CAP == lane[:, None]).astype(BF)
    spot = dot(jnp.where(chosen, rank + 1.0, 0.0).astype(BF), spread)
    to_slot = (spot == (col % CAP + 1).astype(F32)[None, :]).astype(BF)
    chosen = chosen.astype(BF)
    extra = jnp.concatenate([cotangent, chosen], axis=1)
    dy_send = tdot(to_slot, extra).astype(BF).reshape(experts, CAP, width + 128)
    dy_send, xs[1], xs[3] = lax.optimization_barrier((dy_send, xs[1], xs[3]))
    dy_slots = lax.all_to_all(dy_send, "exp", 0, 0, tiled=True).reshape(slots, width + 128)

    order = (
        ((me + jnp.arange(WS, dtype=jnp.int32)) % WS)[:, None] * rows + row_id[None, :]
    ).reshape(-1)
    visible, position = tree_layout(seg_lengths[0], parents[0], order)
    bias = jnp.where(visible, 0.0, MASKED).astype(F32)
    inverse = THETA ** (-(lane % (HEAD // 2)).astype(F32) * 2.0 / HEAD)
    angles = position.astype(F32)[:, None] * inverse[None, :]
    cosines = jnp.cos(angles)
    sines = jnp.where((lane % HEAD < HEAD // 2)[None, :], -1.0, 1.0) * jnp.sin(angles)
    h1, qkv, o_far, lse_far, w_qkv, small_full, gains, *parts = attend(
        experts, place, xs, own, twin, cosines, sines, bias, w_out
    )
    o_own, lse_own, part_own = attend_own(rows, qkv, bias, w_out)
    sums = [part_own] + [to_peer(parts[k - 1], k) for k in (1, 2, 3)]
    x2, h2, x_send = enter(tokens, sums, gains, to_slot)
    x_send, wg_own, wu_own, wd_own = lax.optimization_barrier(
        (x_send, w_gate[0], w_up[0], w_down[0])
    )
    x_slots = lax.all_to_all(
        x_send.reshape(experts, CAP, width), "exp", 0, 0, tiled=True
    ).reshape(slots, width)

    sel = jnp.concatenate(
        [
            (lane == expert).astype(F32)[None],
            (lane == expert + experts).astype(F32)[None],
            jnp.zeros((6, 128), F32),
        ],
        axis=0,
    )
    wd = gathered(wd_own)
    dx_send, hidden, d_gu, slot_gates = expert_pass(
        x_slots, dy_slots, sel, small_full, gathered(wg_own), gathered(wu_own), wd, 256
    )
    gates, gate_slots = gate_terms(h2, small_full, to_slot, chosen, spread)
    hidden, gates, gate_slots = lax.optimization_barrier((hidden, gates, gate_slots))
    dx_back = lax.all_to_all(
        dx_send.reshape(experts, CAP, width + 128), "exp", 0, 0, tiled=True
    ).reshape(slots, width + 128)

    y, own_g, own_u, own_d, gu1, dn1, gu2, dn2, gu3, dn3 = expert_slopes(
        x_slots, d_gu, hidden, dy_slots, slot_gates, wd
    )
    gu1, dn1 = to_peer(gu1, 1), to_peer(dn1, 1)
    gu3, dn3 = to_peer(gu3, 3), to_peer(dn3, 3)
    gu2 = to_peer(gu2, 2)
    dx_back, y, gu1, dn1, gu2, gu3, dn3 = lax.optimization_barrier(
        (dx_back, y, gu1, dn1, gu2, gu3, dn3)
    )
    y_back = lax.all_to_all(y.reshape(experts, CAP, width), "exp", 0, 0, tiled=True).reshape(
        slots, width
    )

    dx2, d_a, dh2, dl = leave(
        experts, dx_back, to_slot, gates, small_full, x2, gains, cotangent
    )
    das = gathered(d_a)
    small_terms = small_slopes(experts, h2, dl, dh2, x2)
    keep, give, *slopes = attend_back(
        experts,
        place,
        das,
        xs,
        w_out,
        qkv,
        (o_own, o_far),
        (lse_own, lse_far),
        h1,
        w_qkv,
        cosines,
        sines,
        bias,
        small_terms,
    )
    sent = (keep + other_core(give).astype(F32)).astype(BF)
    sent, y_back, slopes, dn2, gu1 = lax.optimization_barrier((sent, y_back, slopes, dn2, gu1))
    dn2 = to_peer(dn2, 2)
    grad_gu = jnp.stack([own_g, own_u]) + gu1.astype(F32) + gu2.astype(F32) + gu3.astype(F32)
    grad_wg, grad_wu = grad_gu[0][None], grad_gu[1][None]
    grad_wd = (own_d + dn1.astype(F32) + dn2.astype(F32) + dn3.astype(F32))[None]
    dh1 = slopes[0]
    for k in (1, 2, 3):
        dh1 = dh1 + to_peer(slopes[k], k).astype(F32)
    resid = tokens.astype(F32)
    scale = lax.rsqrt(jnp.mean(resid * resid, axis=-1, keepdims=True) + EPS)
    inner = jnp.mean(gains[0:1] * dh1 * resid, axis=-1, keepdims=True)
    grad_tokens = dx2 + scale * gains[0:1] * dh1 - resid * scale * scale * scale * inner

    half = (q_w + 2 * kv_w + 128) // 2
    flag = jnp.broadcast_to(jnp.stack([core, 1 - core]).astype(F32)[:, None], (2, 128))
    flag = jnp.concatenate([flag, jnp.zeros((6, 128), F32)], axis=0)
    step = shard // CHIPS
    both = dot(gate_slots, y_back)
    layer_out = (x2 + both[:rows] + both[rows:]).astype(BF)
    got = same_core(sent)
    got, layer_out, grad_tokens, grad_wg, grad_wu, grad_wd = lax.optimization_barrier(
        (got, layer_out, grad_tokens, grad_wg, grad_wu, grad_wd)
    )
    total = jnp.sum(got.astype(F32), axis=0).astype(BF)
    final = jnp.stack(
        [lax.dynamic_index_in_dim(total, me, 0, False)]
        + [
            from_peer(lax.dynamic_index_in_dim(total, (me - k) % WS, 0, False), k)
            for k in (1, 2, 3)
        ]
        + [total[WS], total[WS + 1]]
    )
    spread_out = same_core(jnp.broadcast_to(final, (CHIPS,) + final.shape))
    twin_out = other_core(spread_out)
    sum_query, sum_key, sum_value, sum_router, sum_gains, sum_out = finish(
        experts, place, spread_out, twin_out, flag
    )

    return (
        layer_out,
        grad_tokens,
        sum_gains[1],
        sum_query,
        sum_key,
        sum_value,
        sum_out,
        sum_gains[0],
        sum_router.T,
        grad_wg,
        grad_wu,
        grad_wd,
    )


def solution(mesh):
    rows = P(("exp", "ws"), None)
    placed = (
        rows,
        rows,
        P("exp", None),
        P("exp", None),
        rows,
        P("ws"),
        P("ws", None),
        P("ws", None),
        P("ws", None),
        P("ws", None),
        P("ws"),
        P("ws", None),
        P("exp", None, "ws"),
        P("exp", None, "ws"),
        P("exp", "ws", None),
    )
    return jax.shard_map(
        shards,
        mesh=mesh,
        in_specs=placed,
        out_specs=(
            rows,
            rows,
            P("ws"),
            P("ws", None),
            P("ws", None),
            P("ws", None),
            P("ws", None),
            P("ws"),
            P("ws", None),
            P("exp", None, "ws"),
            P("exp", None, "ws"),
            P("exp", "ws", None),
        ),
        check_vma=False,
    )
```

```python
import functools

import jax
import jax.numpy as jnp
from jax import lax
from jax.experimental import pallas as pl
from jax.experimental.pallas import tpu as pltpu
from jax.sharding import PartitionSpec as P

HEADS = 24
KV_HEADS = 8
HEAD = 64
EPS = 1e-06
THETA = 10000.0
MASKED = -1e30
BF = jnp.bfloat16
F32 = jnp.float32
WS = 4
CHIPS = 16
CAP = 48
VM = 60 * 1024 * 1024


def dot(a, b):
    return jnp.dot(a, b, preferred_element_type=F32)


def dot_t(a, b):
    return lax.dot_general(a, b, (((1,), (1,)), ((), ())), preferred_element_type=F32)


def tdot(a, b):
    return lax.dot_general(a, b, (((0,), (0,)), ((), ())), preferred_element_type=F32)


def split(v):
    hi = v.astype(BF)
    return hi, (v - hi.astype(F32)).astype(BF)


def from_peer(v, k):
    return lax.ppermute(v, "ws", [(s, (s - k) % WS) for s in range(WS)])


def to_peer(v, k):
    return lax.ppermute(v, "ws", [(s, (s + k) % WS) for s in range(WS)])


def other_core(v):
    return lax.ppermute(v, "exp", [(s, s ^ 1) for s in range(2 * CHIPS)])


def same_core(v):
    groups = [[2 * chip + core for chip in range(CHIPS)] for core in range(2)]
    return lax.all_to_all(v, "exp", 0, 0, tiled=True, axis_index_groups=groups)


def tree_layout(lengths, parents, token_index):
    seg = lengths.shape[0]
    labels = jnp.arange(seg, dtype=jnp.int32)
    segment_end = jnp.cumsum(lengths, dtype=jnp.int32)
    starts = segment_end - lengths
    segment = jnp.sum((token_index[:, None] >= segment_end[None, :]).astype(jnp.int32), axis=1)
    reach = ((parents[:, None] == labels[None, :]) | (labels[:, None] == labels[None, :])).astype(
        BF
    )
    for _ in range(4):
        reach = (dot(reach, reach) > 0.5).astype(BF)
    above = jnp.sum(reach.astype(jnp.int32) * lengths[None, :], axis=1) - lengths
    members = segment[:, None] == labels[None, :]
    position = jnp.sum(jnp.where(members, (above - starts)[None, :], 0), axis=1) + token_index
    members = members.astype(BF)
    reaches = dot(members, reach).astype(BF)
    visible = (dot_t(reaches, members) > 0.5) & (token_index[None, :] <= token_index[:, None])
    return visible, position


def expert_body(width, ff, x_ref, dy_ref, sel_ref, wr_ref, *rest):
    wg, wu, wd = rest[0:4], rest[4:8], rest[8:12]
    dx_ref, h_ref, dgu_ref, gate_ref = rest[12:16]
    wgu, wdn = rest[16:]
    part = wg[0].shape[1]

    @pl.when(pl.program_id(0) == 0)
    def _():
        for r in range(WS):
            wgu[:, r * part : (r + 1) * part] = wg[r][...]
            wgu[:, ff + r * part : ff + (r + 1) * part] = wu[r][...]
            wdn[r * part : (r + 1) * part, :] = wd[r][...]
        wgu[:, 2 * ff :] = wr_ref[...]

    pre = dot(x_ref[...], wgu[...])
    g, u, logits = pre[:, :ff], pre[:, ff : 2 * ff], pre[:, 2 * ff :]
    mask = dy_ref[:, width:].astype(F32) > 0.5
    logits = jnp.where(mask, logits, MASKED)
    lifted = jnp.where(mask, jnp.exp(logits - jnp.max(logits, axis=1, keepdims=True)), 0.0)
    total = jnp.maximum(jnp.sum(lifted, axis=1, keepdims=True), 1e-30)
    gate = jnp.sum(lifted * sel_ref[0:1, :], axis=1, keepdims=True) / total
    gate_ref[...] = jnp.broadcast_to(gate, gate_ref.shape)
    sig = 1.0 / (1.0 + jnp.exp(-g))
    silu = g * sig
    h = (silu * u).astype(BF)
    h_ref[...] = h
    raw = dot_t(dy_ref[:, :width], wdn[...])
    dgate = jnp.sum(raw * h.astype(F32), axis=1, keepdims=True)
    dh = raw * gate
    dgu_ref[:, :ff] = (dh * u * sig * (1.0 + g * (1.0 - sig))).astype(BF)
    dgu_ref[:, ff:] = (dh * silu).astype(BF)
    dx_ref[:, :width] = dot_t(dgu_ref[...], wgu[:, : 2 * ff]).astype(BF)
    hi = dgate.astype(BF).astype(F32)
    dx_ref[:, width:] = (hi * sel_ref[0:1, :] + (dgate - hi) * sel_ref[1:2, :]).astype(BF)


def expert_pass(x, dy, sel, wr, wg, wu, wd, tile):
    slots, width = x.shape
    part = wg[0].shape[1]
    ff = WS * part
    row = lambda w: pl.BlockSpec((tile, w), lambda i: (i, 0))
    once = lambda a: pl.BlockSpec(a.shape, lambda i: (0, 0))
    return pl.pallas_call(
        functools.partial(expert_body, width, ff),
        grid=(slots // tile,),
        in_specs=[row(width), row(width + 128), once(sel), once(wr)]
        + [once(a) for a in (*wg, *wu, *wd)],
        out_specs=[row(width + 128), row(ff), row(2 * ff), row(128)],
        out_shape=[
            jax.ShapeDtypeStruct((slots, width + 128), BF),
            jax.ShapeDtypeStruct((slots, ff), BF),
            jax.ShapeDtypeStruct((slots, 2 * ff), BF),
            jax.ShapeDtypeStruct((slots, 128), F32),
        ],
        scratch_shapes=[pltpu.VMEM((width, 2 * ff + 128), BF), pltpu.VMEM((ff, width), BF)],
        compiler_params=pltpu.CompilerParams(vmem_limit_bytes=VM),
        cost_estimate=pl.CostEstimate(
            flops=10 * slots * width * ff, bytes_accessed=9 * slots * width, transcendentals=0
        ),
        name="expert_pass",
    )(x, dy, sel, wr, *wg, *wu, *wd)


def in_slope_body(x_ref, dgu_ref, own_g, own_u, *peers):
    part = own_g.shape[1]
    ff = WS * part
    gu = tdot(x_ref[...], dgu_ref[...])
    own_g[...] = gu[:, :part]
    own_u[...] = gu[:, ff : ff + part]
    for k in (1, 2, 3):
        peers[k - 1][0] = gu[:, k * part : (k + 1) * part].astype(BF)
        peers[k - 1][1] = gu[:, ff + k * part : ff + (k + 1) * part].astype(BF)


def in_slopes(x, dgu, tile=256):
    slots, width = x.shape
    part = dgu.shape[1] // (2 * WS)
    tall = pl.BlockSpec((tile, part), lambda i: (i, 0))
    pair = pl.BlockSpec((2, tile, part), lambda i: (0, i, 0))
    return pl.pallas_call(
        in_slope_body,
        grid=(width // tile,),
        in_specs=[pl.BlockSpec((slots, tile), lambda i: (0, i)), whole(dgu.shape)],
        out_specs=[tall, tall] + [pair] * 3,
        out_shape=[sds((width, part), F32)] * 2 + [sds((2, width, part), BF)] * 3,
        compiler_params=pltpu.CompilerParams(vmem_limit_bytes=VM),
        cost_estimate=pl.CostEstimate(
            flops=2 * slots * width * dgu.shape[1],
            bytes_accessed=4 * slots * width,
            transcendentals=0,
        ),
        name="in_slopes",
    )(x, dgu)


def out_slope_body(h_ref, dy_ref, gate_ref, *refs):
    wd = refs[0:4]
    y_ref, own_d = refs[4:6]
    part = own_d.shape[0]
    d_y = (gate_ref[:, 0:1] * dy_ref[...].astype(F32)).astype(BF)
    dn = tdot(h_ref[...], d_y)
    own_d[...] = dn[:part]
    for k in (1, 2, 3):
        refs[5 + k][...] = dn[k * part : (k + 1) * part].astype(BF)
    y_ref[...] = dot(h_ref[...], jnp.concatenate([w[...] for w in wd], axis=0)).astype(BF)


def out_slopes(h, dy, gate, wd, tile=256):
    slots, ff = h.shape
    width = wd[0].shape[1]
    part = ff // WS
    col = pl.BlockSpec((slots, tile), lambda i: (0, i))
    flat = pl.BlockSpec((part, tile), lambda i: (0, i))
    return pl.pallas_call(
        out_slope_body,
        grid=(width // tile,),
        in_specs=[whole(h.shape), col, whole(gate.shape)] + [flat] * WS,
        out_specs=[col, flat] + [flat] * 3,
        out_shape=[sds((slots, width), BF), sds((part, width), F32)]
        + [sds((part, width), BF)] * 3,
        compiler_params=pltpu.CompilerParams(vmem_limit_bytes=VM),
        cost_estimate=pl.CostEstimate(
            flops=4 * slots * width * ff, bytes_accessed=4 * slots * width, transcendentals=0
        ),
        name="out_slopes",
    )(h, dy, gate, *wd)


def finish_body(experts, place_ref, a_ref, b_ref, ao_ref, bo_ref, *refs):
    q_ref, k_ref, v_ref, r_ref, g_ref, o_ref, s_ref = refs
    turn = pl.program_id(0)
    second = place_ref[1] == 1
    rows = q_ref.shape[0]
    half = a_ref.shape[3]
    kv = k_ref.shape[1]
    mine = a_ref[:, 0].astype(F32).reshape(rows, half)
    twin = b_ref[:, 0].astype(F32).reshape(rows, half)
    q_ref[...] = jnp.where(second, twin, mine)
    rest = jnp.where(second, mine, twin)
    k_ref[...] = rest[:, :kv]
    v_ref[...] = rest[:, kv : 2 * kv]

    @pl.when(turn == 0)
    def _():
        s_ref[...] = rest[:, 2 * kv :]

    @pl.when(turn > 0)
    def _():
        s_ref[...] += rest[:, 2 * kv :]

    @pl.when(turn == WS - 1)
    def _():
        turned = s_ref[...].T
        r_ref[...] = turned[:experts]
        g_ref[...] = turned[experts : experts + 8]

    mine = ao_ref[:, 0].astype(F32).reshape(rows, half)
    twin = bo_ref[:, 0].astype(F32).reshape(rows, half)
    o_ref[...] = jnp.where(second == (turn < 2), twin, mine)


def finish(experts, place, mine, twin):
    chips, sets, step, half = mine.shape
    rows = chips * step
    first = pl.BlockSpec((chips, 1, step, half), lambda i, p: (0, i, 0, 0))
    later = pl.BlockSpec((chips, 1, step, half), lambda i, p: (0, WS + i % 2, 0, 0))
    turned = lambda i, p: (0, lax.rem(p[0] + i, WS))
    kv = (half - 128) // 2
    S = jax.ShapeDtypeStruct
    return pl.pallas_call(
        functools.partial(finish_body, experts),
        grid_spec=pltpu.PrefetchScalarGridSpec(
            num_scalar_prefetch=1,
            grid=(WS,),
            in_specs=[first, first, later, later],
            out_specs=[
                pl.BlockSpec((rows, half), turned),
                pl.BlockSpec((rows, kv), turned),
                pl.BlockSpec((rows, kv), turned),
                whole((experts, rows)),
                whole((8, rows)),
                pl.BlockSpec((rows, half), lambda i, p: (0, i)),
            ],
            scratch_shapes=[pltpu.VMEM((rows, 128), F32)],
        ),
        out_shape=[
            S((rows, WS * half), F32),
            S((rows, WS * kv), F32),
            S((rows, WS * kv), F32),
            S((experts, rows), F32),
            S((8, rows), F32),
            S((rows, WS * half), F32),
        ],
        compiler_params=pltpu.CompilerParams(vmem_limit_bytes=VM),
        cost_estimate=pl.CostEstimate(flops=0, bytes_accessed=16 * rows * WS * half, transcendentals=0),
        name="finish",
    )(place, mine, twin, mine, twin)


def whole(shape):
    return pl.BlockSpec(shape, lambda *_: (0,) * len(shape))


def sds(shape, kind):
    return jax.ShapeDtypeStruct(shape, kind)


def one_step(body, name, scalars, arrays, outs, scratch, flops):
    moved = sum(a.size * a.dtype.itemsize for a in arrays)
    return pl.pallas_call(
        body,
        in_specs=[pl.BlockSpec(memory_space=pltpu.SMEM)] * len(scalars)
        + [pl.BlockSpec(memory_space=pltpu.VMEM)] * len(arrays),
        out_specs=[pl.BlockSpec(memory_space=pltpu.VMEM)] * len(outs),
        out_shape=outs,
        scratch_shapes=scratch,
        compiler_params=pltpu.CompilerParams(vmem_limit_bytes=VM),
        cost_estimate=pl.CostEstimate(flops=flops, bytes_accessed=moved, transcendentals=0),
        name=name,
    )(*scalars, *arrays)


def other_half(v):
    lanes = v.shape[1]
    low = lax.broadcasted_iota(jnp.int32, v.shape, 1) % HEAD < HEAD // 2
    ahead = pltpu.roll(v, lanes - HEAD // 2, 1)
    behind = pltpu.roll(v, HEAD // 2, 1)
    return jnp.where(low, ahead, behind)


def wide(ref, times):
    return jnp.concatenate([ref[...]] * times, axis=1)


def rms(x):
    return lax.rsqrt(jnp.mean(x * x, axis=1, keepdims=True) + EPS)


def column_sum(m, lane):
    hi, lo = split(m)
    pick = (lax.broadcasted_iota(jnp.int32, (m.shape[0], 128), 1) == lane).astype(F32).astype(BF)
    return tdot(hi, pick) + tdot(lo, pick)


def pack_body(experts, place_ref, wq, wk, wv, wr, na, nm, *outs):
    small = outs[WS + 1]
    me, core = place_ref[0], place_ref[1]
    strip = wq.shape[0] // 2
    q_w, kv_w = wq.shape[1] // WS, wk.shape[1] // WS
    shard = wq.shape[0]
    gains = jnp.concatenate(
        [na[...].astype(F32), nm[...].astype(F32), jnp.zeros((6, shard), F32)], axis=0
    ).T
    small[...] = jnp.concatenate(
        [wr[...].astype(F32), gains, jnp.zeros((shard, 128 - experts - 8), F32)], axis=1
    ).astype(BF)
    for r in range(WS + 1):
        side = core if r < WS else 1 - core
        d = lax.rem(me + WS - r % WS, WS)
        part = pl.ds(pl.multiple_of(side * strip, 64), strip)
        outs[r][:, :q_w] = wq[part, pl.ds(pl.multiple_of(d * q_w, 128), q_w)]
        spot = pl.ds(pl.multiple_of(d * kv_w, 128), kv_w)
        outs[r][:, q_w : q_w + kv_w] = wk[part, spot]
        outs[r][:, q_w + kv_w : q_w + 2 * kv_w] = wv[part, spot]
        outs[r][:, q_w + 2 * kv_w :] = small[part, :]


def pack(experts, place, wq, wk, wv, wr, na, nm):
    shard = wq.shape[0]
    wide_w = (wq.shape[1] + 2 * wk.shape[1]) // WS + 128
    return one_step(
        functools.partial(pack_body, experts),
        "pack",
        [place],
        [wq, wk, wv, wr, na[None], nm[None]],
        [sds((shard // 2, wide_w), BF)] * (WS + 1),
        [pltpu.VMEM((shard, 128), BF)],
        0,
    )


def attend_rows(qkv_ref, bias_ref, o_ref, lse_ref, start, q_w, kv_w):
    rows = o_ref.shape[0]
    group = q_w // kv_w
    here = slice(start, start + rows)
    for h in range(q_w // HEAD):
        at = h // group * HEAD
        q = qkv_ref[here, h * HEAD : (h + 1) * HEAD]
        k = qkv_ref[:, q_w + at : q_w + at + HEAD]
        v = qkv_ref[:, q_w + kv_w + at : q_w + kv_w + at + HEAD]
        s = dot_t(q, k) * HEAD ** (-0.5) + bias_ref[here, :]
        peak = jnp.max(s, axis=1, keepdims=True)
        p = jnp.exp(s - peak)
        total = jnp.sum(p, axis=1, keepdims=True)
        lse_ref[:, h : h + 1] = peak + jnp.log(total)
        o_ref[:, h * HEAD : (h + 1) * HEAD] = dot((p / total).astype(BF), v).astype(BF)


def attend_body(experts, place_ref, *refs):
    xs, own, twin = refs[0:4], refs[4:8], refs[8:12]
    cos_ref, sin_ref, bias_ref, wo_ref = refs[12:16]
    h1_ref, qkv_ref, o_ref, lse_ref, w_ref, small_ref, rows_ref = refs[16:23]
    parts = refs[23:26]
    me, core = place_ref[0], place_ref[1]
    rows = xs[0].shape[0]
    strip = own[0].shape[0]
    q_w = o_ref.shape[1]
    qkv_w = qkv_ref.shape[1]
    kv_w = (qkv_w - q_w) // 2
    for r in range(WS):
        base = lax.rem(me + r, WS) * (2 * strip)
        for source, side in ((own[r], core), (twin[r], 1 - core)):
            spot = pl.ds(pl.multiple_of(base + side * strip, 64), strip)
            w_ref[spot, :] = source[:, :qkv_w]
            small_ref[spot, :] = source[:, qkv_w:]
    turned = small_ref[...].astype(F32).T
    rows_ref[...] = jnp.concatenate(
        [turned[experts : experts + 2], jnp.zeros((6, turned.shape[1]), F32)], axis=0
    )
    gain = turned[experts : experts + 1]
    for r in range(WS):
        x = xs[r][...].astype(F32)
        h1_ref[r * rows : (r + 1) * rows, :] = (x * rms(x) * gain).astype(BF)
    qkv = dot(h1_ref[...], w_ref[...])
    qk = qkv[:, : q_w + kv_w]
    times = (q_w + kv_w) // 128
    qk = qk * wide(cos_ref, times) + other_half(qk) * wide(sin_ref, times)
    qkv_ref[:, : q_w + kv_w] = qk.astype(BF)
    qkv_ref[:, q_w + kv_w :] = qkv[:, q_w + kv_w :].astype(BF)
    attend_rows(qkv_ref, bias_ref, o_ref, lse_ref, rows, q_w, kv_w)
    for r in range(3):
        part = dot(o_ref[r * rows : (r + 1) * rows, :], wo_ref[...])
        parts[r][...] = part.astype(BF)


def attend(experts, place, xs, own, twin, cos, sin, bias, wo):
    rows, width = xs[0].shape
    tree = rows * WS
    q_w, qkv_w = wo.shape[0], own[0].shape[1] - 128
    outs = [
        sds((tree, width), BF),
        sds((tree, qkv_w), BF),
        sds((tree - rows, q_w), BF),
        sds((tree - rows, 128), F32),
        sds((width, qkv_w), BF),
        sds((width, 128), BF),
        sds((8, width), F32),
    ] + [sds((rows, width), BF)] * 3
    flops = 2 * tree * width * (qkv_w + q_w) + 4 * tree * tree * q_w
    return one_step(
        functools.partial(attend_body, experts),
        "attend",
        [place],
        [*xs, *own, *twin, cos, sin, bias, wo],
        outs,
        [],
        flops,
    )


def attend_own_body(qkv_ref, bias_ref, wo_ref, o_ref, lse_ref, part_ref):
    q_w = o_ref.shape[1]
    kv_w = (qkv_ref.shape[1] - q_w) // 2
    attend_rows(qkv_ref, bias_ref, o_ref, lse_ref, 0, q_w, kv_w)
    part_ref[...] = dot(o_ref[...], wo_ref[...])


def attend_own(rows, qkv, bias, wo):
    q_w, width = wo.shape
    outs = [sds((rows, q_w), BF), sds((rows, 128), F32), sds((rows, width), F32)]
    flops = 2 * rows * width * q_w + 4 * rows * qkv.shape[0] * q_w
    return one_step(attend_own_body, "attend_own", [], [qkv, bias, wo], outs, [], flops)


def enter_body(x_ref, p0, p1, p2, p3, rows_ref, slot_ref, x2_ref, h2_ref, send_ref):
    @pl.when(pl.program_id(0) == 0)
    def _():
        x2 = x_ref[...].astype(F32) + p0[...]
        for p in (p1, p2, p3):
            x2 = x2 + p[...].astype(F32)
        x2_ref[...] = x2
        h2_ref[...] = (x2 * rms(x2) * rows_ref[1:2, :]).astype(BF)

    send_ref[...] = tdot(slot_ref[...], h2_ref[...]).astype(BF)


def enter(x, parts, rows, to_slot, tile=512):
    n, width = x.shape
    slots = to_slot.shape[1]
    arrays = [x, *parts, rows]
    return pl.pallas_call(
        enter_body,
        grid=(slots // tile,),
        in_specs=[whole(a.shape) for a in arrays] + [pl.BlockSpec((n, tile), lambda i: (0, i))],
        out_specs=[
            whole((n, width)),
            whole((n, width)),
            pl.BlockSpec((tile, width), lambda i: (i, 0)),
        ],
        out_shape=[sds((n, width), F32), sds((n, width), BF), sds((slots, width), BF)],
        compiler_params=pltpu.CompilerParams(vmem_limit_bytes=VM),
        cost_estimate=pl.CostEstimate(
            flops=2 * n * width * slots, bytes_accessed=3 * slots * width, transcendentals=0
        ),
        name="enter",
    )(*arrays, to_slot)


def gate_body(h2_ref, router_ref, slot_ref, chosen_ref, spread_ref, gates_ref, gs_ref):
    logits = dot(h2_ref[...], router_ref[...])
    mask = chosen_ref[...].astype(F32) > 0.5
    logits = jnp.where(mask, logits, MASKED)
    lifted = jnp.where(mask, jnp.exp(logits - jnp.max(logits, axis=1, keepdims=True)), 0.0)
    gates = lifted / jnp.maximum(jnp.sum(lifted, axis=1, keepdims=True), 1e-30)
    gates_ref[...] = gates
    hi, lo = split(gates)
    on_slots = dot(hi, spread_ref[...]) + dot(lo, spread_ref[...])
    hi, lo = split(on_slots * slot_ref[...].astype(F32))
    rows = gates.shape[0]
    gs_ref[:rows, :] = hi
    gs_ref[rows:, :] = lo


def gate_terms(h2, router, to_slot, chosen, spread):
    n, slots = to_slot.shape
    outs = [sds((n, 128), F32), sds((2 * n, slots), BF)]
    arrays = [h2, router, to_slot, chosen, spread]
    return one_step(gate_body, "gate_terms", [], arrays, outs, [], 8 * n * 128 * slots)


def leave_body(experts, back_ref, slot_ref, gates_ref, router_ref, x2_ref, rows_ref, cot_ref, *outs):
    dx2_ref, da_ref, dh2_ref, dl_ref, sum_ref = outs
    width = x2_ref.shape[1]
    step = pl.program_id(0)
    more = dot(slot_ref[...], back_ref[...])

    @pl.when(step == 0)
    def _():
        sum_ref[...] = more

    @pl.when(step > 0)
    def _():
        sum_ref[...] += more

    @pl.when(step == pl.num_programs(0) - 1)
    def _():
        tail = sum_ref[:, width:]
        dgate = tail + pltpu.roll(tail, 128 - experts, 1)
        gates = gates_ref[...]
        dl = gates * (dgate - jnp.sum(gates * dgate, axis=1, keepdims=True))
        dl_ref[...] = dl
        hi, lo = split(dl)
        dh2 = sum_ref[:, :width] + dot_t(hi, router_ref[...]) + dot_t(lo, router_ref[...])
        dh2_ref[...] = dh2
        x2 = x2_ref[...]
        scale, gain = rms(x2), rows_ref[1:2, :]
        inner = jnp.mean(gain * dh2 * x2, axis=1, keepdims=True)
        dx2 = cot_ref[...].astype(F32) + scale * gain * dh2 - x2 * scale * scale * scale * inner
        dx2_ref[...] = dx2
        da_ref[...] = dx2.astype(BF)


def leave(experts, back, to_slot, gates, router, x2, rows, cot, tile=512):
    n, width = x2.shape
    slots = back.shape[0]
    outs = [sds((n, width), F32), sds((n, width), BF), sds((n, width), F32), sds((n, 128), F32)]
    rest = [gates, router, x2, rows, cot]
    return pl.pallas_call(
        functools.partial(leave_body, experts),
        grid=(slots // tile,),
        in_specs=[
            pl.BlockSpec((tile, width + 128), lambda i: (i, 0)),
            pl.BlockSpec((n, tile), lambda i: (0, i)),
        ]
        + [whole(a.shape) for a in rest],
        out_specs=[whole(o.shape) for o in outs],
        out_shape=outs,
        scratch_shapes=[pltpu.VMEM((n, width + 128), F32)],
        compiler_params=pltpu.CompilerParams(vmem_limit_bytes=VM),
        cost_estimate=pl.CostEstimate(
            flops=2 * n * width * slots, bytes_accessed=3 * slots * width, transcendentals=0
        ),
        name="leave",
    )(back, to_slot, *rest)


def small_body(experts, h2_ref, dl_ref, dh2_ref, x2_ref, out_ref):
    hi, lo = split(dl_ref[...])
    h2, x2 = h2_ref[...], x2_ref[...]
    out_ref[...] = tdot(h2, hi) + tdot(h2, lo) + column_sum(dh2_ref[...] * x2 * rms(x2), experts)


def small_slopes(experts, h2, dl, dh2, x2):
    n, width = x2.shape
    return one_step(
        functools.partial(small_body, experts),
        "small_slopes",
        [],
        [h2, dl, dh2, x2],
        [sds((width, 128), F32)],
        [],
        8 * n * width * 128,
    )[0]


def attend_back_body(experts, place_ref, *refs):
    das, xs = refs[0:4], refs[4:8]
    wo_ref, qkv_ref, o_own, o_far, lse_own, lse_far, h1_ref, w_ref = refs[8:16]
    cos_ref, sin_ref, bias_ref, small_ref = refs[16:20]
    keep_ref, give_ref = refs[20:22]
    parts = refs[22:26]
    da, do, dqk, dqkv, o_ref, lse_ref = refs[26:32]
    core = place_ref[1]
    rows = xs[0].shape[0]
    q_w, qkv_w = o_ref.shape[1], qkv_ref.shape[1]
    kv_w = (qkv_w - q_w) // 2
    group = q_w // kv_w
    scale = HEAD ** (-0.5)
    for r in range(WS):
        da[r * rows : (r + 1) * rows, :] = das[r][...]
    o_ref[:rows, :] = o_own[...]
    o_ref[rows:, :] = o_far[...]
    lse_ref[:rows, :] = lse_own[...]
    lse_ref[rows:, :] = lse_far[...]
    do[...] = dot_t(da[...], wo_ref[...]).astype(BF)
    for n in range(kv_w // HEAD):
        at = n * HEAD
        k = qkv_ref[:, q_w + at : q_w + at + HEAD]
        v = qkv_ref[:, q_w + kv_w + at : q_w + kv_w + at + HEAD]
        dk, dv = None, None
        for h in range(n * group, (n + 1) * group):
            q = qkv_ref[:, h * HEAD : (h + 1) * HEAD]
            doh = do[:, h * HEAD : (h + 1) * HEAD]
            p = jnp.exp(dot_t(q, k) * scale + bias_ref[...] - lse_ref[:, h : h + 1])
            dp = dot_t(doh, v)
            delta = jnp.sum(p * dp, axis=1, keepdims=True)
            ds = (p * (dp - delta)).astype(BF)
            dqk[:, h * HEAD : (h + 1) * HEAD] = dot(ds, k) * scale
            more_k, more_v = tdot(ds, q), tdot(p.astype(BF), doh)
            dk = more_k if dk is None else dk + more_k
            dv = more_v if dv is None else dv + more_v
        dqk[:, q_w + at : q_w + at + HEAD] = dk * scale
        dqkv[:, q_w + kv_w + at : q_w + kv_w + at + HEAD] = dv.astype(BF)
    dqkv[:, qkv_w:] = jnp.zeros((da.shape[0], 128), BF)
    d = dqk[...]
    times = (q_w + kv_w) // 128
    d = d * wide(cos_ref, times) - other_half(d) * wide(sin_ref, times)
    dqkv[:, : q_w + kv_w] = d.astype(BF)
    small = small_ref[...]
    for r in range(WS):
        dh1 = dot_t(dqkv[r * rows : (r + 1) * rows, :qkv_w], w_ref[...])
        parts[r][...] = dh1.astype(parts[r].dtype)
        x = xs[r][...].astype(F32)
        small = small + column_sum(dh1 * x * rms(x), experts + 1)
    half = keep_ref.shape[3]
    chips, step = keep_ref.shape[0], keep_ref.shape[2]
    count = chips * step

    def put(i, first, second):
        kept = jnp.where(core == 0, first, second)
        given = jnp.where(core == 0, second, first)
        keep_ref[:, i] = kept.reshape(chips, step, half)
        give_ref[:, i] = given.reshape(chips, step, half).astype(BF)

    for i in range(WS):
        both = tdot(h1_ref[:, i * count : (i + 1) * count], dqkv[...])
        mine = small[i * count : (i + 1) * count]
        second = jnp.concatenate([both[:, half : 2 * half - 128], both[:, 2 * half - 128 :] + mine], axis=1)
        put(i, both[:, :half], second)
    slope = tdot(o_ref[...], da[...])
    for i in range(2):
        put(WS + i, slope[:, i * half : (i + 1) * half], slope[:, (2 + i) * half : (3 + i) * half])


def attend_back(experts, place, das, xs, wo, qkv, os, lses, h1, w, cos, sin, bias, small):
    rows, width = xs[0].shape
    tree = rows * WS
    q_w, qkv_w = wo.shape[0], qkv.shape[1]
    half = (qkv_w + 128) // 2
    load = (CHIPS, WS + 2, width // WS // CHIPS, half)
    outs = [sds(load, F32), sds(load, BF), sds((rows, width), F32)] + [sds((rows, width), BF)] * 3
    scratch = [
        pltpu.VMEM((tree, width), BF),
        pltpu.VMEM((tree, q_w), BF),
        pltpu.VMEM((tree, (q_w + qkv_w) // 2), F32),
        pltpu.VMEM((tree, qkv_w + 128), BF),
        pltpu.VMEM((tree, q_w), BF),
        pltpu.VMEM((tree, 128), F32),
    ]
    flops = 4 * tree * width * (qkv_w + q_w) + 10 * tree * tree * q_w
    return one_step(
        functools.partial(attend_back_body, experts),
        "attend_back",
        [place],
        [*das, *xs, wo, qkv, *os, *lses, h1, w, cos, sin, bias, small],
        outs,
        scratch,
        flops,
    )


def shards(
    tokens,
    cotangent,
    seg_lengths,
    parents,
    routes,
    norm_attn,
    w_query,
    w_key,
    w_value,
    w_out,
    norm_moe,
    w_router,
    w_gate,
    w_up,
    w_down,
):
    me = lax.axis_index("ws")
    expert = lax.axis_index("exp")
    core = expert % 2
    place = jnp.stack([me, core]).astype(jnp.int32)
    rows, width = tokens.shape
    shard = width // WS
    strip = shard // 2
    experts = 2 * CHIPS
    q_w, kv_w = HEADS // WS * HEAD, KV_HEADS // WS * HEAD
    slots = experts * CAP

    def gathered(v):
        return [v] + [from_peer(v, k) for k in (1, 2, 3)]

    xs = gathered(tokens)

    pieces = pack(experts, place, w_query, w_key, w_value, w_router, norm_attn, norm_moe)
    pieces, routes = lax.optimization_barrier((pieces, routes))
    own = [pieces[0]] + [from_peer(pieces[k], k) for k in (1, 2, 3)]

    labels = jnp.arange(experts, dtype=jnp.int32)
    lane = jnp.arange(128, dtype=jnp.int32)
    chosen = jnp.any(routes[:, :, None] == lane[None, None, :], axis=1)
    row_id = jnp.arange(rows, dtype=jnp.int32)
    before = (row_id[None, :] < row_id[:, None]).astype(BF)
    rank = dot(before, chosen.astype(BF))
    col = jnp.arange(slots, dtype=jnp.int32)
    spread = (col[None, :] // CAP == lane[:, None]).astype(BF)
    spot = dot(jnp.where(chosen, rank + 1.0, 0.0).astype(BF), spread)
    to_slot = (spot == (col % CAP + 1).astype(F32)[None, :]).astype(BF)
    chosen = chosen.astype(BF)
    extra = jnp.concatenate([cotangent, chosen], axis=1)
    dy_send = tdot(to_slot, extra).astype(BF).reshape(experts, CAP, width + 128)
    dy_send, xs[1], xs[3] = lax.optimization_barrier((dy_send, xs[1], xs[3]))
    dy_slots = lax.all_to_all(dy_send, "exp", 0, 0, tiled=True).reshape(slots, width + 128)

    order = (
        ((me + jnp.arange(WS, dtype=jnp.int32)) % WS)[:, None] * rows + row_id[None, :]
    ).reshape(-1)
    visible, position = tree_layout(seg_lengths[0], parents[0], order)
    bias = jnp.where(visible, 0.0, MASKED).astype(F32)
    inverse = THETA ** (-(lane % (HEAD // 2)).astype(F32) * 2.0 / HEAD)
    angles = position.astype(F32)[:, None] * inverse[None, :]
    cosines = jnp.cos(angles)
    sines = jnp.where((lane % HEAD < HEAD // 2)[None, :], -1.0, 1.0) * jnp.sin(angles)
    own[1], bias, cosines, sines = lax.optimization_barrier((own[1], bias, cosines, sines))
    twin = [pieces[WS]] + [other_core(own[k]) for k in (1, 2, 3)]
    h1, qkv, o_far, lse_far, w_qkv, small_full, gains, *parts = attend(
        experts, place, xs, own, twin, cosines, sines, bias, w_out
    )
    o_own, lse_own, part_own = attend_own(rows, qkv, bias, w_out)
    sums = [part_own] + [to_peer(parts[k - 1], k) for k in (1, 2, 3)]
    x2, h2, x_send = enter(tokens, sums, gains, to_slot)
    x_send, wg_own, wu_own, wd_own = lax.optimization_barrier(
        (x_send, w_gate[0], w_up[0], w_down[0])
    )
    x_slots = lax.all_to_all(
        x_send.reshape(experts, CAP, width), "exp", 0, 0, tiled=True
    ).reshape(slots, width)

    sel = jnp.concatenate(
        [
            (lane == expert).astype(F32)[None],
            (lane == expert + experts).astype(F32)[None],
            jnp.zeros((6, 128), F32),
        ],
        axis=0,
    )
    wd = gathered(wd_own)
    gates, gate_slots = gate_terms(h2, small_full, to_slot, chosen, spread)
    wd[1], gates, gate_slots = lax.optimization_barrier((wd[1], gates, gate_slots))
    dx_send, hidden, d_gu, slot_gates = expert_pass(
        x_slots, dy_slots, sel, small_full, gathered(wg_own), gathered(wu_own), wd, 256
    )
    dx_back = lax.all_to_all(
        dx_send.reshape(experts, CAP, width + 128), "exp", 0, 0, tiled=True
    ).reshape(slots, width + 128)

    own_g, own_u, gu1, gu2, gu3 = in_slopes(x_slots, d_gu)
    gu1, gu2, gu3 = to_peer(gu1, 1), to_peer(gu2, 2), to_peer(gu3, 3)
    hidden, gu1 = lax.optimization_barrier((hidden, gu1))
    y, own_d, dn1, dn2, dn3 = out_slopes(hidden, dy_slots, slot_gates, wd)
    dn1, dn2, dn3 = to_peer(dn1, 1), to_peer(dn2, 2), to_peer(dn3, 3)
    dx_back, y, gu1, dn1, gu2, dn2, gu3, dn3 = lax.optimization_barrier(
        (dx_back, y, gu1, dn1, gu2, dn2, gu3, dn3)
    )
    y_back = lax.all_to_all(y.reshape(experts, CAP, width), "exp", 0, 0, tiled=True).reshape(
        slots, width
    )

    dx2, d_a, dh2, dl = leave(
        experts, dx_back, to_slot, gates, small_full, x2, gains, cotangent
    )
    das = gathered(d_a)
    small_terms = small_slopes(experts, h2, dl, dh2, x2)
    grad_gu = jnp.stack([own_g, own_u]) + gu1.astype(F32) + gu2.astype(F32) + gu3.astype(F32)
    grad_wg, grad_wu = grad_gu[0][None], grad_gu[1][None]
    grad_wd = (own_d + dn1.astype(F32) + dn2.astype(F32) + dn3.astype(F32))[None]
    das, grad_wg, grad_wu, grad_wd = lax.optimization_barrier((das, grad_wg, grad_wu, grad_wd))
    keep, give, *slopes = attend_back(
        experts,
        place,
        das,
        xs,
        w_out,
        qkv,
        (o_own, o_far),
        (lse_own, lse_far),
        h1,
        w_qkv,
        cosines,
        sines,
        bias,
        small_terms,
    )
    sent = (keep + other_core(give).astype(F32)).astype(BF)
    sent, y_back = lax.optimization_barrier((sent, y_back))
    step = shard // CHIPS
    both = dot(gate_slots, y_back)
    layer_out = (x2 + both[:rows] + both[rows:]).astype(BF)
    got = same_core(sent)
    slopes = [slopes[0]] + [to_peer(slopes[k], k) for k in (1, 2, 3)]
    got, layer_out, slopes = lax.optimization_barrier((got, layer_out, slopes))
    dh1 = slopes[0]
    for k in (1, 2, 3):
        dh1 = dh1 + slopes[k].astype(F32)
    resid = tokens.astype(F32)
    scale = lax.rsqrt(jnp.mean(resid * resid, axis=-1, keepdims=True) + EPS)
    inner = jnp.mean(gains[0:1] * dh1 * resid, axis=-1, keepdims=True)
    grad_tokens = dx2 + scale * gains[0:1] * dh1 - resid * scale * scale * scale * inner

    total = jnp.sum(got.astype(F32), axis=0).astype(BF)
    final = jnp.stack(
        [lax.dynamic_index_in_dim(total, me, 0, False)]
        + [
            from_peer(lax.dynamic_index_in_dim(total, (me - k) % WS, 0, False), k)
            for k in (1, 2, 3)
        ]
        + [total[WS], total[WS + 1]]
    )
    spread_out = same_core(jnp.broadcast_to(final, (CHIPS,) + final.shape))
    twin_out = other_core(spread_out)
    sum_query, sum_key, sum_value, sum_router, sum_gains, sum_out = finish(
        experts, place, spread_out, twin_out
    )

    return (
        layer_out,
        grad_tokens,
        sum_gains[1],
        sum_query,
        sum_key,
        sum_value,
        sum_out,
        sum_gains[0],
        sum_router.T,
        grad_wg,
        grad_wu,
        grad_wd,
    )


def solution(mesh):
    rows = P(("exp", "ws"), None)
    placed = (
        rows,
        rows,
        P("exp", None),
        P("exp", None),
        rows,
        P("ws"),
        P("ws", None),
        P("ws", None),
        P("ws", None),
        P("ws", None),
        P("ws"),
        P("ws", None),
        P("exp", None, "ws"),
        P("exp", None, "ws"),
        P("exp", "ws", None),
    )
    return jax.shard_map(
        shards,
        mesh=mesh,
        in_specs=placed,
        out_specs=(
            rows,
            rows,
            P("ws"),
            P("ws", None),
            P("ws", None),
            P("ws", None),
            P("ws", None),
            P("ws"),
            P("ws", None),
            P("exp", None, "ws"),
            P("exp", None, "ws"),
            P("exp", "ws", None),
        ),
        check_vma=False,
    )
```

```python
import functools

import jax
import jax.numpy as jnp
from jax import lax
from jax.experimental import pallas as pl
from jax.experimental.pallas import tpu as pltpu
from jax.sharding import PartitionSpec as P

HEADS = 24
KV_HEADS = 8
HEAD = 64
EPS = 1e-06
THETA = 10000.0
MASKED = -1e30
BF = jnp.bfloat16
F32 = jnp.float32
WS = 4
CHIPS = 16
CAP = 48
VM = 60 * 1024 * 1024


def dot(a, b):
    return jnp.dot(a, b, preferred_element_type=F32)


def dot_t(a, b):
    return lax.dot_general(a, b, (((1,), (1,)), ((), ())), preferred_element_type=F32)


def tdot(a, b):
    return lax.dot_general(a, b, (((0,), (0,)), ((), ())), preferred_element_type=F32)


def split(v):
    hi = v.astype(BF)
    return hi, (v - hi.astype(F32)).astype(BF)


def from_peer(v, k):
    return lax.ppermute(v, "ws", [(s, (s - k) % WS) for s in range(WS)])


def to_peer(v, k):
    return lax.ppermute(v, "ws", [(s, (s + k) % WS) for s in range(WS)])


def other_core(v):
    return lax.ppermute(v, "exp", [(s, s ^ 1) for s in range(2 * CHIPS)])


def same_core(v):
    groups = [[2 * chip + core for chip in range(CHIPS)] for core in range(2)]
    return lax.all_to_all(v, "exp", 0, 0, tiled=True, axis_index_groups=groups)


def tree_layout(lengths, parents, token_index):
    seg = lengths.shape[0]
    labels = jnp.arange(seg, dtype=jnp.int32)
    segment_end = jnp.cumsum(lengths, dtype=jnp.int32)
    starts = segment_end - lengths
    segment = jnp.sum((token_index[:, None] >= segment_end[None, :]).astype(jnp.int32), axis=1)
    reach = ((parents[:, None] == labels[None, :]) | (labels[:, None] == labels[None, :])).astype(
        BF
    )
    for _ in range(4):
        reach = (dot(reach, reach) > 0.5).astype(BF)
    above = jnp.sum(reach.astype(jnp.int32) * lengths[None, :], axis=1) - lengths
    members = segment[:, None] == labels[None, :]
    position = jnp.sum(jnp.where(members, (above - starts)[None, :], 0), axis=1) + token_index
    members = members.astype(BF)
    reaches = dot(members, reach).astype(BF)
    visible = (dot_t(reaches, members) > 0.5) & (token_index[None, :] <= token_index[:, None])
    return visible, position


def expert_body(width, ff, x_ref, dy_ref, sel_ref, wr_ref, *rest):
    wg, wu, wd = rest[0:4], rest[4:8], rest[8:12]
    dx_ref, h_ref, dgu_ref, gate_ref = rest[12:16]
    wgu, wdn = rest[16:]
    part = wg[0].shape[1]

    @pl.when(pl.program_id(0) == 0)
    def _():
        for r in range(WS):
            wgu[:, r * part : (r + 1) * part] = wg[r][...]
            wgu[:, ff + r * part : ff + (r + 1) * part] = wu[r][...]
            wdn[r * part : (r + 1) * part, :] = wd[r][...]
        wgu[:, 2 * ff :] = wr_ref[...]

    pre = dot(x_ref[...], wgu[...])
    g, u, logits = pre[:, :ff], pre[:, ff : 2 * ff], pre[:, 2 * ff :]
    mask = dy_ref[:, width:].astype(F32) > 0.5
    logits = jnp.where(mask, logits, MASKED)
    lifted = jnp.where(mask, jnp.exp(logits - jnp.max(logits, axis=1, keepdims=True)), 0.0)
    total = jnp.maximum(jnp.sum(lifted, axis=1, keepdims=True), 1e-30)
    gate = jnp.sum(lifted * sel_ref[0:1, :], axis=1, keepdims=True) / total
    gate_ref[...] = jnp.broadcast_to(gate, gate_ref.shape)
    sig = 1.0 / (1.0 + jnp.exp(-g))
    silu = g * sig
    h = (silu * u).astype(BF)
    h_ref[...] = h
    raw = dot_t(dy_ref[:, :width], wdn[...])
    dgate = jnp.sum(raw * h.astype(F32), axis=1, keepdims=True)
    dh = raw * gate
    dgu_ref[:, :ff] = (dh * u * sig * (1.0 + g * (1.0 - sig))).astype(BF)
    dgu_ref[:, ff:] = (dh * silu).astype(BF)
    dx_ref[:, :width] = dot_t(dgu_ref[...], wgu[:, : 2 * ff]).astype(BF)
    hi = dgate.astype(BF).astype(F32)
    dx_ref[:, width:] = (hi * sel_ref[0:1, :] + (dgate - hi) * sel_ref[1:2, :]).astype(BF)


def expert_pass(x, dy, sel, wr, wg, wu, wd, tile):
    slots, width = x.shape
    part = wg[0].shape[1]
    ff = WS * part
    row = lambda w: pl.BlockSpec((tile, w), lambda i: (i, 0))
    once = lambda a: pl.BlockSpec(a.shape, lambda i: (0, 0))
    return pl.pallas_call(
        functools.partial(expert_body, width, ff),
        grid=(slots // tile,),
        in_specs=[row(width), row(width + 128), once(sel), once(wr)]
        + [once(a) for a in (*wg, *wu, *wd)],
        out_specs=[row(width + 128), row(ff), row(2 * ff), row(128)],
        out_shape=[
            jax.ShapeDtypeStruct((slots, width + 128), BF),
            jax.ShapeDtypeStruct((slots, ff), BF),
            jax.ShapeDtypeStruct((slots, 2 * ff), BF),
            jax.ShapeDtypeStruct((slots, 128), F32),
        ],
        scratch_shapes=[pltpu.VMEM((width, 2 * ff + 128), BF), pltpu.VMEM((ff, width), BF)],
        compiler_params=pltpu.CompilerParams(vmem_limit_bytes=VM),
        cost_estimate=pl.CostEstimate(
            flops=10 * slots * width * ff, bytes_accessed=9 * slots * width, transcendentals=0
        ),
        name="expert_pass",
    )(x, dy, sel, wr, *wg, *wu, *wd)


def in_slope_body(x_ref, dgu_ref, own_g, own_u, *peers):
    part = own_g.shape[1]
    ff = WS * part
    gu = tdot(x_ref[...], dgu_ref[...])
    own_g[...] = gu[:, :part]
    own_u[...] = gu[:, ff : ff + part]
    for k in (1, 2, 3):
        peers[k - 1][0] = gu[:, k * part : (k + 1) * part].astype(BF)
        peers[k - 1][1] = gu[:, ff + k * part : ff + (k + 1) * part].astype(BF)


def in_slopes(x, dgu, tile=256):
    slots, width = x.shape
    part = dgu.shape[1] // (2 * WS)
    tall = pl.BlockSpec((tile, part), lambda i: (i, 0))
    pair = pl.BlockSpec((2, tile, part), lambda i: (0, i, 0))
    return pl.pallas_call(
        in_slope_body,
        grid=(width // tile,),
        in_specs=[pl.BlockSpec((slots, tile), lambda i: (0, i)), whole(dgu.shape)],
        out_specs=[tall, tall] + [pair] * 3,
        out_shape=[sds((width, part), F32)] * 2 + [sds((2, width, part), BF)] * 3,
        compiler_params=pltpu.CompilerParams(vmem_limit_bytes=VM),
        cost_estimate=pl.CostEstimate(
            flops=2 * slots * width * dgu.shape[1],
            bytes_accessed=4 * slots * width,
            transcendentals=0,
        ),
        name="in_slopes",
    )(x, dgu)


def out_slope_body(h_ref, dy_ref, gate_ref, *refs):
    wd = refs[0:4]
    y_ref, own_d = refs[4:6]
    part = own_d.shape[0]
    d_y = (gate_ref[:, 0:1] * dy_ref[...].astype(F32)).astype(BF)
    dn = tdot(h_ref[...], d_y)
    own_d[...] = dn[:part]
    for k in (1, 2, 3):
        refs[5 + k][...] = dn[k * part : (k + 1) * part].astype(BF)
    y_ref[...] = dot(h_ref[...], jnp.concatenate([w[...] for w in wd], axis=0)).astype(BF)


def out_slopes(h, dy, gate, wd, tile=256):
    slots, ff = h.shape
    width = wd[0].shape[1]
    part = ff // WS
    col = pl.BlockSpec((slots, tile), lambda i: (0, i))
    flat = pl.BlockSpec((part, tile), lambda i: (0, i))
    return pl.pallas_call(
        out_slope_body,
        grid=(width // tile,),
        in_specs=[whole(h.shape), col, whole(gate.shape)] + [flat] * WS,
        out_specs=[col, flat] + [flat] * 3,
        out_shape=[sds((slots, width), BF), sds((part, width), F32)]
        + [sds((part, width), BF)] * 3,
        compiler_params=pltpu.CompilerParams(vmem_limit_bytes=VM),
        cost_estimate=pl.CostEstimate(
            flops=4 * slots * width * ff, bytes_accessed=4 * slots * width, transcendentals=0
        ),
        name="out_slopes",
    )(h, dy, gate, *wd)


def finish_body(experts, place_ref, a_ref, b_ref, ao_ref, bo_ref, *refs):
    q_ref, k_ref, v_ref, r_ref, g_ref, o_ref, s_ref = refs
    turn = pl.program_id(0)
    second = place_ref[1] == 1
    rows = q_ref.shape[0]
    half = a_ref.shape[3]
    kv = k_ref.shape[1]
    mine = a_ref[:, 0].astype(F32).reshape(rows, half)
    twin = b_ref[:, 0].astype(F32).reshape(rows, half)
    q_ref[...] = jnp.where(second, twin, mine)
    rest = jnp.where(second, mine, twin)
    k_ref[...] = rest[:, :kv]
    v_ref[...] = rest[:, kv : 2 * kv]

    @pl.when(turn == 0)
    def _():
        s_ref[...] = rest[:, 2 * kv :]

    @pl.when(turn > 0)
    def _():
        s_ref[...] += rest[:, 2 * kv :]

    @pl.when(turn == WS - 1)
    def _():
        turned = s_ref[...].T
        r_ref[...] = turned[:experts]
        g_ref[...] = turned[experts : experts + 8]

    mine = ao_ref[:, 0].astype(F32).reshape(rows, half)
    twin = bo_ref[:, 0].astype(F32).reshape(rows, half)
    o_ref[...] = jnp.where(second == (turn < 2), twin, mine)


def finish(experts, place, mine, twin):
    chips, sets, step, half = mine.shape
    rows = chips * step
    first = pl.BlockSpec((chips, 1, step, half), lambda i, p: (0, i, 0, 0))
    later = pl.BlockSpec((chips, 1, step, half), lambda i, p: (0, WS + i % 2, 0, 0))
    turned = lambda i, p: (0, lax.rem(p[0] + i, WS))
    kv = (half - 128) // 2
    S = jax.ShapeDtypeStruct
    return pl.pallas_call(
        functools.partial(finish_body, experts),
        grid_spec=pltpu.PrefetchScalarGridSpec(
            num_scalar_prefetch=1,
            grid=(WS,),
            in_specs=[first, first, later, later],
            out_specs=[
                pl.BlockSpec((rows, half), turned),
                pl.BlockSpec((rows, kv), turned),
                pl.BlockSpec((rows, kv), turned),
                whole((experts, rows)),
                whole((8, rows)),
                pl.BlockSpec((rows, half), lambda i, p: (0, i)),
            ],
            scratch_shapes=[pltpu.VMEM((rows, 128), F32)],
        ),
        out_shape=[
            S((rows, WS * half), F32),
            S((rows, WS * kv), F32),
            S((rows, WS * kv), F32),
            S((experts, rows), F32),
            S((8, rows), F32),
            S((rows, WS * half), F32),
        ],
        compiler_params=pltpu.CompilerParams(vmem_limit_bytes=VM),
        cost_estimate=pl.CostEstimate(flops=0, bytes_accessed=16 * rows * WS * half, transcendentals=0),
        name="finish",
    )(place, mine, twin, mine, twin)


def whole(shape):
    return pl.BlockSpec(shape, lambda *_: (0,) * len(shape))


def sds(shape, kind):
    return jax.ShapeDtypeStruct(shape, kind)


def one_step(body, name, scalars, arrays, outs, scratch, flops):
    moved = sum(a.size * a.dtype.itemsize for a in arrays)
    return pl.pallas_call(
        body,
        in_specs=[pl.BlockSpec(memory_space=pltpu.SMEM)] * len(scalars)
        + [pl.BlockSpec(memory_space=pltpu.VMEM)] * len(arrays),
        out_specs=[pl.BlockSpec(memory_space=pltpu.VMEM)] * len(outs),
        out_shape=outs,
        scratch_shapes=scratch,
        compiler_params=pltpu.CompilerParams(vmem_limit_bytes=VM),
        cost_estimate=pl.CostEstimate(flops=flops, bytes_accessed=moved, transcendentals=0),
        name=name,
    )(*scalars, *arrays)


def other_half(v):
    lanes = v.shape[1]
    low = lax.broadcasted_iota(jnp.int32, v.shape, 1) % HEAD < HEAD // 2
    ahead = pltpu.roll(v, lanes - HEAD // 2, 1)
    behind = pltpu.roll(v, HEAD // 2, 1)
    return jnp.where(low, ahead, behind)


def wide(ref, times):
    return jnp.concatenate([ref[...]] * times, axis=1)


def rms(x):
    return lax.rsqrt(jnp.mean(x * x, axis=1, keepdims=True) + EPS)


def column_sum(m, lane):
    hi, lo = split(m)
    pick = (lax.broadcasted_iota(jnp.int32, (m.shape[0], 128), 1) == lane).astype(F32).astype(BF)
    return tdot(hi, pick) + tdot(lo, pick)


def pack_body(experts, place_ref, x_ref, wq, wk, wv, wr, norms, *outs):
    small = outs[WS + 1]
    me, core = place_ref[0], place_ref[1]
    rows = x_ref.shape[0]
    strip = wq.shape[0] // 2
    q_w, kv_w = wq.shape[1] // WS, wk.shape[1] // WS
    shard = wq.shape[0]
    few = [wr[...].astype(F32), norms[...].astype(F32), jnp.zeros((126 - experts, shard), F32)]
    small[...] = jnp.concatenate(few, axis=0).T.astype(BF)

    def place(out, top, left, side, d, start, count):
        part = pl.ds(pl.multiple_of(side * strip + start, 32), count)
        here = slice(top, top + count)
        spot = pl.ds(pl.multiple_of(d * kv_w, 128), kv_w)
        out[here, left : left + q_w] = wq[part, pl.ds(pl.multiple_of(d * q_w, 128), q_w)]
        out[here, left + q_w : left + q_w + kv_w] = wk[part, spot]
        out[here, left + q_w + kv_w : left + q_w + 2 * kv_w] = wv[part, spot]
        out[here, left + q_w + 2 * kv_w : left + q_w + 2 * kv_w + 128] = small[part, :]

    for r in range(WS + 1):
        side = core if r < WS else 1 - core
        d = lax.rem(me + WS - r % WS, WS)
        if r == 2:
            outs[r][:rows, :] = x_ref[...]
            for half in range(2):
                left = half * (q_w + 2 * kv_w + 128)
                place(outs[r], rows, left, side, d, half * strip // 2, strip // 2)
        else:
            place(outs[r], 0, 0, side, d, 0, strip)


def pack(experts, place, x, wq, wk, wv, wr, norms):
    shard = wq.shape[0]
    rows, width = x.shape
    wide_w = (wq.shape[1] + 2 * wk.shape[1]) // WS + 128
    outs = [sds((shard // 2, wide_w), BF)] * (WS + 1)
    outs[2] = sds((rows + shard // 4, 2 * wide_w), BF)
    return one_step(
        functools.partial(pack_body, experts),
        "pack",
        [place],
        [x, wq, wk, wv, wr, norms],
        outs,
        [pltpu.VMEM((shard, 128), BF)],
        0,
    )


def attend_rows(qkv_ref, bias_ref, o_ref, lse_ref, start, q_w, kv_w):
    rows = o_ref.shape[0]
    group = q_w // kv_w
    here = slice(start, start + rows)
    for h in range(q_w // HEAD):
        at = h // group * HEAD
        q = qkv_ref[here, h * HEAD : (h + 1) * HEAD]
        k = qkv_ref[:, q_w + at : q_w + at + HEAD]
        v = qkv_ref[:, q_w + kv_w + at : q_w + kv_w + at + HEAD]
        s = dot_t(q, k) * HEAD ** (-0.5) + bias_ref[here, :]
        peak = jnp.max(s, axis=1, keepdims=True)
        p = jnp.exp(s - peak)
        total = jnp.sum(p, axis=1, keepdims=True)
        lse_ref[:, h : h + 1] = peak + jnp.log(total)
        o_ref[:, h * HEAD : (h + 1) * HEAD] = dot((p / total).astype(BF), v).astype(BF)


def attend_body(experts, place_ref, *refs):
    xs, own, twin = refs[0:4], refs[4:8], refs[8:12]
    cos_ref, sin_ref, bias_ref, wo_ref = refs[12:16]
    h1_ref, qkv_ref, o_ref, lse_ref, w_ref, small_ref, rows_ref = refs[16:23]
    parts = refs[23:26]
    me, core = place_ref[0], place_ref[1]
    rows = xs[0].shape[0]
    strip = own[0].shape[0]
    wide_w = own[0].shape[1]
    q_w = o_ref.shape[1]
    qkv_w = qkv_ref.shape[1]
    kv_w = (qkv_w - q_w) // 2
    for r in range(WS):
        base = lax.rem(me + r, WS) * (2 * strip)
        for source, side in ((own[r], core), (twin[r], 1 - core)):
            folds = source.shape[1] // wide_w
            count = strip // folds
            for f in range(folds):
                left = f * wide_w
                spot = pl.ds(pl.multiple_of(base + side * strip + f * count, 32), count)
                w_ref[spot, :] = source[:, left : left + qkv_w]
                small_ref[spot, :] = source[:, left + qkv_w : left + wide_w]
    turned = small_ref[...].astype(F32).T
    rows_ref[...] = jnp.concatenate(
        [turned[experts : experts + 2], jnp.zeros((6, turned.shape[1]), F32)], axis=0
    )
    gain = turned[experts : experts + 1]
    for r in range(WS):
        x = xs[r][:rows, :].astype(F32)
        h1_ref[r * rows : (r + 1) * rows, :] = (x * rms(x) * gain).astype(BF)
    qkv = dot(h1_ref[...], w_ref[...])
    qk = qkv[:, : q_w + kv_w]
    times = (q_w + kv_w) // 128
    qk = qk * wide(cos_ref, times) + other_half(qk) * wide(sin_ref, times)
    qkv_ref[:, : q_w + kv_w] = qk.astype(BF)
    qkv_ref[:, q_w + kv_w :] = qkv[:, q_w + kv_w :].astype(BF)
    attend_rows(qkv_ref, bias_ref, o_ref, lse_ref, rows, q_w, kv_w)
    for r in range(3):
        part = dot(o_ref[r * rows : (r + 1) * rows, :], wo_ref[...])
        parts[r][...] = part.astype(BF)


def attend(experts, place, xs, own, twin, cos, sin, bias, wo):
    rows, width = xs[0].shape
    tree = rows * WS
    q_w, qkv_w = wo.shape[0], own[0].shape[1] - 128
    outs = [
        sds((tree, width), BF),
        sds((tree, qkv_w), BF),
        sds((tree - rows, q_w), BF),
        sds((tree - rows, 128), F32),
        sds((width, qkv_w), BF),
        sds((width, 128), BF),
        sds((8, width), F32),
    ] + [sds((rows, width), BF)] * 3
    flops = 27 * tree * width * (qkv_w + q_w)
    return one_step(
        functools.partial(attend_body, experts),
        "attend",
        [place],
        [*xs, *own, *twin, cos, sin, bias, wo],
        outs,
        [],
        flops,
    )


def attend_own_body(qkv_ref, bias_ref, wo_ref, o_ref, lse_ref, part_ref):
    q_w = o_ref.shape[1]
    kv_w = (qkv_ref.shape[1] - q_w) // 2
    attend_rows(qkv_ref, bias_ref, o_ref, lse_ref, 0, q_w, kv_w)
    part_ref[...] = dot(o_ref[...], wo_ref[...])


def attend_own(rows, qkv, bias, wo):
    q_w, width = wo.shape
    outs = [sds((rows, q_w), BF), sds((rows, 128), F32), sds((rows, width), F32)]
    flops = 2 * rows * width * q_w + 4 * rows * qkv.shape[0] * q_w
    return one_step(attend_own_body, "attend_own", [], [qkv, bias, wo], outs, [], flops)


def enter_body(x_ref, p0, p1, p2, p3, rows_ref, slot_ref, x2_ref, h2_ref, send_ref):
    @pl.when(pl.program_id(0) == 0)
    def _():
        x2 = x_ref[...].astype(F32) + p0[...]
        for p in (p1, p2, p3):
            x2 = x2 + p[...].astype(F32)
        x2_ref[...] = x2
        h2_ref[...] = (x2 * rms(x2) * rows_ref[1:2, :]).astype(BF)

    send_ref[...] = tdot(slot_ref[...], h2_ref[...]).astype(BF)


def enter(x, parts, rows, to_slot, tile=512):
    n, width = x.shape
    slots = to_slot.shape[1]
    arrays = [x, *parts, rows]
    return pl.pallas_call(
        enter_body,
        grid=(slots // tile,),
        in_specs=[whole(a.shape) for a in arrays] + [pl.BlockSpec((n, tile), lambda i: (0, i))],
        out_specs=[
            whole((n, width)),
            whole((n, width)),
            pl.BlockSpec((tile, width), lambda i: (i, 0)),
        ],
        out_shape=[sds((n, width), F32), sds((n, width), BF), sds((slots, width), BF)],
        compiler_params=pltpu.CompilerParams(vmem_limit_bytes=VM),
        cost_estimate=pl.CostEstimate(
            flops=2 * n * width * slots, bytes_accessed=3 * slots * width, transcendentals=0
        ),
        name="enter",
    )(*arrays, to_slot)


def gate_body(h2_ref, router_ref, slot_ref, chosen_ref, spread_ref, gates_ref, gs_ref):
    logits = dot(h2_ref[...], router_ref[...])
    mask = chosen_ref[...].astype(F32) > 0.5
    logits = jnp.where(mask, logits, MASKED)
    lifted = jnp.where(mask, jnp.exp(logits - jnp.max(logits, axis=1, keepdims=True)), 0.0)
    gates = lifted / jnp.maximum(jnp.sum(lifted, axis=1, keepdims=True), 1e-30)
    gates_ref[...] = gates
    hi, lo = split(gates)
    on_slots = dot(hi, spread_ref[...]) + dot(lo, spread_ref[...])
    hi, lo = split(on_slots * slot_ref[...].astype(F32))
    rows = gates.shape[0]
    gs_ref[:rows, :] = hi
    gs_ref[rows:, :] = lo


def gate_terms(h2, router, to_slot, chosen, spread):
    n, slots = to_slot.shape
    outs = [sds((n, 128), F32), sds((2 * n, slots), BF)]
    arrays = [h2, router, to_slot, chosen, spread]
    return one_step(gate_body, "gate_terms", [], arrays, outs, [], 8 * n * 128 * slots)


def leave_body(experts, back_ref, slot_ref, gates_ref, router_ref, x2_ref, rows_ref, cot_ref, *outs):
    dx2_ref, da_ref, dh2_ref, dl_ref, sum_ref = outs
    width = x2_ref.shape[1]
    step = pl.program_id(0)
    more = dot(slot_ref[...], back_ref[...])

    @pl.when(step == 0)
    def _():
        sum_ref[...] = more

    @pl.when(step > 0)
    def _():
        sum_ref[...] += more

    @pl.when(step == pl.num_programs(0) - 1)
    def _():
        tail = sum_ref[:, width:]
        dgate = tail + pltpu.roll(tail, 128 - experts, 1)
        gates = gates_ref[...]
        dl = gates * (dgate - jnp.sum(gates * dgate, axis=1, keepdims=True))
        dl_ref[...] = dl
        hi, lo = split(dl)
        dh2 = sum_ref[:, :width] + dot_t(hi, router_ref[...]) + dot_t(lo, router_ref[...])
        dh2_ref[...] = dh2
        x2 = x2_ref[...]
        scale, gain = rms(x2), rows_ref[1:2, :]
        inner = jnp.mean(gain * dh2 * x2, axis=1, keepdims=True)
        dx2 = cot_ref[...].astype(F32) + scale * gain * dh2 - x2 * scale * scale * scale * inner
        dx2_ref[...] = dx2
        da_ref[...] = dx2.astype(BF)


def leave(experts, back, to_slot, gates, router, x2, rows, cot, tile=512):
    n, width = x2.shape
    slots = back.shape[0]
    outs = [sds((n, width), F32), sds((n, width), BF), sds((n, width), F32), sds((n, 128), F32)]
    rest = [gates, router, x2, rows, cot]
    return pl.pallas_call(
        functools.partial(leave_body, experts),
        grid=(slots // tile,),
        in_specs=[
            pl.BlockSpec((tile, width + 128), lambda i: (i, 0)),
            pl.BlockSpec((n, tile), lambda i: (0, i)),
        ]
        + [whole(a.shape) for a in rest],
        out_specs=[whole(o.shape) for o in outs],
        out_shape=outs,
        scratch_shapes=[pltpu.VMEM((n, width + 128), F32)],
        compiler_params=pltpu.CompilerParams(vmem_limit_bytes=VM),
        cost_estimate=pl.CostEstimate(
            flops=2 * n * width * slots, bytes_accessed=3 * slots * width, transcendentals=0
        ),
        name="leave",
    )(back, to_slot, *rest)


def small_body(experts, h2_ref, dl_ref, dh2_ref, x2_ref, out_ref):
    hi, lo = split(dl_ref[...])
    h2, x2 = h2_ref[...], x2_ref[...]
    out_ref[...] = tdot(h2, hi) + tdot(h2, lo) + column_sum(dh2_ref[...] * x2 * rms(x2), experts)


def small_slopes(experts, h2, dl, dh2, x2):
    n, width = x2.shape
    return one_step(
        functools.partial(small_body, experts),
        "small_slopes",
        [],
        [h2, dl, dh2, x2],
        [sds((width, 128), F32)],
        [],
        8 * n * width * 128,
    )[0]


def attend_back_body(experts, place_ref, *refs):
    das, xs = refs[0:4], refs[4:8]
    wo_ref, qkv_ref, o_own, o_far, lse_own, lse_far, h1_ref, w_ref = refs[8:16]
    cos_ref, sin_ref, bias_ref, small_ref = refs[16:20]
    keep_ref, give_ref = refs[20:22]
    parts = refs[22:26]
    da, do, dqk, dqkv, o_ref, lse_ref = refs[26:32]
    core = place_ref[1]
    rows = xs[0].shape[0]
    q_w, qkv_w = o_ref.shape[1], qkv_ref.shape[1]
    kv_w = (qkv_w - q_w) // 2
    group = q_w // kv_w
    scale = HEAD ** (-0.5)
    for r in range(WS):
        da[r * rows : (r + 1) * rows, :] = das[r][...]
    o_ref[:rows, :] = o_own[...]
    o_ref[rows:, :] = o_far[...]
    lse_ref[:rows, :] = lse_own[...]
    lse_ref[rows:, :] = lse_far[...]
    do[...] = dot_t(da[...], wo_ref[...]).astype(BF)
    for n in range(kv_w // HEAD):
        at = n * HEAD
        k = qkv_ref[:, q_w + at : q_w + at + HEAD]
        v = qkv_ref[:, q_w + kv_w + at : q_w + kv_w + at + HEAD]
        dk, dv = None, None
        for h in range(n * group, (n + 1) * group):
            q = qkv_ref[:, h * HEAD : (h + 1) * HEAD]
            doh = do[:, h * HEAD : (h + 1) * HEAD]
            p = jnp.exp(dot_t(q, k) * scale + bias_ref[...] - lse_ref[:, h : h + 1])
            dp = dot_t(doh, v)
            delta = jnp.sum(p * dp, axis=1, keepdims=True)
            ds = (p * (dp - delta)).astype(BF)
            dqk[:, h * HEAD : (h + 1) * HEAD] = dot(ds, k) * scale
            more_k, more_v = tdot(ds, q), tdot(p.astype(BF), doh)
            dk = more_k if dk is None else dk + more_k
            dv = more_v if dv is None else dv + more_v
        dqk[:, q_w + at : q_w + at + HEAD] = dk * scale
        dqkv[:, q_w + kv_w + at : q_w + kv_w + at + HEAD] = dv.astype(BF)
    dqkv[:, qkv_w:] = jnp.zeros((da.shape[0], 128), BF)
    d = dqk[...]
    times = (q_w + kv_w) // 128
    d = d * wide(cos_ref, times) - other_half(d) * wide(sin_ref, times)
    dqkv[:, : q_w + kv_w] = d.astype(BF)
    small = small_ref[...]
    for r in range(WS):
        dh1 = dot_t(dqkv[r * rows : (r + 1) * rows, :qkv_w], w_ref[...])
        parts[r][...] = dh1.astype(parts[r].dtype)
        x = xs[r][:rows, :].astype(F32)
        small = small + column_sum(dh1 * x * rms(x), experts + 1)
    half = keep_ref.shape[3]
    chips, step = keep_ref.shape[0], keep_ref.shape[2]
    count = chips * step

    def put(i, first, second):
        kept = jnp.where(core == 0, first, second)
        given = jnp.where(core == 0, second, first)
        keep_ref[:, i] = kept.reshape(chips, step, half)
        give_ref[:, i] = given.reshape(chips, step, half).astype(BF)

    for i in range(WS):
        both = tdot(h1_ref[:, i * count : (i + 1) * count], dqkv[...])
        mine = small[i * count : (i + 1) * count]
        second = jnp.concatenate([both[:, half : 2 * half - 128], both[:, 2 * half - 128 :] + mine], axis=1)
        put(i, both[:, :half], second)
    slope = tdot(o_ref[...], da[...])
    for i in range(2):
        put(WS + i, slope[:, i * half : (i + 1) * half], slope[:, (2 + i) * half : (3 + i) * half])


def attend_back(experts, place, das, xs, wo, qkv, os, lses, h1, w, cos, sin, bias, small):
    rows, width = xs[0].shape
    tree = rows * WS
    q_w, qkv_w = wo.shape[0], qkv.shape[1]
    half = (qkv_w + 128) // 2
    load = (CHIPS, WS + 2, width // WS // CHIPS, half)
    outs = [sds(load, F32), sds(load, BF), sds((rows, width), F32)] + [sds((rows, width), BF)] * 3
    scratch = [
        pltpu.VMEM((tree, width), BF),
        pltpu.VMEM((tree, q_w), BF),
        pltpu.VMEM((tree, (q_w + qkv_w) // 2), F32),
        pltpu.VMEM((tree, qkv_w + 128), BF),
        pltpu.VMEM((tree, q_w), BF),
        pltpu.VMEM((tree, 128), F32),
    ]
    flops = 4 * tree * width * (qkv_w + q_w) + 10 * tree * tree * q_w
    return one_step(
        functools.partial(attend_back_body, experts),
        "attend_back",
        [place],
        [*das, *xs, wo, qkv, *os, *lses, h1, w, cos, sin, bias, small],
        outs,
        scratch,
        flops,
    )


def shards(
    tokens,
    cotangent,
    seg_lengths,
    parents,
    routes,
    norm_attn,
    w_query,
    w_key,
    w_value,
    w_out,
    norm_moe,
    w_router,
    w_gate,
    w_up,
    w_down,
):
    me = lax.axis_index("ws")
    expert = lax.axis_index("exp")
    core = expert % 2
    place = jnp.stack([me, core]).astype(jnp.int32)
    rows, width = tokens.shape
    shard = width // WS
    strip = shard // 2
    experts = 2 * CHIPS
    q_w, kv_w = HEADS // WS * HEAD, KV_HEADS // WS * HEAD
    slots = experts * CAP

    def gathered(v):
        return [v] + [from_peer(v, k) for k in (1, 2, 3)]

    norms = jnp.stack([norm_attn, norm_moe])
    pieces = pack(experts, place, tokens, w_query, w_key, w_value, w_router.T, norms)
    came = [None] + [from_peer(pieces[k], k) for k in (1, 2, 3)]
    xs = [tokens, from_peer(tokens, 1), came[2], from_peer(tokens, 3)]
    own = [pieces[0], came[1], came[2][rows:], came[3]]

    labels = jnp.arange(experts, dtype=jnp.int32)
    lane = jnp.arange(128, dtype=jnp.int32)
    chosen = jnp.any(routes[:, :, None] == lane[None, None, :], axis=1)
    row_id = jnp.arange(rows, dtype=jnp.int32)
    before = (row_id[None, :] < row_id[:, None]).astype(BF)
    rank = dot(before, chosen.astype(BF))
    col = jnp.arange(slots, dtype=jnp.int32)
    spread = (col[None, :] // CAP == lane[:, None]).astype(BF)
    spot = dot(jnp.where(chosen, rank + 1.0, 0.0).astype(BF), spread)
    to_slot = (spot == (col % CAP + 1).astype(F32)[None, :]).astype(BF)
    chosen = chosen.astype(BF)
    extra = jnp.concatenate([cotangent, chosen], axis=1)
    dy_send = tdot(to_slot, extra).astype(BF).reshape(experts, CAP, width + 128)
    dy_slots = lax.all_to_all(dy_send, "exp", 0, 0, tiled=True).reshape(slots, width + 128)

    order = (
        ((me + jnp.arange(WS, dtype=jnp.int32)) % WS)[:, None] * rows + row_id[None, :]
    ).reshape(-1)
    visible, position = tree_layout(seg_lengths[0], parents[0], order)
    bias = jnp.where(visible, 0.0, MASKED).astype(F32)
    inverse = THETA ** (-(lane % (HEAD // 2)).astype(F32) * 2.0 / HEAD)
    angles = position.astype(F32)[:, None] * inverse[None, :]
    cosines = jnp.cos(angles)
    sines = jnp.where((lane % HEAD < HEAD // 2)[None, :], -1.0, 1.0) * jnp.sin(angles)
    own[1], bias, cosines, sines = lax.optimization_barrier((own[1], bias, cosines, sines))
    twin = [pieces[WS]] + [other_core(own[k]) for k in (1, 2, 3)]
    h1, qkv, o_far, lse_far, w_qkv, small_full, gains, *parts = attend(
        experts, place, xs, own, twin, cosines, sines, bias, w_out
    )
    o_own, lse_own, part_own = attend_own(rows, qkv, bias, w_out)
    sums = [part_own] + [to_peer(parts[k - 1], k) for k in (1, 2, 3)]
    x2, h2, x_send = enter(tokens, sums, gains, to_slot)
    x_send, wg_own, wu_own, wd_own = lax.optimization_barrier(
        (x_send, w_gate[0], w_up[0], w_down[0])
    )
    x_slots = lax.all_to_all(
        x_send.reshape(experts, CAP, width), "exp", 0, 0, tiled=True
    ).reshape(slots, width)

    sel = jnp.concatenate(
        [
            (lane == expert).astype(F32)[None],
            (lane == expert + experts).astype(F32)[None],
            jnp.zeros((6, 128), F32),
        ],
        axis=0,
    )
    wd = gathered(wd_own)
    gates, gate_slots = gate_terms(h2, small_full, to_slot, chosen, spread)
    wd[1], gates, gate_slots = lax.optimization_barrier((wd[1], gates, gate_slots))
    dx_send, hidden, d_gu, slot_gates = expert_pass(
        x_slots, dy_slots, sel, small_full, gathered(wg_own), gathered(wu_own), wd, 256
    )
    dx_back = lax.all_to_all(
        dx_send.reshape(experts, CAP, width + 128), "exp", 0, 0, tiled=True
    ).reshape(slots, width + 128)

    own_g, own_u, gu1, gu2, gu3 = in_slopes(x_slots, d_gu)
    gu1, gu2, gu3 = to_peer(gu1, 1), to_peer(gu2, 2), to_peer(gu3, 3)
    hidden, gu1 = lax.optimization_barrier((hidden, gu1))
    y, own_d, dn1, dn2, dn3 = out_slopes(hidden, dy_slots, slot_gates, wd)
    dn1, dn2, dn3 = to_peer(dn1, 1), to_peer(dn2, 2), to_peer(dn3, 3)
    dx_back, y, gu1, dn1, gu2, dn2, gu3, dn3 = lax.optimization_barrier(
        (dx_back, y, gu1, dn1, gu2, dn2, gu3, dn3)
    )
    y_back = lax.all_to_all(y.reshape(experts, CAP, width), "exp", 0, 0, tiled=True).reshape(
        slots, width
    )

    dx2, d_a, dh2, dl = leave(
        experts, dx_back, to_slot, gates, small_full, x2, gains, cotangent
    )
    das = gathered(d_a)
    small_terms = small_slopes(experts, h2, dl, dh2, x2)
    grad_gu = jnp.stack([own_g, own_u]) + gu1.astype(F32) + gu2.astype(F32) + gu3.astype(F32)
    grad_wg, grad_wu = grad_gu[0][None], grad_gu[1][None]
    grad_wd = (own_d + dn1.astype(F32) + dn2.astype(F32) + dn3.astype(F32))[None]
    das, grad_wg, grad_wu, grad_wd = lax.optimization_barrier((das, grad_wg, grad_wu, grad_wd))
    keep, give, *slopes = attend_back(
        experts,
        place,
        das,
        xs,
        w_out,
        qkv,
        (o_own, o_far),
        (lse_own, lse_far),
        h1,
        w_qkv,
        cosines,
        sines,
        bias,
        small_terms,
    )
    sent = (keep + other_core(give).astype(F32)).astype(BF)
    sent, y_back = lax.optimization_barrier((sent, y_back))
    step = shard // CHIPS
    both = dot(gate_slots, y_back)
    layer_out = (x2 + both[:rows] + both[rows:]).astype(BF)
    got = same_core(sent)
    slopes = [slopes[0]] + [to_peer(slopes[k], k) for k in (1, 2, 3)]
    got, layer_out, slopes = lax.optimization_barrier((got, layer_out, slopes))
    dh1 = slopes[0]
    for k in (1, 2, 3):
        dh1 = dh1 + slopes[k].astype(F32)
    resid = tokens.astype(F32)
    scale = lax.rsqrt(jnp.mean(resid * resid, axis=-1, keepdims=True) + EPS)
    inner = jnp.mean(gains[0:1] * dh1 * resid, axis=-1, keepdims=True)
    grad_tokens = dx2 + scale * gains[0:1] * dh1 - resid * scale * scale * scale * inner

    total = jnp.sum(got.astype(F32), axis=0).astype(BF)
    final = jnp.stack(
        [lax.dynamic_index_in_dim(total, me, 0, False)]
        + [
            from_peer(lax.dynamic_index_in_dim(total, (me - k) % WS, 0, False), k)
            for k in (1, 2, 3)
        ]
        + [total[WS], total[WS + 1]]
    )
    spread_out = same_core(jnp.broadcast_to(final, (CHIPS,) + final.shape))
    twin_out = other_core(spread_out)
    sum_query, sum_key, sum_value, sum_router, sum_gains, sum_out = finish(
        experts, place, spread_out, twin_out
    )

    return (
        layer_out,
        grad_tokens,
        sum_gains[1],
        sum_query,
        sum_key,
        sum_value,
        sum_out,
        sum_gains[0],
        sum_router.T,
        grad_wg,
        grad_wu,
        grad_wd,
    )


def solution(mesh):
    rows = P(("exp", "ws"), None)
    placed = (
        rows,
        rows,
        P("exp", None),
        P("exp", None),
        rows,
        P("ws"),
        P("ws", None),
        P("ws", None),
        P("ws", None),
        P("ws", None),
        P("ws"),
        P("ws", None),
        P("exp", None, "ws"),
        P("exp", None, "ws"),
        P("exp", "ws", None),
    )
    return jax.shard_map(
        shards,
        mesh=mesh,
        in_specs=placed,
        out_specs=(
            rows,
            rows,
            P("ws"),
            P("ws", None),
            P("ws", None),
            P("ws", None),
            P("ws", None),
            P("ws"),
            P("ws", None),
            P("exp", None, "ws"),
            P("exp", None, "ws"),
            P("exp", "ws", None),
        ),
        check_vma=False,
    )
```

```python
import functools

import jax
import jax.numpy as jnp
from jax import lax
from jax.experimental import pallas as pl
from jax.experimental.pallas import tpu as pltpu
from jax.sharding import PartitionSpec as P

HEADS = 24
KV_HEADS = 8
HEAD = 64
EPS = 1e-06
THETA = 10000.0
MASKED = -1e30
BF = jnp.bfloat16
F32 = jnp.float32
WS = 4
CHIPS = 16
CAP = 48
VM = 60 * 1024 * 1024


def dot(a, b):
    return jnp.dot(a, b, preferred_element_type=F32)


def dot_t(a, b):
    return lax.dot_general(a, b, (((1,), (1,)), ((), ())), preferred_element_type=F32)


def tdot(a, b):
    return lax.dot_general(a, b, (((0,), (0,)), ((), ())), preferred_element_type=F32)


def split(v):
    hi = v.astype(BF)
    return hi, (v - hi.astype(F32)).astype(BF)


def from_peer(v, k):
    return lax.ppermute(v, "ws", [(s, (s - k) % WS) for s in range(WS)])


def to_peer(v, k):
    return lax.ppermute(v, "ws", [(s, (s + k) % WS) for s in range(WS)])


def other_core(v):
    return lax.ppermute(v, "exp", [(s, s ^ 1) for s in range(2 * CHIPS)])


def same_core(v):
    groups = [[2 * chip + core for chip in range(CHIPS)] for core in range(2)]
    return lax.all_to_all(v, "exp", 0, 0, tiled=True, axis_index_groups=groups)


def tree_layout(lengths, parents, token_index):
    seg = lengths.shape[0]
    labels = jnp.arange(seg, dtype=jnp.int32)
    segment_end = jnp.cumsum(lengths, dtype=jnp.int32)
    starts = segment_end - lengths
    segment = jnp.sum((token_index[:, None] >= segment_end[None, :]).astype(jnp.int32), axis=1)
    reach = ((parents[:, None] == labels[None, :]) | (labels[:, None] == labels[None, :])).astype(
        BF
    )
    for _ in range(4):
        reach = (dot(reach, reach) > 0.5).astype(BF)
    above = jnp.sum(reach.astype(jnp.int32) * lengths[None, :], axis=1) - lengths
    members = segment[:, None] == labels[None, :]
    position = jnp.sum(jnp.where(members, (above - starts)[None, :], 0), axis=1) + token_index
    members = members.astype(BF)
    reaches = dot(members, reach).astype(BF)
    visible = (dot_t(reaches, members) > 0.5) & (token_index[None, :] <= token_index[:, None])
    return visible, position


def expert_body(width, ff, x_ref, dy_ref, sel_ref, wr_ref, *rest):
    wg, wu, wd = rest[0:4], rest[4:8], rest[8:12]
    dx_ref, h_ref, dgu_ref, gate_ref = rest[12:16]
    wgu, wdn = rest[16:]
    part = wg[0].shape[1]

    @pl.when(pl.program_id(0) == 0)
    def _():
        for r in range(WS):
            wgu[:, r * part : (r + 1) * part] = wg[r][...]
            wgu[:, ff + r * part : ff + (r + 1) * part] = wu[r][...]
            wdn[r * part : (r + 1) * part, :] = wd[r][...]
        wgu[:, 2 * ff :] = wr_ref[...]

    pre = dot(x_ref[...], wgu[...])
    g, u, logits = pre[:, :ff], pre[:, ff : 2 * ff], pre[:, 2 * ff :]
    mask = dy_ref[:, width:].astype(F32) > 0.5
    logits = jnp.where(mask, logits, MASKED)
    lifted = jnp.where(mask, jnp.exp(logits - jnp.max(logits, axis=1, keepdims=True)), 0.0)
    total = jnp.maximum(jnp.sum(lifted, axis=1, keepdims=True), 1e-30)
    gate = jnp.sum(lifted * sel_ref[0:1, :], axis=1, keepdims=True) / total
    gate_ref[...] = jnp.broadcast_to(gate, gate_ref.shape)
    sig = 1.0 / (1.0 + jnp.exp(-g))
    silu = g * sig
    h = (silu * u).astype(BF)
    h_ref[...] = h
    raw = dot_t(dy_ref[:, :width], wdn[...])
    dgate = jnp.sum(raw * h.astype(F32), axis=1, keepdims=True)
    dh = raw * gate
    dgu_ref[:, :ff] = (dh * u * sig * (1.0 + g * (1.0 - sig))).astype(BF)
    dgu_ref[:, ff:] = (dh * silu).astype(BF)
    dx_ref[:, :width] = dot_t(dgu_ref[...], wgu[:, : 2 * ff]).astype(BF)
    hi = dgate.astype(BF).astype(F32)
    dx_ref[:, width:] = (hi * sel_ref[0:1, :] + (dgate - hi) * sel_ref[1:2, :]).astype(BF)


def expert_pass(x, dy, sel, wr, wg, wu, wd, tile):
    slots, width = x.shape
    part = wg[0].shape[1]
    ff = WS * part
    row = lambda w: pl.BlockSpec((tile, w), lambda i: (i, 0))
    once = lambda a: pl.BlockSpec(a.shape, lambda i: (0, 0))
    return pl.pallas_call(
        functools.partial(expert_body, width, ff),
        grid=(slots // tile,),
        in_specs=[row(width), row(width + 128), once(sel), once(wr)]
        + [once(a) for a in (*wg, *wu, *wd)],
        out_specs=[row(width + 128), row(ff), row(2 * ff), row(128)],
        out_shape=[
            jax.ShapeDtypeStruct((slots, width + 128), BF),
            jax.ShapeDtypeStruct((slots, ff), BF),
            jax.ShapeDtypeStruct((slots, 2 * ff), BF),
            jax.ShapeDtypeStruct((slots, 128), F32),
        ],
        scratch_shapes=[pltpu.VMEM((width, 2 * ff + 128), BF), pltpu.VMEM((ff, width), BF)],
        compiler_params=pltpu.CompilerParams(vmem_limit_bytes=VM),
        cost_estimate=pl.CostEstimate(
            flops=10 * slots * width * ff, bytes_accessed=9 * slots * width, transcendentals=0
        ),
        name="expert_pass",
    )(x, dy, sel, wr, *wg, *wu, *wd)


def in_slope_body(x_ref, dgu_ref, own_g, own_u, *peers):
    part = own_g.shape[1]
    ff = WS * part
    gu = tdot(x_ref[...], dgu_ref[...])
    own_g[...] = gu[:, :part]
    own_u[...] = gu[:, ff : ff + part]
    for k in (1, 2, 3):
        peers[k - 1][0] = gu[:, k * part : (k + 1) * part].astype(BF)
        peers[k - 1][1] = gu[:, ff + k * part : ff + (k + 1) * part].astype(BF)


def in_slopes(x, dgu, tile=256):
    slots, width = x.shape
    part = dgu.shape[1] // (2 * WS)
    tall = pl.BlockSpec((tile, part), lambda i: (i, 0))
    pair = pl.BlockSpec((2, tile, part), lambda i: (0, i, 0))
    return pl.pallas_call(
        in_slope_body,
        grid=(width // tile,),
        in_specs=[pl.BlockSpec((slots, tile), lambda i: (0, i)), whole(dgu.shape)],
        out_specs=[tall, tall] + [pair] * 3,
        out_shape=[sds((width, part), F32)] * 2 + [sds((2, width, part), BF)] * 3,
        compiler_params=pltpu.CompilerParams(vmem_limit_bytes=VM),
        cost_estimate=pl.CostEstimate(
            flops=2 * slots * width * dgu.shape[1],
            bytes_accessed=4 * slots * width,
            transcendentals=0,
        ),
        name="in_slopes",
    )(x, dgu)


def out_slope_body(h_ref, dy_ref, gate_ref, *refs):
    wd = refs[0:4]
    y_ref, own_d = refs[4:6]
    part = own_d.shape[0]
    d_y = (gate_ref[:, 0:1] * dy_ref[...].astype(F32)).astype(BF)
    dn = tdot(h_ref[...], d_y)
    own_d[...] = dn[:part]
    for k in (1, 2, 3):
        refs[5 + k][...] = dn[k * part : (k + 1) * part].astype(BF)
    y_ref[...] = dot(h_ref[...], jnp.concatenate([w[...] for w in wd], axis=0)).astype(BF)


def out_slopes(h, dy, gate, wd, tile=256):
    slots, ff = h.shape
    width = wd[0].shape[1]
    part = ff // WS
    col = pl.BlockSpec((slots, tile), lambda i: (0, i))
    flat = pl.BlockSpec((part, tile), lambda i: (0, i))
    return pl.pallas_call(
        out_slope_body,
        grid=(width // tile,),
        in_specs=[whole(h.shape), col, whole(gate.shape)] + [flat] * WS,
        out_specs=[col, flat] + [flat] * 3,
        out_shape=[sds((slots, width), BF), sds((part, width), F32)]
        + [sds((part, width), BF)] * 3,
        compiler_params=pltpu.CompilerParams(vmem_limit_bytes=VM),
        cost_estimate=pl.CostEstimate(
            flops=4 * slots * width * ff, bytes_accessed=4 * slots * width, transcendentals=0
        ),
        name="out_slopes",
    )(h, dy, gate, *wd)


def finish_body(experts, place_ref, a_ref, b_ref, ao_ref, bo_ref, *refs):
    q_ref, k_ref, v_ref, r_ref, g_ref, o_ref, s_ref = refs
    turn = pl.program_id(0)
    second = place_ref[1] == 1
    rows = q_ref.shape[0]
    half = a_ref.shape[3]
    kv = k_ref.shape[1]
    mine = a_ref[:, 0].astype(F32).reshape(rows, half)
    twin = b_ref[:, 0].astype(F32).reshape(rows, half)
    q_ref[...] = jnp.where(second, twin, mine)
    rest = jnp.where(second, mine, twin)
    k_ref[...] = rest[:, :kv]
    v_ref[...] = rest[:, kv : 2 * kv]

    @pl.when(turn == 0)
    def _():
        s_ref[...] = rest[:, 2 * kv :]

    @pl.when(turn > 0)
    def _():
        s_ref[...] += rest[:, 2 * kv :]

    @pl.when(turn == WS - 1)
    def _():
        turned = s_ref[...].T
        r_ref[...] = turned[:experts]
        g_ref[...] = turned[experts : experts + 8]

    mine = ao_ref[:, 0].astype(F32).reshape(rows, half)
    twin = bo_ref[:, 0].astype(F32).reshape(rows, half)
    o_ref[...] = jnp.where(second == (turn < 2), twin, mine)


def finish(experts, place, mine, twin):
    chips, sets, step, half = mine.shape
    rows = chips * step
    first = pl.BlockSpec((chips, 1, step, half), lambda i, p: (0, i, 0, 0))
    later = pl.BlockSpec((chips, 1, step, half), lambda i, p: (0, WS + i % 2, 0, 0))
    turned = lambda i, p: (0, lax.rem(p[0] + i, WS))
    kv = (half - 128) // 2
    S = jax.ShapeDtypeStruct
    return pl.pallas_call(
        functools.partial(finish_body, experts),
        grid_spec=pltpu.PrefetchScalarGridSpec(
            num_scalar_prefetch=1,
            grid=(WS,),
            in_specs=[first, first, later, later],
            out_specs=[
                pl.BlockSpec((rows, half), turned),
                pl.BlockSpec((rows, kv), turned),
                pl.BlockSpec((rows, kv), turned),
                whole((experts, rows)),
                whole((8, rows)),
                pl.BlockSpec((rows, half), lambda i, p: (0, i)),
            ],
            scratch_shapes=[pltpu.VMEM((rows, 128), F32)],
        ),
        out_shape=[
            S((rows, WS * half), F32),
            S((rows, WS * kv), F32),
            S((rows, WS * kv), F32),
            S((experts, rows), F32),
            S((8, rows), F32),
            S((rows, WS * half), F32),
        ],
        compiler_params=pltpu.CompilerParams(vmem_limit_bytes=VM),
        cost_estimate=pl.CostEstimate(flops=0, bytes_accessed=16 * rows * WS * half, transcendentals=0),
        name="finish",
    )(place, mine, twin, mine, twin)


def whole(shape):
    return pl.BlockSpec(shape, lambda *_: (0,) * len(shape))


def sds(shape, kind):
    return jax.ShapeDtypeStruct(shape, kind)


def one_step(body, name, scalars, arrays, outs, scratch, flops):
    moved = sum(a.size * a.dtype.itemsize for a in arrays)
    return pl.pallas_call(
        body,
        in_specs=[pl.BlockSpec(memory_space=pltpu.SMEM)] * len(scalars)
        + [pl.BlockSpec(memory_space=pltpu.VMEM)] * len(arrays),
        out_specs=[pl.BlockSpec(memory_space=pltpu.VMEM)] * len(outs),
        out_shape=outs,
        scratch_shapes=scratch,
        compiler_params=pltpu.CompilerParams(vmem_limit_bytes=VM),
        cost_estimate=pl.CostEstimate(flops=flops, bytes_accessed=moved, transcendentals=0),
        name=name,
    )(*scalars, *arrays)


def other_half(v):
    lanes = v.shape[1]
    low = lax.broadcasted_iota(jnp.int32, v.shape, 1) % HEAD < HEAD // 2
    ahead = pltpu.roll(v, lanes - HEAD // 2, 1)
    behind = pltpu.roll(v, HEAD // 2, 1)
    return jnp.where(low, ahead, behind)


def wide(ref, times):
    return jnp.concatenate([ref[...]] * times, axis=1)


def rms(x):
    return lax.rsqrt(jnp.mean(x * x, axis=1, keepdims=True) + EPS)


def column_sum(m, lane):
    hi, lo = split(m)
    pick = (lax.broadcasted_iota(jnp.int32, (m.shape[0], 128), 1) == lane).astype(F32).astype(BF)
    return tdot(hi, pick) + tdot(lo, pick)


def pack_body(experts, place_ref, x_ref, wq, wk, wv, wr, norms, *outs):
    small = outs[WS + 1]
    me, core = place_ref[0], place_ref[1]
    rows = x_ref.shape[0]
    strip = wq.shape[0] // 2
    q_w, kv_w = wq.shape[1] // WS, wk.shape[1] // WS
    shard = wq.shape[0]
    few = [wr[...].astype(F32), norms[...].astype(F32), jnp.zeros((126 - experts, shard), F32)]
    small[...] = jnp.concatenate(few, axis=0).T.astype(BF)

    def place(out, top, left, side, d, start, count):
        part = pl.ds(pl.multiple_of(side * strip + start, 32), count)
        here = slice(top, top + count)
        spot = pl.ds(pl.multiple_of(d * kv_w, 128), kv_w)
        out[here, left : left + q_w] = wq[part, pl.ds(pl.multiple_of(d * q_w, 128), q_w)]
        out[here, left + q_w : left + q_w + kv_w] = wk[part, spot]
        out[here, left + q_w + kv_w : left + q_w + 2 * kv_w] = wv[part, spot]
        out[here, left + q_w + 2 * kv_w : left + q_w + 2 * kv_w + 128] = small[part, :]

    for r in range(WS + 1):
        side = core if r < WS else 1 - core
        d = lax.rem(me + WS - r % WS, WS)
        if r == 2:
            outs[r][:rows, :] = x_ref[...]
            for half in range(2):
                left = half * (q_w + 2 * kv_w + 128)
                place(outs[r], rows, left, side, d, half * strip // 2, strip // 2)
        else:
            place(outs[r], 0, 0, side, d, 0, strip)


def pack(experts, place, x, wq, wk, wv, wr, norms):
    shard = wq.shape[0]
    rows, width = x.shape
    wide_w = (wq.shape[1] + 2 * wk.shape[1]) // WS + 128
    outs = [sds((shard // 2, wide_w), BF)] * (WS + 1)
    outs[2] = sds((rows + shard // 4, 2 * wide_w), BF)
    return one_step(
        functools.partial(pack_body, experts),
        "pack",
        [place],
        [x, wq, wk, wv, wr, norms],
        outs,
        [pltpu.VMEM((shard, 128), BF)],
        0,
    )


def dispatch_body(experts, routes_ref, cot_ref, send_ref, slot_ref, chosen_ref, spread_ref):
    rows, width = cot_ref.shape
    slots = slot_ref.shape[1]
    tile = send_ref.shape[0]
    step = pl.program_id(0)

    @pl.when(step == 0)
    def _():
        name = lax.broadcasted_iota(jnp.int32, (128, rows), 0)
        named = jnp.zeros((128, rows), F32)
        for k in range(routes_ref.shape[0]):
            named = named + (routes_ref[k : k + 1, :] == name).astype(F32)
        chosen = named.T
        chosen_ref[...] = chosen.astype(BF)
        this = lax.broadcasted_iota(jnp.int32, (rows, rows), 0)
        that = lax.broadcasted_iota(jnp.int32, (rows, rows), 1)
        rank = dot((that < this).astype(F32).astype(BF), chosen.astype(BF))
        col = lax.broadcasted_iota(jnp.int32, (128, slots), 1)
        first = lax.broadcasted_iota(jnp.int32, (128, slots), 0) * CAP
        spread = jnp.where((col >= first) & (col < first + CAP), 1.0, 0.0)
        spread_ref[...] = spread.astype(BF)
        spot = dot((chosen * (rank + 1.0)).astype(BF), spread.astype(BF))
        want = jnp.sum(spread * (col - first + 1).astype(F32), axis=0, keepdims=True)
        slot_ref[...] = jnp.where(spot == want, 1.0, 0.0).astype(BF)

    part = slot_ref[:, pl.ds(pl.multiple_of(step * tile, tile), tile)]
    send_ref[:, :width] = tdot(part, cot_ref[...]).astype(BF)
    send_ref[:, width:] = tdot(part, chosen_ref[...]).astype(BF)


def dispatch(experts, routes, cot, tile=512):
    rows, width = cot.shape
    slots = experts * CAP
    outs = [
        sds((slots, width + 128), BF),
        sds((rows, slots), BF),
        sds((rows, 128), BF),
        sds((128, slots), BF),
    ]
    return pl.pallas_call(
        functools.partial(dispatch_body, experts),
        grid=(slots // tile,),
        in_specs=[whole((routes.shape[1], rows)), whole((rows, width))],
        out_specs=[pl.BlockSpec((tile, width + 128), lambda i: (i, 0))]
        + [whole(o.shape) for o in outs[1:]],
        out_shape=outs,
        compiler_params=pltpu.CompilerParams(vmem_limit_bytes=VM),
        cost_estimate=pl.CostEstimate(
            flops=2 * rows * width * slots, bytes_accessed=3 * slots * width, transcendentals=0
        ),
        name="dispatch",
    )(routes.T, cot)


def attend_rows(qkv_ref, bias_ref, o_ref, lse_ref, start, q_w, kv_w):
    rows = o_ref.shape[0]
    group = q_w // kv_w
    here = slice(start, start + rows)
    for h in range(q_w // HEAD):
        at = h // group * HEAD
        q = qkv_ref[here, h * HEAD : (h + 1) * HEAD]
        k = qkv_ref[:, q_w + at : q_w + at + HEAD]
        v = qkv_ref[:, q_w + kv_w + at : q_w + kv_w + at + HEAD]
        s = dot_t(q, k) * HEAD ** (-0.5) + bias_ref[here, :]
        peak = jnp.max(s, axis=1, keepdims=True)
        p = jnp.exp(s - peak)
        total = jnp.sum(p, axis=1, keepdims=True)
        lse_ref[:, h : h + 1] = peak + jnp.log(total)
        o_ref[:, h * HEAD : (h + 1) * HEAD] = dot((p / total).astype(BF), v).astype(BF)


def attend_body(experts, place_ref, *refs):
    xs, own, twin = refs[0:4], refs[4:8], refs[8:12]
    cos_ref, sin_ref, bias_ref, wo_ref = refs[12:16]
    h1_ref, qkv_ref, o_ref, lse_ref, w_ref, small_ref, rows_ref = refs[16:23]
    parts = refs[23:26]
    me, core = place_ref[0], place_ref[1]
    rows = xs[0].shape[0]
    strip = own[0].shape[0]
    wide_w = own[0].shape[1]
    q_w = o_ref.shape[1]
    qkv_w = qkv_ref.shape[1]
    kv_w = (qkv_w - q_w) // 2
    for r in range(WS):
        base = lax.rem(me + r, WS) * (2 * strip)
        for source, side in ((own[r], core), (twin[r], 1 - core)):
            folds = source.shape[1] // wide_w
            count = strip // folds
            for f in range(folds):
                left = f * wide_w
                spot = pl.ds(pl.multiple_of(base + side * strip + f * count, 32), count)
                w_ref[spot, :] = source[:, left : left + qkv_w]
                small_ref[spot, :] = source[:, left + qkv_w : left + wide_w]
    turned = small_ref[...].astype(F32).T
    rows_ref[...] = jnp.concatenate(
        [turned[experts : experts + 2], jnp.zeros((6, turned.shape[1]), F32)], axis=0
    )
    gain = turned[experts : experts + 1]
    for r in range(WS):
        x = xs[r][:rows, :].astype(F32)
        h1_ref[r * rows : (r + 1) * rows, :] = (x * rms(x) * gain).astype(BF)
    qkv = dot(h1_ref[...], w_ref[...])
    qk = qkv[:, : q_w + kv_w]
    times = (q_w + kv_w) // 128
    qk = qk * wide(cos_ref, times) + other_half(qk) * wide(sin_ref, times)
    qkv_ref[:, : q_w + kv_w] = qk.astype(BF)
    qkv_ref[:, q_w + kv_w :] = qkv[:, q_w + kv_w :].astype(BF)
    attend_rows(qkv_ref, bias_ref, o_ref, lse_ref, rows, q_w, kv_w)
    for r in range(3):
        part = dot(o_ref[r * rows : (r + 1) * rows, :], wo_ref[...])
        parts[r][...] = part.astype(BF)


def attend(experts, place, xs, own, twin, cos, sin, bias, wo):
    rows, width = xs[0].shape
    tree = rows * WS
    q_w, qkv_w = wo.shape[0], own[0].shape[1] - 128
    outs = [
        sds((tree, width), BF),
        sds((tree, qkv_w), BF),
        sds((tree - rows, q_w), BF),
        sds((tree - rows, 128), F32),
        sds((width, qkv_w), BF),
        sds((width, 128), BF),
        sds((8, width), F32),
    ] + [sds((rows, width), BF)] * 3
    flops = 40 * tree * width * (qkv_w + q_w)
    return one_step(
        functools.partial(attend_body, experts),
        "attend",
        [place],
        [*xs, *own, *twin, cos, sin, bias, wo],
        outs,
        [],
        flops,
    )


def attend_own_body(qkv_ref, bias_ref, wo_ref, o_ref, lse_ref, part_ref):
    q_w = o_ref.shape[1]
    kv_w = (qkv_ref.shape[1] - q_w) // 2
    attend_rows(qkv_ref, bias_ref, o_ref, lse_ref, 0, q_w, kv_w)
    part_ref[...] = dot(o_ref[...], wo_ref[...])


def attend_own(rows, qkv, bias, wo):
    q_w, width = wo.shape
    outs = [sds((rows, q_w), BF), sds((rows, 128), F32), sds((rows, width), F32)]
    flops = 2 * rows * width * q_w + 4 * rows * qkv.shape[0] * q_w
    return one_step(attend_own_body, "attend_own", [], [qkv, bias, wo], outs, [], flops)


def enter_body(x_ref, p0, p1, p2, p3, rows_ref, slot_ref, x2_ref, h2_ref, send_ref):
    @pl.when(pl.program_id(0) == 0)
    def _():
        x2 = x_ref[...].astype(F32) + p0[...]
        for p in (p1, p2, p3):
            x2 = x2 + p[...].astype(F32)
        x2_ref[...] = x2
        h2_ref[...] = (x2 * rms(x2) * rows_ref[1:2, :]).astype(BF)

    send_ref[...] = tdot(slot_ref[...], h2_ref[...]).astype(BF)


def enter(x, parts, rows, to_slot, tile=512):
    n, width = x.shape
    slots = to_slot.shape[1]
    arrays = [x, *parts, rows]
    return pl.pallas_call(
        enter_body,
        grid=(slots // tile,),
        in_specs=[whole(a.shape) for a in arrays] + [pl.BlockSpec((n, tile), lambda i: (0, i))],
        out_specs=[
            whole((n, width)),
            whole((n, width)),
            pl.BlockSpec((tile, width), lambda i: (i, 0)),
        ],
        out_shape=[sds((n, width), F32), sds((n, width), BF), sds((slots, width), BF)],
        compiler_params=pltpu.CompilerParams(vmem_limit_bytes=VM),
        cost_estimate=pl.CostEstimate(
            flops=2 * n * width * slots, bytes_accessed=3 * slots * width, transcendentals=0
        ),
        name="enter",
    )(*arrays, to_slot)


def gate_body(h2_ref, router_ref, slot_ref, chosen_ref, spread_ref, gates_ref, gs_ref):
    logits = dot(h2_ref[...], router_ref[...])
    mask = chosen_ref[...].astype(F32) > 0.5
    logits = jnp.where(mask, logits, MASKED)
    lifted = jnp.where(mask, jnp.exp(logits - jnp.max(logits, axis=1, keepdims=True)), 0.0)
    gates = lifted / jnp.maximum(jnp.sum(lifted, axis=1, keepdims=True), 1e-30)
    gates_ref[...] = gates
    hi, lo = split(gates)
    on_slots = dot(hi, spread_ref[...]) + dot(lo, spread_ref[...])
    hi, lo = split(on_slots * slot_ref[...].astype(F32))
    rows = gates.shape[0]
    gs_ref[:rows, :] = hi
    gs_ref[rows:, :] = lo


def gate_terms(h2, router, to_slot, chosen, spread):
    n, slots = to_slot.shape
    outs = [sds((n, 128), F32), sds((2 * n, slots), BF)]
    arrays = [h2, router, to_slot, chosen, spread]
    return one_step(gate_body, "gate_terms", [], arrays, outs, [], 8 * n * 128 * slots)


def leave_body(experts, back_ref, slot_ref, gates_ref, router_ref, x2_ref, rows_ref, cot_ref, *outs):
    dx2_ref, da_ref, dh2_ref, dl_ref, sum_ref = outs
    width = x2_ref.shape[1]
    step = pl.program_id(0)
    more = dot(slot_ref[...], back_ref[...])

    @pl.when(step == 0)
    def _():
        sum_ref[...] = more

    @pl.when(step > 0)
    def _():
        sum_ref[...] += more

    @pl.when(step == pl.num_programs(0) - 1)
    def _():
        tail = sum_ref[:, width:]
        dgate = tail + pltpu.roll(tail, 128 - experts, 1)
        gates = gates_ref[...]
        dl = gates * (dgate - jnp.sum(gates * dgate, axis=1, keepdims=True))
        dl_ref[...] = dl
        hi, lo = split(dl)
        dh2 = sum_ref[:, :width] + dot_t(hi, router_ref[...]) + dot_t(lo, router_ref[...])
        dh2_ref[...] = dh2
        x2 = x2_ref[...]
        scale, gain = rms(x2), rows_ref[1:2, :]
        inner = jnp.mean(gain * dh2 * x2, axis=1, keepdims=True)
        dx2 = cot_ref[...].astype(F32) + scale * gain * dh2 - x2 * scale * scale * scale * inner
        dx2_ref[...] = dx2
        da_ref[...] = dx2.astype(BF)


def leave(experts, back, to_slot, gates, router, x2, rows, cot, tile=512):
    n, width = x2.shape
    slots = back.shape[0]
    outs = [sds((n, width), F32), sds((n, width), BF), sds((n, width), F32), sds((n, 128), F32)]
    rest = [gates, router, x2, rows, cot]
    return pl.pallas_call(
        functools.partial(leave_body, experts),
        grid=(slots // tile,),
        in_specs=[
            pl.BlockSpec((tile, width + 128), lambda i: (i, 0)),
            pl.BlockSpec((n, tile), lambda i: (0, i)),
        ]
        + [whole(a.shape) for a in rest],
        out_specs=[whole(o.shape) for o in outs],
        out_shape=outs,
        scratch_shapes=[pltpu.VMEM((n, width + 128), F32)],
        compiler_params=pltpu.CompilerParams(vmem_limit_bytes=VM),
        cost_estimate=pl.CostEstimate(
            flops=2 * n * width * slots, bytes_accessed=3 * slots * width, transcendentals=0
        ),
        name="leave",
    )(back, to_slot, *rest)


def small_body(experts, h2_ref, dl_ref, dh2_ref, x2_ref, out_ref):
    hi, lo = split(dl_ref[...])
    h2, x2 = h2_ref[...], x2_ref[...]
    out_ref[...] = tdot(h2, hi) + tdot(h2, lo) + column_sum(dh2_ref[...] * x2 * rms(x2), experts)


def small_slopes(experts, h2, dl, dh2, x2):
    n, width = x2.shape
    return one_step(
        functools.partial(small_body, experts),
        "small_slopes",
        [],
        [h2, dl, dh2, x2],
        [sds((width, 128), F32)],
        [],
        8 * n * width * 128,
    )[0]


def attend_back_body(experts, place_ref, *refs):
    das, xs = refs[0:4], refs[4:8]
    wo_ref, qkv_ref, o_own, o_far, lse_own, lse_far, h1_ref, w_ref = refs[8:16]
    cos_ref, sin_ref, bias_ref, small_ref = refs[16:20]
    keep_ref, give_ref = refs[20:22]
    parts = refs[22:26]
    da, do, dqk, dqkv, o_ref, lse_ref = refs[26:32]
    core = place_ref[1]
    rows = xs[0].shape[0]
    q_w, qkv_w = o_ref.shape[1], qkv_ref.shape[1]
    kv_w = (qkv_w - q_w) // 2
    group = q_w // kv_w
    scale = HEAD ** (-0.5)
    for r in range(WS):
        da[r * rows : (r + 1) * rows, :] = das[r][...]
    o_ref[:rows, :] = o_own[...]
    o_ref[rows:, :] = o_far[...]
    lse_ref[:rows, :] = lse_own[...]
    lse_ref[rows:, :] = lse_far[...]
    do[...] = dot_t(da[...], wo_ref[...]).astype(BF)
    for n in range(kv_w // HEAD):
        at = n * HEAD
        k = qkv_ref[:, q_w + at : q_w + at + HEAD]
        v = qkv_ref[:, q_w + kv_w + at : q_w + kv_w + at + HEAD]
        dk, dv = None, None
        for h in range(n * group, (n + 1) * group):
            q = qkv_ref[:, h * HEAD : (h + 1) * HEAD]
            doh = do[:, h * HEAD : (h + 1) * HEAD]
            p = jnp.exp(dot_t(q, k) * scale + bias_ref[...] - lse_ref[:, h : h + 1])
            dp = dot_t(doh, v)
            delta = jnp.sum(p * dp, axis=1, keepdims=True)
            ds = (p * (dp - delta)).astype(BF)
            dqk[:, h * HEAD : (h + 1) * HEAD] = dot(ds, k) * scale
            more_k, more_v = tdot(ds, q), tdot(p.astype(BF), doh)
            dk = more_k if dk is None else dk + more_k
            dv = more_v if dv is None else dv + more_v
        dqk[:, q_w + at : q_w + at + HEAD] = dk * scale
        dqkv[:, q_w + kv_w + at : q_w + kv_w + at + HEAD] = dv.astype(BF)
    dqkv[:, qkv_w:] = jnp.zeros((da.shape[0], 128), BF)
    d = dqk[...]
    times = (q_w + kv_w) // 128
    d = d * wide(cos_ref, times) - other_half(d) * wide(sin_ref, times)
    dqkv[:, : q_w + kv_w] = d.astype(BF)
    small = small_ref[...]
    for r in range(WS):
        dh1 = dot_t(dqkv[r * rows : (r + 1) * rows, :qkv_w], w_ref[...])
        parts[r][...] = dh1.astype(parts[r].dtype)
        x = xs[r][:rows, :].astype(F32)
        small = small + column_sum(dh1 * x * rms(x), experts + 1)
    half = keep_ref.shape[3]
    chips, step = keep_ref.shape[0], keep_ref.shape[2]
    count = chips * step

    def put(i, first, second):
        kept = jnp.where(core == 0, first, second)
        given = jnp.where(core == 0, second, first)
        keep_ref[:, i] = kept.reshape(chips, step, half)
        give_ref[:, i] = given.reshape(chips, step, half).astype(BF)

    for i in range(WS):
        both = tdot(h1_ref[:, i * count : (i + 1) * count], dqkv[...])
        mine = small[i * count : (i + 1) * count]
        second = jnp.concatenate([both[:, half : 2 * half - 128], both[:, 2 * half - 128 :] + mine], axis=1)
        put(i, both[:, :half], second)
    slope = tdot(o_ref[...], da[...])
    for i in range(2):
        put(WS + i, slope[:, i * half : (i + 1) * half], slope[:, (2 + i) * half : (3 + i) * half])


def attend_back(experts, place, das, xs, wo, qkv, os, lses, h1, w, cos, sin, bias, small):
    rows, width = xs[0].shape
    tree = rows * WS
    q_w, qkv_w = wo.shape[0], qkv.shape[1]
    half = (qkv_w + 128) // 2
    load = (CHIPS, WS + 2, width // WS // CHIPS, half)
    outs = [sds(load, F32), sds(load, BF), sds((rows, width), F32)] + [sds((rows, width), BF)] * 3
    scratch = [
        pltpu.VMEM((tree, width), BF),
        pltpu.VMEM((tree, q_w), BF),
        pltpu.VMEM((tree, (q_w + qkv_w) // 2), F32),
        pltpu.VMEM((tree, qkv_w + 128), BF),
        pltpu.VMEM((tree, q_w), BF),
        pltpu.VMEM((tree, 128), F32),
    ]
    flops = 4 * tree * width * (qkv_w + q_w) + 10 * tree * tree * q_w
    return one_step(
        functools.partial(attend_back_body, experts),
        "attend_back",
        [place],
        [*das, *xs, wo, qkv, *os, *lses, h1, w, cos, sin, bias, small],
        outs,
        scratch,
        flops,
    )


def shards(
    tokens,
    cotangent,
    seg_lengths,
    parents,
    routes,
    norm_attn,
    w_query,
    w_key,
    w_value,
    w_out,
    norm_moe,
    w_router,
    w_gate,
    w_up,
    w_down,
):
    me = lax.axis_index("ws")
    expert = lax.axis_index("exp")
    core = expert % 2
    place = jnp.stack([me, core]).astype(jnp.int32)
    rows, width = tokens.shape
    shard = width // WS
    strip = shard // 2
    experts = 2 * CHIPS
    q_w, kv_w = HEADS // WS * HEAD, KV_HEADS // WS * HEAD
    slots = experts * CAP

    def gathered(v):
        return [v] + [from_peer(v, k) for k in (1, 2, 3)]

    norms = jnp.stack([norm_attn, norm_moe])
    pieces = pack(experts, place, tokens, w_query, w_key, w_value, w_router.T, norms)
    came = [None] + [from_peer(pieces[k], k) for k in (1, 2, 3)]
    mine, came[1] = lax.optimization_barrier((tokens, came[1]))
    xs = [tokens, from_peer(mine, 1), came[2], from_peer(mine, 3)]
    own = [pieces[0], came[1], came[2][rows:], came[3]]

    lane = jnp.arange(128, dtype=jnp.int32)
    row_id = jnp.arange(rows, dtype=jnp.int32)
    dy_send, to_slot, chosen, spread = dispatch(experts, routes, cotangent)
    dy_send = dy_send.reshape(experts, CAP, width + 128)
    dy_slots = lax.all_to_all(dy_send, "exp", 0, 0, tiled=True).reshape(slots, width + 128)

    order = (
        ((me + jnp.arange(WS, dtype=jnp.int32)) % WS)[:, None] * rows + row_id[None, :]
    ).reshape(-1)
    visible, position = tree_layout(seg_lengths[0], parents[0], order)
    bias = jnp.where(visible, 0.0, MASKED).astype(F32)
    inverse = THETA ** (-(lane % (HEAD // 2)).astype(F32) * 2.0 / HEAD)
    angles = position.astype(F32)[:, None] * inverse[None, :]
    cosines = jnp.cos(angles)
    sines = jnp.where((lane % HEAD < HEAD // 2)[None, :], -1.0, 1.0) * jnp.sin(angles)
    own[1], bias, cosines, sines = lax.optimization_barrier((own[1], bias, cosines, sines))
    twin = [pieces[WS]] + [other_core(own[k]) for k in (1, 2, 3)]
    h1, qkv, o_far, lse_far, w_qkv, small_full, gains, *parts = attend(
        experts, place, xs, own, twin, cosines, sines, bias, w_out
    )
    o_own, lse_own, part_own = attend_own(rows, qkv, bias, w_out)
    sums = [part_own] + [to_peer(parts[k - 1], k) for k in (1, 2, 3)]
    x2, h2, x_send = enter(tokens, sums, gains, to_slot)
    x_send, wg_own, wu_own, wd_own = lax.optimization_barrier(
        (x_send, w_gate[0], w_up[0], w_down[0])
    )
    x_slots = lax.all_to_all(
        x_send.reshape(experts, CAP, width), "exp", 0, 0, tiled=True
    ).reshape(slots, width)

    sel = jnp.concatenate(
        [
            (lane == expert).astype(F32)[None],
            (lane == expert + experts).astype(F32)[None],
            jnp.zeros((6, 128), F32),
        ],
        axis=0,
    )
    wd = gathered(wd_own)
    gates, gate_slots = gate_terms(h2, small_full, to_slot, chosen, spread)
    wd[1], gates, gate_slots = lax.optimization_barrier((wd[1], gates, gate_slots))
    dx_send, hidden, d_gu, slot_gates = expert_pass(
        x_slots, dy_slots, sel, small_full, gathered(wg_own), gathered(wu_own), wd, 256
    )
    dx_back = lax.all_to_all(
        dx_send.reshape(experts, CAP, width + 128), "exp", 0, 0, tiled=True
    ).reshape(slots, width + 128)

    own_g, own_u, gu1, gu2, gu3 = in_slopes(x_slots, d_gu)
    gu1, gu2, gu3 = to_peer(gu1, 1), to_peer(gu2, 2), to_peer(gu3, 3)
    hidden, gu1 = lax.optimization_barrier((hidden, gu1))
    y, own_d, dn1, dn2, dn3 = out_slopes(hidden, dy_slots, slot_gates, wd)
    dn1, dn2, dn3 = to_peer(dn1, 1), to_peer(dn2, 2), to_peer(dn3, 3)
    dx_back, y, gu1, dn1, gu2, dn2, gu3, dn3 = lax.optimization_barrier(
        (dx_back, y, gu1, dn1, gu2, dn2, gu3, dn3)
    )
    y_back = lax.all_to_all(y.reshape(experts, CAP, width), "exp", 0, 0, tiled=True).reshape(
        slots, width
    )

    dx2, d_a, dh2, dl = leave(
        experts, dx_back, to_slot, gates, small_full, x2, gains, cotangent
    )
    das = gathered(d_a)
    small_terms = small_slopes(experts, h2, dl, dh2, x2)
    grad_gu = jnp.stack([own_g, own_u]) + gu1.astype(F32) + gu2.astype(F32) + gu3.astype(F32)
    grad_wg, grad_wu = grad_gu[0][None], grad_gu[1][None]
    grad_wd = (own_d + dn1.astype(F32) + dn2.astype(F32) + dn3.astype(F32))[None]
    das, grad_wg, grad_wu, grad_wd = lax.optimization_barrier((das, grad_wg, grad_wu, grad_wd))
    keep, give, *slopes = attend_back(
        experts,
        place,
        das,
        xs,
        w_out,
        qkv,
        (o_own, o_far),
        (lse_own, lse_far),
        h1,
        w_qkv,
        cosines,
        sines,
        bias,
        small_terms,
    )
    sent = (keep + other_core(give).astype(F32)).astype(BF)
    sent, y_back = lax.optimization_barrier((sent, y_back))
    step = shard // CHIPS
    both = dot(gate_slots, y_back)
    layer_out = (x2 + both[:rows] + both[rows:]).astype(BF)
    got = same_core(sent)
    slopes = [slopes[0]] + [to_peer(slopes[k], k) for k in (1, 2, 3)]
    got, layer_out, slopes = lax.optimization_barrier((got, layer_out, slopes))
    dh1 = slopes[0]
    for k in (1, 2, 3):
        dh1 = dh1 + slopes[k].astype(F32)
    resid = tokens.astype(F32)
    scale = lax.rsqrt(jnp.mean(resid * resid, axis=-1, keepdims=True) + EPS)
    inner = jnp.mean(gains[0:1] * dh1 * resid, axis=-1, keepdims=True)
    grad_tokens = dx2 + scale * gains[0:1] * dh1 - resid * scale * scale * scale * inner

    total = jnp.sum(got.astype(F32), axis=0).astype(BF)
    final = jnp.stack(
        [lax.dynamic_index_in_dim(total, me, 0, False)]
        + [
            from_peer(lax.dynamic_index_in_dim(total, (me - k) % WS, 0, False), k)
            for k in (1, 2, 3)
        ]
        + [total[WS], total[WS + 1]]
    )
    spread_out = same_core(jnp.broadcast_to(final, (CHIPS,) + final.shape))
    twin_out = other_core(spread_out)
    sum_query, sum_key, sum_value, sum_router, sum_gains, sum_out = finish(
        experts, place, spread_out, twin_out
    )

    return (
        layer_out,
        grad_tokens,
        sum_gains[1],
        sum_query,
        sum_key,
        sum_value,
        sum_out,
        sum_gains[0],
        sum_router.T,
        grad_wg,
        grad_wu,
        grad_wd,
    )


def solution(mesh):
    rows = P(("exp", "ws"), None)
    placed = (
        rows,
        rows,
        P("exp", None),
        P("exp", None),
        rows,
        P("ws"),
        P("ws", None),
        P("ws", None),
        P("ws", None),
        P("ws", None),
        P("ws"),
        P("ws", None),
        P("exp", None, "ws"),
        P("exp", None, "ws"),
        P("exp", "ws", None),
    )
    return jax.shard_map(
        shards,
        mesh=mesh,
        in_specs=placed,
        out_specs=(
            rows,
            rows,
            P("ws"),
            P("ws", None),
            P("ws", None),
            P("ws", None),
            P("ws", None),
            P("ws"),
            P("ws", None),
            P("exp", None, "ws"),
            P("exp", None, "ws"),
            P("exp", "ws", None),
        ),
        check_vma=False,
    )
```

```python
import functools

import jax
import jax.numpy as jnp
from jax import lax
from jax.experimental import pallas as pl
from jax.experimental.pallas import tpu as pltpu
from jax.sharding import PartitionSpec as P

HEADS = 24
KV_HEADS = 8
HEAD = 64
EPS = 1e-06
THETA = 10000.0
MASKED = -1e30
BF = jnp.bfloat16
F32 = jnp.float32
WS = 4
CHIPS = 16
CAP = 48
VM = 60 * 1024 * 1024


def dot(a, b):
    return jnp.dot(a, b, preferred_element_type=F32)


def dot_t(a, b):
    return lax.dot_general(a, b, (((1,), (1,)), ((), ())), preferred_element_type=F32)


def tdot(a, b):
    return lax.dot_general(a, b, (((0,), (0,)), ((), ())), preferred_element_type=F32)


def split(v):
    hi = v.astype(BF)
    return hi, (v - hi.astype(F32)).astype(BF)


def from_peer(v, k):
    return lax.ppermute(v, "ws", [(s, (s - k) % WS) for s in range(WS)])


def to_peer(v, k):
    return lax.ppermute(v, "ws", [(s, (s + k) % WS) for s in range(WS)])


def other_core(v):
    return lax.ppermute(v, "exp", [(s, s ^ 1) for s in range(2 * CHIPS)])


def same_core(v):
    groups = [[2 * chip + core for chip in range(CHIPS)] for core in range(2)]
    return lax.all_to_all(v, "exp", 0, 0, tiled=True, axis_index_groups=groups)


def tree_layout(lengths, parents, token_index):
    seg = lengths.shape[0]
    labels = jnp.arange(seg, dtype=jnp.int32)
    segment_end = jnp.cumsum(lengths, dtype=jnp.int32)
    starts = segment_end - lengths
    segment = jnp.sum((token_index[:, None] >= segment_end[None, :]).astype(jnp.int32), axis=1)
    reach = ((parents[:, None] == labels[None, :]) | (labels[:, None] == labels[None, :])).astype(
        BF
    )
    for _ in range(4):
        reach = (dot(reach, reach) > 0.5).astype(BF)
    above = jnp.sum(reach.astype(jnp.int32) * lengths[None, :], axis=1) - lengths
    members = segment[:, None] == labels[None, :]
    position = jnp.sum(jnp.where(members, (above - starts)[None, :], 0), axis=1) + token_index
    members = members.astype(BF)
    reaches = dot(members, reach).astype(BF)
    visible = (dot_t(reaches, members) > 0.5) & (token_index[None, :] <= token_index[:, None])
    return visible, position


def expert_body(width, ff, x_ref, dy_ref, sel_ref, wr_ref, *rest):
    wg, wu, wd = rest[0:4], rest[4:8], rest[8:12]
    dx_ref, h_ref, dgu_ref, gate_ref = rest[12:16]
    wgu, wdn = rest[16:]
    part = wg[0].shape[1]

    @pl.when(pl.program_id(0) == 0)
    def _():
        for r in range(WS):
            wgu[:, r * part : (r + 1) * part] = wg[r][...]
            wgu[:, ff + r * part : ff + (r + 1) * part] = wu[r][...]
            wdn[r * part : (r + 1) * part, :] = wd[r][...]
        wgu[:, 2 * ff :] = wr_ref[...]

    pre = dot(x_ref[...], wgu[...])
    g, u, logits = pre[:, :ff], pre[:, ff : 2 * ff], pre[:, 2 * ff :]
    mask = dy_ref[:, width:].astype(F32) > 0.5
    logits = jnp.where(mask, logits, MASKED)
    lifted = jnp.where(mask, jnp.exp(logits - jnp.max(logits, axis=1, keepdims=True)), 0.0)
    total = jnp.maximum(jnp.sum(lifted, axis=1, keepdims=True), 1e-30)
    gate = jnp.sum(lifted * sel_ref[0:1, :], axis=1, keepdims=True) / total
    gate_ref[...] = jnp.broadcast_to(gate, gate_ref.shape)
    sig = 1.0 / (1.0 + jnp.exp(-g))
    silu = g * sig
    h = (silu * u).astype(BF)
    h_ref[...] = h
    raw = dot_t(dy_ref[:, :width], wdn[...])
    dgate = jnp.sum(raw * h.astype(F32), axis=1, keepdims=True)
    dh = raw * gate
    dgu_ref[:, :ff] = (dh * u * sig * (1.0 + g * (1.0 - sig))).astype(BF)
    dgu_ref[:, ff:] = (dh * silu).astype(BF)
    dx_ref[:, :width] = dot_t(dgu_ref[...], wgu[:, : 2 * ff]).astype(BF)
    hi = dgate.astype(BF).astype(F32)
    dx_ref[:, width:] = (hi * sel_ref[0:1, :] + (dgate - hi) * sel_ref[1:2, :]).astype(BF)


def expert_pass(x, dy, sel, wr, wg, wu, wd, tile):
    slots, width = x.shape
    part = wg[0].shape[1]
    ff = WS * part
    row = lambda w: pl.BlockSpec((tile, w), lambda i: (i, 0))
    once = lambda a: pl.BlockSpec(a.shape, lambda i: (0, 0))
    return pl.pallas_call(
        functools.partial(expert_body, width, ff),
        grid=(slots // tile,),
        in_specs=[row(width), row(width + 128), once(sel), once(wr)]
        + [once(a) for a in (*wg, *wu, *wd)],
        out_specs=[row(width + 128), row(ff), row(2 * ff), row(128)],
        out_shape=[
            jax.ShapeDtypeStruct((slots, width + 128), BF),
            jax.ShapeDtypeStruct((slots, ff), BF),
            jax.ShapeDtypeStruct((slots, 2 * ff), BF),
            jax.ShapeDtypeStruct((slots, 128), F32),
        ],
        scratch_shapes=[pltpu.VMEM((width, 2 * ff + 128), BF), pltpu.VMEM((ff, width), BF)],
        compiler_params=pltpu.CompilerParams(vmem_limit_bytes=VM),
        cost_estimate=pl.CostEstimate(
            flops=10 * slots * width * ff, bytes_accessed=9 * slots * width, transcendentals=0
        ),
        name="expert_pass",
    )(x, dy, sel, wr, *wg, *wu, *wd)


def in_slope_body(x_ref, dgu_ref, own_g, own_u, *peers):
    part = own_g.shape[1]
    ff = WS * part
    gu = tdot(x_ref[...], dgu_ref[...])
    own_g[...] = gu[:, :part]
    own_u[...] = gu[:, ff : ff + part]
    for k in (1, 2, 3):
        peers[k - 1][0] = gu[:, k * part : (k + 1) * part].astype(BF)
        peers[k - 1][1] = gu[:, ff + k * part : ff + (k + 1) * part].astype(BF)


def in_slopes(x, dgu, tile=256):
    slots, width = x.shape
    part = dgu.shape[1] // (2 * WS)
    tall = pl.BlockSpec((tile, part), lambda i: (i, 0))
    pair = pl.BlockSpec((2, tile, part), lambda i: (0, i, 0))
    return pl.pallas_call(
        in_slope_body,
        grid=(width // tile,),
        in_specs=[pl.BlockSpec((slots, tile), lambda i: (0, i)), whole(dgu.shape)],
        out_specs=[tall, tall] + [pair] * 3,
        out_shape=[sds((width, part), F32)] * 2 + [sds((2, width, part), BF)] * 3,
        compiler_params=pltpu.CompilerParams(vmem_limit_bytes=VM),
        cost_estimate=pl.CostEstimate(
            flops=2 * slots * width * dgu.shape[1],
            bytes_accessed=4 * slots * width,
            transcendentals=0,
        ),
        name="in_slopes",
    )(x, dgu)


def out_slope_body(h_ref, dy_ref, gate_ref, *refs):
    wd = refs[0:4]
    y_ref, own_d = refs[4:6]
    part = own_d.shape[0]
    d_y = (gate_ref[:, 0:1] * dy_ref[...].astype(F32)).astype(BF)
    dn = tdot(h_ref[...], d_y)
    own_d[...] = dn[:part]
    for k in (1, 2, 3):
        refs[5 + k][...] = dn[k * part : (k + 1) * part].astype(BF)
    y_ref[...] = dot(h_ref[...], jnp.concatenate([w[...] for w in wd], axis=0)).astype(BF)


def out_slopes(h, dy, gate, wd, tile=256):
    slots, ff = h.shape
    width = wd[0].shape[1]
    part = ff // WS
    col = pl.BlockSpec((slots, tile), lambda i: (0, i))
    flat = pl.BlockSpec((part, tile), lambda i: (0, i))
    return pl.pallas_call(
        out_slope_body,
        grid=(width // tile,),
        in_specs=[whole(h.shape), col, whole(gate.shape)] + [flat] * WS,
        out_specs=[col, flat] + [flat] * 3,
        out_shape=[sds((slots, width), BF), sds((part, width), F32)]
        + [sds((part, width), BF)] * 3,
        compiler_params=pltpu.CompilerParams(vmem_limit_bytes=VM),
        cost_estimate=pl.CostEstimate(
            flops=4 * slots * width * ff, bytes_accessed=4 * slots * width, transcendentals=0
        ),
        name="out_slopes",
    )(h, dy, gate, *wd)


def finish_body(experts, place_ref, a_ref, b_ref, ao_ref, bo_ref, *refs):
    q_ref, k_ref, v_ref, r_ref, g_ref, o_ref, s_ref = refs
    turn = pl.program_id(0)
    second = place_ref[1] == 1
    rows = q_ref.shape[0]
    half = a_ref.shape[3]
    kv = k_ref.shape[1]
    mine = a_ref[:, 0].astype(F32).reshape(rows, half)
    twin = b_ref[:, 0].astype(F32).reshape(rows, half)
    q_ref[...] = jnp.where(second, twin, mine)
    rest = jnp.where(second, mine, twin)
    k_ref[...] = rest[:, :kv]
    v_ref[...] = rest[:, kv : 2 * kv]

    @pl.when(turn == 0)
    def _():
        s_ref[...] = rest[:, 2 * kv :]

    @pl.when(turn > 0)
    def _():
        s_ref[...] += rest[:, 2 * kv :]

    @pl.when(turn == WS - 1)
    def _():
        turned = s_ref[...].T
        r_ref[...] = turned[:experts]
        g_ref[...] = turned[experts : experts + 8]

    mine = ao_ref[:, 0].astype(F32).reshape(rows, half)
    twin = bo_ref[:, 0].astype(F32).reshape(rows, half)
    o_ref[...] = jnp.where(second == (turn < 2), twin, mine)


def finish(experts, place, mine, twin):
    chips, sets, step, half = mine.shape
    rows = chips * step
    first = pl.BlockSpec((chips, 1, step, half), lambda i, p: (0, i, 0, 0))
    later = pl.BlockSpec((chips, 1, step, half), lambda i, p: (0, WS + i % 2, 0, 0))
    turned = lambda i, p: (0, lax.rem(p[0] + i, WS))
    kv = (half - 128) // 2
    S = jax.ShapeDtypeStruct
    return pl.pallas_call(
        functools.partial(finish_body, experts),
        grid_spec=pltpu.PrefetchScalarGridSpec(
            num_scalar_prefetch=1,
            grid=(WS,),
            in_specs=[first, first, later, later],
            out_specs=[
                pl.BlockSpec((rows, half), turned),
                pl.BlockSpec((rows, kv), turned),
                pl.BlockSpec((rows, kv), turned),
                whole((experts, rows)),
                whole((8, rows)),
                pl.BlockSpec((rows, half), lambda i, p: (0, i)),
            ],
            scratch_shapes=[pltpu.VMEM((rows, 128), F32)],
        ),
        out_shape=[
            S((rows, WS * half), F32),
            S((rows, WS * kv), F32),
            S((rows, WS * kv), F32),
            S((experts, rows), F32),
            S((8, rows), F32),
            S((rows, WS * half), F32),
        ],
        compiler_params=pltpu.CompilerParams(vmem_limit_bytes=VM),
        cost_estimate=pl.CostEstimate(flops=0, bytes_accessed=16 * rows * WS * half, transcendentals=0),
        name="finish",
    )(place, mine, twin, mine, twin)


def whole(shape):
    return pl.BlockSpec(shape, lambda *_: (0,) * len(shape))


def sds(shape, kind):
    return jax.ShapeDtypeStruct(shape, kind)


def one_step(body, name, scalars, arrays, outs, scratch, flops):
    moved = sum(a.size * a.dtype.itemsize for a in arrays)
    return pl.pallas_call(
        body,
        in_specs=[pl.BlockSpec(memory_space=pltpu.SMEM)] * len(scalars)
        + [pl.BlockSpec(memory_space=pltpu.VMEM)] * len(arrays),
        out_specs=[pl.BlockSpec(memory_space=pltpu.VMEM)] * len(outs),
        out_shape=outs,
        scratch_shapes=scratch,
        compiler_params=pltpu.CompilerParams(vmem_limit_bytes=VM),
        cost_estimate=pl.CostEstimate(flops=flops, bytes_accessed=moved, transcendentals=0),
        name=name,
    )(*scalars, *arrays)


def other_half(v):
    lanes = v.shape[1]
    low = lax.broadcasted_iota(jnp.int32, v.shape, 1) % HEAD < HEAD // 2
    ahead = pltpu.roll(v, lanes - HEAD // 2, 1)
    behind = pltpu.roll(v, HEAD // 2, 1)
    return jnp.where(low, ahead, behind)


def wide(ref, times):
    return jnp.concatenate([ref[...]] * times, axis=1)


def rms(x):
    return lax.rsqrt(jnp.mean(x * x, axis=1, keepdims=True) + EPS)


def column_sum(m, lane):
    hi, lo = split(m)
    pick = (lax.broadcasted_iota(jnp.int32, (m.shape[0], 128), 1) == lane).astype(F32).astype(BF)
    return tdot(hi, pick) + tdot(lo, pick)


def pack_body(experts, x_ref, wq, wk, wv, wr, na, nm, *outs):
    small = outs[WS + 1]
    me, core = lax.axis_index("ws"), lax.rem(lax.axis_index("exp"), 2)
    rows = x_ref.shape[0]
    strip = wq.shape[0] // 2
    q_w, kv_w = wq.shape[1] // WS, wk.shape[1] // WS
    shard = wq.shape[0]
    norms = [n[...].astype(F32).reshape(1, shard) for n in (na, nm)]
    few = [wr[...].astype(F32), *norms, jnp.zeros((126 - experts, shard), F32)]
    small[...] = jnp.concatenate(few, axis=0).T.astype(BF)

    def place(out, top, left, side, d, start, count):
        part = pl.ds(pl.multiple_of(side * strip + start, 32), count)
        here = slice(top, top + count)
        spot = pl.ds(pl.multiple_of(d * kv_w, 128), kv_w)
        out[here, left : left + q_w] = wq[part, pl.ds(pl.multiple_of(d * q_w, 128), q_w)]
        out[here, left + q_w : left + q_w + kv_w] = wk[part, spot]
        out[here, left + q_w + kv_w : left + q_w + 2 * kv_w] = wv[part, spot]
        out[here, left + q_w + 2 * kv_w : left + q_w + 2 * kv_w + 128] = small[part, :]

    for r in range(WS + 1):
        side = core if r < WS else 1 - core
        d = lax.rem(me + WS - r % WS, WS)
        if r == 2:
            outs[r][:rows, :] = x_ref[...]
            for half in range(2):
                left = half * (q_w + 2 * kv_w + 128)
                place(outs[r], rows, left, side, d, half * strip // 2, strip // 2)
        else:
            place(outs[r], 0, 0, side, d, 0, strip)


def pack(experts, x, wq, wk, wv, wr, na, nm):
    shard = wq.shape[0]
    rows, width = x.shape
    wide_w = (wq.shape[1] + 2 * wk.shape[1]) // WS + 128
    outs = [sds((shard // 2, wide_w), BF)] * (WS + 1)
    outs[2] = sds((rows + shard // 4, 2 * wide_w), BF)
    return one_step(
        functools.partial(pack_body, experts),
        "pack",
        [],
        [x, wq, wk, wv, wr, na, nm],
        outs,
        [pltpu.VMEM((shard, 128), BF)],
        0,
    )


def dispatch_body(experts, routes_ref, cot_ref, send_ref, slot_ref, chosen_ref, spread_ref):
    rows, width = cot_ref.shape
    slots = slot_ref.shape[1]
    tile = send_ref.shape[0]
    step = pl.program_id(0)

    @pl.when(step == 0)
    def _():
        name = lax.broadcasted_iota(jnp.int32, (128, rows), 0)
        named = jnp.zeros((128, rows), F32)
        for k in range(routes_ref.shape[0]):
            named = named + (routes_ref[k : k + 1, :] == name).astype(F32)
        chosen = named.T
        chosen_ref[...] = chosen.astype(BF)
        this = lax.broadcasted_iota(jnp.int32, (rows, rows), 0)
        that = lax.broadcasted_iota(jnp.int32, (rows, rows), 1)
        rank = dot((that < this).astype(F32).astype(BF), chosen.astype(BF))
        col = lax.broadcasted_iota(jnp.int32, (128, slots), 1)
        first = lax.broadcasted_iota(jnp.int32, (128, slots), 0) * CAP
        spread = jnp.where((col >= first) & (col < first + CAP), 1.0, 0.0)
        spread_ref[...] = spread.astype(BF)
        spot = dot((chosen * (rank + 1.0)).astype(BF), spread.astype(BF))
        want = jnp.sum(spread * (col - first + 1).astype(F32), axis=0, keepdims=True)
        slot_ref[...] = jnp.where(spot == want, 1.0, 0.0).astype(BF)

    part = slot_ref[:, pl.ds(pl.multiple_of(step * tile, tile), tile)]
    send_ref[:, :width] = tdot(part, cot_ref[...]).astype(BF)
    send_ref[:, width:] = tdot(part, chosen_ref[...]).astype(BF)


def dispatch(experts, routes, cot, tile=512):
    rows, width = cot.shape
    slots = experts * CAP
    outs = [
        sds((slots, width + 128), BF),
        sds((rows, slots), BF),
        sds((rows, 128), BF),
        sds((128, slots), BF),
    ]
    return pl.pallas_call(
        functools.partial(dispatch_body, experts),
        grid=(slots // tile,),
        in_specs=[whole((routes.shape[1], rows)), whole((rows, width))],
        out_specs=[pl.BlockSpec((tile, width + 128), lambda i: (i, 0))]
        + [whole(o.shape) for o in outs[1:]],
        out_shape=outs,
        compiler_params=pltpu.CompilerParams(vmem_limit_bytes=VM),
        cost_estimate=pl.CostEstimate(
            flops=2 * rows * width * slots, bytes_accessed=3 * slots * width, transcendentals=0
        ),
        name="dispatch",
    )(routes.T, cot)


def attend_rows(qkv_ref, bias_ref, o_ref, lse_ref, start, q_w, kv_w):
    rows = o_ref.shape[0]
    group = q_w // kv_w
    here = slice(start, start + rows)
    for h in range(q_w // HEAD):
        at = h // group * HEAD
        q = qkv_ref[here, h * HEAD : (h + 1) * HEAD]
        k = qkv_ref[:, q_w + at : q_w + at + HEAD]
        v = qkv_ref[:, q_w + kv_w + at : q_w + kv_w + at + HEAD]
        s = dot_t(q, k) * HEAD ** (-0.5) + bias_ref[here, :]
        peak = jnp.max(s, axis=1, keepdims=True)
        p = jnp.exp(s - peak)
        total = jnp.sum(p, axis=1, keepdims=True)
        lse_ref[:, h : h + 1] = peak + jnp.log(total)
        o_ref[:, h * HEAD : (h + 1) * HEAD] = dot((p / total).astype(BF), v).astype(BF)


def attend_body(experts, place_ref, *refs):
    xs, own, twin = refs[0:4], refs[4:8], refs[8:12]
    cos_ref, sin_ref, bias_ref, wo_ref = refs[12:16]
    h1_ref, qkv_ref, o_ref, lse_ref, w_ref, small_ref, rows_ref = refs[16:23]
    parts = refs[23:26]
    me, core = place_ref[0], place_ref[1]
    rows = xs[0].shape[0]
    strip = own[0].shape[0]
    wide_w = own[0].shape[1]
    q_w = o_ref.shape[1]
    qkv_w = qkv_ref.shape[1]
    kv_w = (qkv_w - q_w) // 2
    for r in range(WS):
        base = lax.rem(me + r, WS) * (2 * strip)
        for source, side in ((own[r], core), (twin[r], 1 - core)):
            folds = source.shape[1] // wide_w
            count = strip // folds
            for f in range(folds):
                left = f * wide_w
                spot = pl.ds(pl.multiple_of(base + side * strip + f * count, 32), count)
                w_ref[spot, :] = source[:, left : left + qkv_w]
                small_ref[spot, :] = source[:, left + qkv_w : left + wide_w]
    turned = small_ref[...].astype(F32).T
    rows_ref[...] = jnp.concatenate(
        [turned[experts : experts + 2], jnp.zeros((6, turned.shape[1]), F32)], axis=0
    )
    gain = turned[experts : experts + 1]
    for r in range(WS):
        x = xs[r][:rows, :].astype(F32)
        h1_ref[r * rows : (r + 1) * rows, :] = (x * rms(x) * gain).astype(BF)
    qkv = dot(h1_ref[...], w_ref[...])
    qk = qkv[:, : q_w + kv_w]
    times = (q_w + kv_w) // 128
    qk = qk * wide(cos_ref, times) + other_half(qk) * wide(sin_ref, times)
    qkv_ref[:, : q_w + kv_w] = qk.astype(BF)
    qkv_ref[:, q_w + kv_w :] = qkv[:, q_w + kv_w :].astype(BF)
    attend_rows(qkv_ref, bias_ref, o_ref, lse_ref, rows, q_w, kv_w)
    for r in range(3):
        part = dot(o_ref[r * rows : (r + 1) * rows, :], wo_ref[...])
        parts[r][...] = part.astype(BF)


def attend(experts, place, xs, own, twin, cos, sin, bias, wo):
    rows, width = xs[0].shape
    tree = rows * WS
    q_w, qkv_w = wo.shape[0], own[0].shape[1] - 128
    outs = [
        sds((tree, width), BF),
        sds((tree, qkv_w), BF),
        sds((tree - rows, q_w), BF),
        sds((tree - rows, 128), F32),
        sds((width, qkv_w), BF),
        sds((width, 128), BF),
        sds((8, width), F32),
    ] + [sds((rows, width), BF)] * 3
    flops = 40 * tree * width * (qkv_w + q_w)
    return one_step(
        functools.partial(attend_body, experts),
        "attend",
        [place],
        [*xs, *own, *twin, cos, sin, bias, wo],
        outs,
        [],
        flops,
    )


def attend_own_body(qkv_ref, bias_ref, wo_ref, o_ref, lse_ref, part_ref):
    q_w = o_ref.shape[1]
    kv_w = (qkv_ref.shape[1] - q_w) // 2
    attend_rows(qkv_ref, bias_ref, o_ref, lse_ref, 0, q_w, kv_w)
    part_ref[...] = dot(o_ref[...], wo_ref[...])


def attend_own(rows, qkv, bias, wo):
    q_w, width = wo.shape
    outs = [sds((rows, q_w), BF), sds((rows, 128), F32), sds((rows, width), F32)]
    flops = 2 * rows * width * q_w + 4 * rows * qkv.shape[0] * q_w
    return one_step(attend_own_body, "attend_own", [], [qkv, bias, wo], outs, [], flops)


def enter_body(x_ref, p0, p1, p2, p3, rows_ref, slot_ref, x2_ref, h2_ref, send_ref):
    @pl.when(pl.program_id(0) == 0)
    def _():
        x2 = x_ref[...].astype(F32) + p0[...]
        for p in (p1, p2, p3):
            x2 = x2 + p[...].astype(F32)
        x2_ref[...] = x2
        h2_ref[...] = (x2 * rms(x2) * rows_ref[1:2, :]).astype(BF)

    send_ref[...] = tdot(slot_ref[...], h2_ref[...]).astype(BF)


def enter(x, parts, rows, to_slot, tile=512):
    n, width = x.shape
    slots = to_slot.shape[1]
    arrays = [x, *parts, rows]
    return pl.pallas_call(
        enter_body,
        grid=(slots // tile,),
        in_specs=[whole(a.shape) for a in arrays] + [pl.BlockSpec((n, tile), lambda i: (0, i))],
        out_specs=[
            whole((n, width)),
            whole((n, width)),
            pl.BlockSpec((tile, width), lambda i: (i, 0)),
        ],
        out_shape=[sds((n, width), F32), sds((n, width), BF), sds((slots, width), BF)],
        compiler_params=pltpu.CompilerParams(vmem_limit_bytes=VM),
        cost_estimate=pl.CostEstimate(
            flops=2 * n * width * slots, bytes_accessed=3 * slots * width, transcendentals=0
        ),
        name="enter",
    )(*arrays, to_slot)


def gate_body(h2_ref, router_ref, slot_ref, chosen_ref, spread_ref, gates_ref, gs_ref):
    logits = dot(h2_ref[...], router_ref[...])
    mask = chosen_ref[...].astype(F32) > 0.5
    logits = jnp.where(mask, logits, MASKED)
    lifted = jnp.where(mask, jnp.exp(logits - jnp.max(logits, axis=1, keepdims=True)), 0.0)
    gates = lifted / jnp.maximum(jnp.sum(lifted, axis=1, keepdims=True), 1e-30)
    gates_ref[...] = gates
    hi, lo = split(gates)
    on_slots = dot(hi, spread_ref[...]) + dot(lo, spread_ref[...])
    hi, lo = split(on_slots * slot_ref[...].astype(F32))
    rows = gates.shape[0]
    gs_ref[:rows, :] = hi
    gs_ref[rows:, :] = lo


def gate_terms(h2, router, to_slot, chosen, spread):
    n, slots = to_slot.shape
    outs = [sds((n, 128), F32), sds((2 * n, slots), BF)]
    arrays = [h2, router, to_slot, chosen, spread]
    return one_step(gate_body, "gate_terms", [], arrays, outs, [], 8 * n * 128 * slots)


def leave_body(experts, back_ref, slot_ref, gates_ref, router_ref, x2_ref, rows_ref, cot_ref, *outs):
    dx2_ref, da_ref, dh2_ref, dl_ref, sum_ref = outs
    width = x2_ref.shape[1]
    step = pl.program_id(0)
    more = dot(slot_ref[...], back_ref[...])

    @pl.when(step == 0)
    def _():
        sum_ref[...] = more

    @pl.when(step > 0)
    def _():
        sum_ref[...] += more

    @pl.when(step == pl.num_programs(0) - 1)
    def _():
        tail = sum_ref[:, width:]
        dgate = tail + pltpu.roll(tail, 128 - experts, 1)
        gates = gates_ref[...]
        dl = gates * (dgate - jnp.sum(gates * dgate, axis=1, keepdims=True))
        dl_ref[...] = dl
        hi, lo = split(dl)
        dh2 = sum_ref[:, :width] + dot_t(hi, router_ref[...]) + dot_t(lo, router_ref[...])
        dh2_ref[...] = dh2
        x2 = x2_ref[...]
        scale, gain = rms(x2), rows_ref[1:2, :]
        inner = jnp.mean(gain * dh2 * x2, axis=1, keepdims=True)
        dx2 = cot_ref[...].astype(F32) + scale * gain * dh2 - x2 * scale * scale * scale * inner
        dx2_ref[...] = dx2
        da_ref[...] = dx2.astype(BF)


def leave(experts, back, to_slot, gates, router, x2, rows, cot, tile=512):
    n, width = x2.shape
    slots = back.shape[0]
    outs = [sds((n, width), F32), sds((n, width), BF), sds((n, width), F32), sds((n, 128), F32)]
    rest = [gates, router, x2, rows, cot]
    return pl.pallas_call(
        functools.partial(leave_body, experts),
        grid=(slots // tile,),
        in_specs=[
            pl.BlockSpec((tile, width + 128), lambda i: (i, 0)),
            pl.BlockSpec((n, tile), lambda i: (0, i)),
        ]
        + [whole(a.shape) for a in rest],
        out_specs=[whole(o.shape) for o in outs],
        out_shape=outs,
        scratch_shapes=[pltpu.VMEM((n, width + 128), F32)],
        compiler_params=pltpu.CompilerParams(vmem_limit_bytes=VM),
        cost_estimate=pl.CostEstimate(
            flops=2 * n * width * slots, bytes_accessed=3 * slots * width, transcendentals=0
        ),
        name="leave",
    )(back, to_slot, *rest)


def small_body(experts, h2_ref, dl_ref, dh2_ref, x2_ref, out_ref):
    hi, lo = split(dl_ref[...])
    h2, x2 = h2_ref[...], x2_ref[...]
    out_ref[...] = tdot(h2, hi) + tdot(h2, lo) + column_sum(dh2_ref[...] * x2 * rms(x2), experts)


def small_slopes(experts, h2, dl, dh2, x2):
    n, width = x2.shape
    return one_step(
        functools.partial(small_body, experts),
        "small_slopes",
        [],
        [h2, dl, dh2, x2],
        [sds((width, 128), F32)],
        [],
        8 * n * width * 128,
    )[0]


def attend_back_body(experts, place_ref, *refs):
    das, xs = refs[0:4], refs[4:8]
    wo_ref, qkv_ref, o_own, o_far, lse_own, lse_far, h1_ref, w_ref = refs[8:16]
    cos_ref, sin_ref, bias_ref, small_ref = refs[16:20]
    keep_ref, give_ref = refs[20:22]
    parts = refs[22:26]
    da, do, dqk, dqkv, o_ref, lse_ref = refs[26:32]
    core = place_ref[1]
    rows = xs[0].shape[0]
    q_w, qkv_w = o_ref.shape[1], qkv_ref.shape[1]
    kv_w = (qkv_w - q_w) // 2
    group = q_w // kv_w
    scale = HEAD ** (-0.5)
    for r in range(WS):
        da[r * rows : (r + 1) * rows, :] = das[r][...]
    o_ref[:rows, :] = o_own[...]
    o_ref[rows:, :] = o_far[...]
    lse_ref[:rows, :] = lse_own[...]
    lse_ref[rows:, :] = lse_far[...]
    do[...] = dot_t(da[...], wo_ref[...]).astype(BF)
    for n in range(kv_w // HEAD):
        at = n * HEAD
        k = qkv_ref[:, q_w + at : q_w + at + HEAD]
        v = qkv_ref[:, q_w + kv_w + at : q_w + kv_w + at + HEAD]
        dk, dv = None, None
        for h in range(n * group, (n + 1) * group):
            q = qkv_ref[:, h * HEAD : (h + 1) * HEAD]
            doh = do[:, h * HEAD : (h + 1) * HEAD]
            p = jnp.exp(dot_t(q, k) * scale + bias_ref[...] - lse_ref[:, h : h + 1])
            dp = dot_t(doh, v)
            delta = jnp.sum(p * dp, axis=1, keepdims=True)
            ds = (p * (dp - delta)).astype(BF)
            dqk[:, h * HEAD : (h + 1) * HEAD] = dot(ds, k) * scale
            more_k, more_v = tdot(ds, q), tdot(p.astype(BF), doh)
            dk = more_k if dk is None else dk + more_k
            dv = more_v if dv is None else dv + more_v
        dqk[:, q_w + at : q_w + at + HEAD] = dk * scale
        dqkv[:, q_w + kv_w + at : q_w + kv_w + at + HEAD] = dv.astype(BF)
    dqkv[:, qkv_w:] = jnp.zeros((da.shape[0], 128), BF)
    d = dqk[...]
    times = (q_w + kv_w) // 128
    d = d * wide(cos_ref, times) - other_half(d) * wide(sin_ref, times)
    dqkv[:, : q_w + kv_w] = d.astype(BF)
    small = small_ref[...]
    for r in range(WS):
        dh1 = dot_t(dqkv[r * rows : (r + 1) * rows, :qkv_w], w_ref[...])
        parts[r][...] = dh1.astype(parts[r].dtype)
        x = xs[r][:rows, :].astype(F32)
        small = small + column_sum(dh1 * x * rms(x), experts + 1)
    half = keep_ref.shape[3]
    chips, step = keep_ref.shape[0], keep_ref.shape[2]
    count = chips * step

    def put(i, first, second):
        kept = jnp.where(core == 0, first, second)
        given = jnp.where(core == 0, second, first)
        keep_ref[:, i] = kept.reshape(chips, step, half)
        give_ref[:, i] = given.reshape(chips, step, half).astype(BF)

    for i in range(WS):
        both = tdot(h1_ref[:, i * count : (i + 1) * count], dqkv[...])
        mine = small[i * count : (i + 1) * count]
        second = jnp.concatenate([both[:, half : 2 * half - 128], both[:, 2 * half - 128 :] + mine], axis=1)
        put(i, both[:, :half], second)
    slope = tdot(o_ref[...], da[...])
    for i in range(2):
        put(WS + i, slope[:, i * half : (i + 1) * half], slope[:, (2 + i) * half : (3 + i) * half])


def attend_back(experts, place, das, xs, wo, qkv, os, lses, h1, w, cos, sin, bias, small):
    rows, width = xs[0].shape
    tree = rows * WS
    q_w, qkv_w = wo.shape[0], qkv.shape[1]
    half = (qkv_w + 128) // 2
    load = (CHIPS, WS + 2, width // WS // CHIPS, half)
    outs = [sds(load, F32), sds(load, BF), sds((rows, width), F32)] + [sds((rows, width), BF)] * 3
    scratch = [
        pltpu.VMEM((tree, width), BF),
        pltpu.VMEM((tree, q_w), BF),
        pltpu.VMEM((tree, (q_w + qkv_w) // 2), F32),
        pltpu.VMEM((tree, qkv_w + 128), BF),
        pltpu.VMEM((tree, q_w), BF),
        pltpu.VMEM((tree, 128), F32),
    ]
    flops = 4 * tree * width * (qkv_w + q_w) + 10 * tree * tree * q_w
    return one_step(
        functools.partial(attend_back_body, experts),
        "attend_back",
        [place],
        [*das, *xs, wo, qkv, *os, *lses, h1, w, cos, sin, bias, small],
        outs,
        scratch,
        flops,
    )


def shards(
    tokens,
    cotangent,
    seg_lengths,
    parents,
    routes,
    norm_attn,
    w_query,
    w_key,
    w_value,
    w_out,
    norm_moe,
    w_router,
    w_gate,
    w_up,
    w_down,
):
    me = lax.axis_index("ws")
    expert = lax.axis_index("exp")
    core = expert % 2
    place = jnp.stack([me, core]).astype(jnp.int32)
    rows, width = tokens.shape
    shard = width // WS
    strip = shard // 2
    experts = 2 * CHIPS
    q_w, kv_w = HEADS // WS * HEAD, KV_HEADS // WS * HEAD
    slots = experts * CAP

    def gathered(v):
        return [v] + [from_peer(v, k) for k in (1, 2, 3)]

    pieces = pack(
        experts, tokens, w_query, w_key, w_value, w_router.T, norm_attn, norm_moe
    )
    came = [None] + [from_peer(pieces[k], k) for k in (1, 2, 3)]
    mine, came[1] = lax.optimization_barrier((tokens, came[1]))
    xs = [tokens, from_peer(mine, 1), came[2], from_peer(mine, 3)]
    own = [pieces[0], came[1], came[2][rows:], came[3]]

    lane = jnp.arange(128, dtype=jnp.int32)
    row_id = jnp.arange(rows, dtype=jnp.int32)
    dy_send, to_slot, chosen, spread = dispatch(experts, routes, cotangent)
    dy_send = dy_send.reshape(experts, CAP, width + 128)
    dy_slots = lax.all_to_all(dy_send, "exp", 0, 0, tiled=True).reshape(slots, width + 128)

    order = (
        ((me + jnp.arange(WS, dtype=jnp.int32)) % WS)[:, None] * rows + row_id[None, :]
    ).reshape(-1)
    visible, position = tree_layout(seg_lengths[0], parents[0], order)
    bias = jnp.where(visible, 0.0, MASKED).astype(F32)
    inverse = THETA ** (-(lane % (HEAD // 2)).astype(F32) * 2.0 / HEAD)
    angles = position.astype(F32)[:, None] * inverse[None, :]
    cosines = jnp.cos(angles)
    sines = jnp.where((lane % HEAD < HEAD // 2)[None, :], -1.0, 1.0) * jnp.sin(angles)
    own[1], bias, cosines, sines = lax.optimization_barrier((own[1], bias, cosines, sines))
    twin = [pieces[WS]] + [other_core(own[k]) for k in (1, 2, 3)]
    h1, qkv, o_far, lse_far, w_qkv, small_full, gains, *parts = attend(
        experts, place, xs, own, twin, cosines, sines, bias, w_out
    )
    o_own, lse_own, part_own = attend_own(rows, qkv, bias, w_out)
    sums = [part_own] + [to_peer(parts[k - 1], k) for k in (1, 2, 3)]
    x2, h2, x_send = enter(tokens, sums, gains, to_slot)
    x_send, wg_own, wu_own, wd_own = lax.optimization_barrier(
        (x_send, w_gate[0], w_up[0], w_down[0])
    )
    x_slots = lax.all_to_all(
        x_send.reshape(experts, CAP, width), "exp", 0, 0, tiled=True
    ).reshape(slots, width)

    sel = jnp.concatenate(
        [
            (lane == expert).astype(F32)[None],
            (lane == expert + experts).astype(F32)[None],
            jnp.zeros((6, 128), F32),
        ],
        axis=0,
    )
    wd = gathered(wd_own)
    gates, gate_slots = gate_terms(h2, small_full, to_slot, chosen, spread)
    wd[1], gates, gate_slots = lax.optimization_barrier((wd[1], gates, gate_slots))
    dx_send, hidden, d_gu, slot_gates = expert_pass(
        x_slots, dy_slots, sel, small_full, gathered(wg_own), gathered(wu_own), wd, 256
    )
    dx_back = lax.all_to_all(
        dx_send.reshape(experts, CAP, width + 128), "exp", 0, 0, tiled=True
    ).reshape(slots, width + 128)

    own_g, own_u, gu1, gu2, gu3 = in_slopes(x_slots, d_gu)
    gu1, gu2, gu3 = to_peer(gu1, 1), to_peer(gu2, 2), to_peer(gu3, 3)
    hidden, gu1 = lax.optimization_barrier((hidden, gu1))
    y, own_d, dn1, dn2, dn3 = out_slopes(hidden, dy_slots, slot_gates, wd)
    dn1, dn2, dn3 = to_peer(dn1, 1), to_peer(dn2, 2), to_peer(dn3, 3)
    dx_back, y, gu1, dn1, gu2, dn2, gu3, dn3 = lax.optimization_barrier(
        (dx_back, y, gu1, dn1, gu2, dn2, gu3, dn3)
    )
    y_back = lax.all_to_all(y.reshape(experts, CAP, width), "exp", 0, 0, tiled=True).reshape(
        slots, width
    )

    dx2, d_a, dh2, dl = leave(
        experts, dx_back, to_slot, gates, small_full, x2, gains, cotangent
    )
    das = gathered(d_a)
    small_terms = small_slopes(experts, h2, dl, dh2, x2)
    grad_gu = jnp.stack([own_g, own_u]) + gu1.astype(F32) + gu2.astype(F32) + gu3.astype(F32)
    grad_wg, grad_wu = grad_gu[0][None], grad_gu[1][None]
    grad_wd = (own_d + dn1.astype(F32) + dn2.astype(F32) + dn3.astype(F32))[None]
    das, grad_wg, grad_wu, grad_wd = lax.optimization_barrier((das, grad_wg, grad_wu, grad_wd))
    keep, give, *slopes = attend_back(
        experts,
        place,
        das,
        xs,
        w_out,
        qkv,
        (o_own, o_far),
        (lse_own, lse_far),
        h1,
        w_qkv,
        cosines,
        sines,
        bias,
        small_terms,
    )
    sent = (keep + other_core(give).astype(F32)).astype(BF)
    sent, y_back = lax.optimization_barrier((sent, y_back))
    step = shard // CHIPS
    both = dot(gate_slots, y_back)
    layer_out = (x2 + both[:rows] + both[rows:]).astype(BF)
    got = same_core(sent)
    slopes = [slopes[0]] + [to_peer(slopes[k], k) for k in (1, 2, 3)]
    got, layer_out, slopes = lax.optimization_barrier((got, layer_out, slopes))
    dh1 = slopes[0]
    for k in (1, 2, 3):
        dh1 = dh1 + slopes[k].astype(F32)
    resid = tokens.astype(F32)
    scale = lax.rsqrt(jnp.mean(resid * resid, axis=-1, keepdims=True) + EPS)
    inner = jnp.mean(gains[0:1] * dh1 * resid, axis=-1, keepdims=True)
    grad_tokens = dx2 + scale * gains[0:1] * dh1 - resid * scale * scale * scale * inner

    total = jnp.sum(got.astype(F32), axis=0).astype(BF)
    final = jnp.stack(
        [lax.dynamic_index_in_dim(total, me, 0, False)]
        + [
            from_peer(lax.dynamic_index_in_dim(total, (me - k) % WS, 0, False), k)
            for k in (1, 2, 3)
        ]
        + [total[WS], total[WS + 1]]
    )
    spread_out = same_core(jnp.broadcast_to(final, (CHIPS,) + final.shape))
    twin_out = other_core(spread_out)
    sum_query, sum_key, sum_value, sum_router, sum_gains, sum_out = finish(
        experts, place, spread_out, twin_out
    )

    return (
        layer_out,
        grad_tokens,
        sum_gains[1],
        sum_query,
        sum_key,
        sum_value,
        sum_out,
        sum_gains[0],
        sum_router.T,
        grad_wg,
        grad_wu,
        grad_wd,
    )


def solution(mesh):
    rows = P(("exp", "ws"), None)
    placed = (
        rows,
        rows,
        P("exp", None),
        P("exp", None),
        rows,
        P("ws"),
        P("ws", None),
        P("ws", None),
        P("ws", None),
        P("ws", None),
        P("ws"),
        P("ws", None),
        P("exp", None, "ws"),
        P("exp", None, "ws"),
        P("exp", "ws", None),
    )
    return jax.shard_map(
        shards,
        mesh=mesh,
        in_specs=placed,
        out_specs=(
            rows,
            rows,
            P("ws"),
            P("ws", None),
            P("ws", None),
            P("ws", None),
            P("ws", None),
            P("ws"),
            P("ws", None),
            P("exp", None, "ws"),
            P("exp", None, "ws"),
            P("exp", "ws", None),
        ),
        check_vma=False,
    )
```

```python
import functools

import jax
import jax.numpy as jnp
from jax import lax
from jax.experimental import pallas as pl
from jax.experimental.pallas import tpu as pltpu
from jax.sharding import PartitionSpec as P

HEADS = 24
KV_HEADS = 8
HEAD = 64
EPS = 1e-06
THETA = 10000.0
MASKED = -1e30
BF = jnp.bfloat16
F32 = jnp.float32
WS = 4
CHIPS = 16
CAP = 48
VM = 60 * 1024 * 1024


def dot(a, b):
    return jnp.dot(a, b, preferred_element_type=F32)


def dot_t(a, b):
    return lax.dot_general(a, b, (((1,), (1,)), ((), ())), preferred_element_type=F32)


def tdot(a, b):
    return lax.dot_general(a, b, (((0,), (0,)), ((), ())), preferred_element_type=F32)


def split(v):
    hi = v.astype(BF)
    return hi, (v - hi.astype(F32)).astype(BF)


def from_peer(v, k):
    return lax.ppermute(v, "ws", [(s, (s - k) % WS) for s in range(WS)])


def to_peer(v, k):
    return lax.ppermute(v, "ws", [(s, (s + k) % WS) for s in range(WS)])


def other_core(v):
    return lax.ppermute(v, "exp", [(s, s ^ 1) for s in range(2 * CHIPS)])


def same_core(v):
    groups = [[2 * chip + core for chip in range(CHIPS)] for core in range(2)]
    return lax.all_to_all(v, "exp", 0, 0, tiled=True, axis_index_groups=groups)


def tree_layout(lengths, parents, token_index):
    seg = lengths.shape[0]
    labels = jnp.arange(seg, dtype=jnp.int32)
    segment_end = jnp.cumsum(lengths, dtype=jnp.int32)
    starts = segment_end - lengths
    segment = jnp.sum((token_index[:, None] >= segment_end[None, :]).astype(jnp.int32), axis=1)
    reach = ((parents[:, None] == labels[None, :]) | (labels[:, None] == labels[None, :])).astype(
        BF
    )
    for _ in range(4):
        reach = (dot(reach, reach) > 0.5).astype(BF)
    above = jnp.sum(reach.astype(jnp.int32) * lengths[None, :], axis=1) - lengths
    members = segment[:, None] == labels[None, :]
    position = jnp.sum(jnp.where(members, (above - starts)[None, :], 0), axis=1) + token_index
    members = members.astype(BF)
    reaches = dot(members, reach).astype(BF)
    visible = (dot_t(reaches, members) > 0.5) & (token_index[None, :] <= token_index[:, None])
    return visible, position


def expert_body(width, ff, x_ref, dy_ref, sel_ref, wr_ref, *rest):
    wg, wu, wd = rest[0:4], rest[4:8], rest[8:12]
    dx_ref, h_ref, dgu_ref, gate_ref = rest[12:16]
    wgu, wdn = rest[16:]
    part = wg[0].shape[1]

    @pl.when(pl.program_id(0) == 0)
    def _():
        for r in range(WS):
            wgu[:, r * part : (r + 1) * part] = wg[r][...]
            wgu[:, ff + r * part : ff + (r + 1) * part] = wu[r][...]
            wdn[r * part : (r + 1) * part, :] = wd[r][...]
        wgu[:, 2 * ff :] = wr_ref[...]

    pre = dot(x_ref[...], wgu[...])
    g, u, logits = pre[:, :ff], pre[:, ff : 2 * ff], pre[:, 2 * ff :]
    mask = dy_ref[:, width:].astype(F32) > 0.5
    logits = jnp.where(mask, logits, MASKED)
    lifted = jnp.where(mask, jnp.exp(logits - jnp.max(logits, axis=1, keepdims=True)), 0.0)
    total = jnp.maximum(jnp.sum(lifted, axis=1, keepdims=True), 1e-30)
    gate = jnp.sum(lifted * sel_ref[0:1, :], axis=1, keepdims=True) / total
    gate_ref[...] = jnp.broadcast_to(gate, gate_ref.shape)
    sig = 1.0 / (1.0 + jnp.exp(-g))
    silu = g * sig
    h = (silu * u).astype(BF)
    h_ref[...] = h
    raw = dot_t(dy_ref[:, :width], wdn[...])
    dgate = jnp.sum(raw * h.astype(F32), axis=1, keepdims=True)
    dh = raw * gate
    dgu_ref[:, :ff] = (dh * u * sig * (1.0 + g * (1.0 - sig))).astype(BF)
    dgu_ref[:, ff:] = (dh * silu).astype(BF)
    dx_ref[:, :width] = dot_t(dgu_ref[...], wgu[:, : 2 * ff]).astype(BF)
    hi = dgate.astype(BF).astype(F32)
    dx_ref[:, width:] = (hi * sel_ref[0:1, :] + (dgate - hi) * sel_ref[1:2, :]).astype(BF)


def expert_pass(x, dy, sel, wr, wg, wu, wd, tile):
    slots, width = x.shape
    part = wg[0].shape[1]
    ff = WS * part
    row = lambda w: pl.BlockSpec((tile, w), lambda i: (i, 0))
    once = lambda a: pl.BlockSpec(a.shape, lambda i: (0, 0))
    return pl.pallas_call(
        functools.partial(expert_body, width, ff),
        grid=(slots // tile,),
        in_specs=[row(width), row(width + 128), once(sel), once(wr)]
        + [once(a) for a in (*wg, *wu, *wd)],
        out_specs=[row(width + 128), row(ff), row(2 * ff), row(128)],
        out_shape=[
            jax.ShapeDtypeStruct((slots, width + 128), BF),
            jax.ShapeDtypeStruct((slots, ff), BF),
            jax.ShapeDtypeStruct((slots, 2 * ff), BF),
            jax.ShapeDtypeStruct((slots, 128), F32),
        ],
        scratch_shapes=[pltpu.VMEM((width, 2 * ff + 128), BF), pltpu.VMEM((ff, width), BF)],
        compiler_params=pltpu.CompilerParams(vmem_limit_bytes=VM),
        cost_estimate=pl.CostEstimate(
            flops=10 * slots * width * ff, bytes_accessed=9 * slots * width, transcendentals=0
        ),
        name="expert_pass",
    )(x, dy, sel, wr, *wg, *wu, *wd)


def in_slope_body(x_ref, dgu_ref, own_g, own_u, *peers):
    part = own_g.shape[1]
    ff = WS * part
    gu = tdot(x_ref[...], dgu_ref[...])
    own_g[...] = gu[:, :part]
    own_u[...] = gu[:, ff : ff + part]
    for k in (1, 2, 3):
        peers[k - 1][0] = gu[:, k * part : (k + 1) * part].astype(BF)
        peers[k - 1][1] = gu[:, ff + k * part : ff + (k + 1) * part].astype(BF)


def in_slopes(x, dgu, tile=256):
    slots, width = x.shape
    part = dgu.shape[1] // (2 * WS)
    tall = pl.BlockSpec((tile, part), lambda i: (i, 0))
    pair = pl.BlockSpec((2, tile, part), lambda i: (0, i, 0))
    return pl.pallas_call(
        in_slope_body,
        grid=(width // tile,),
        in_specs=[pl.BlockSpec((slots, tile), lambda i: (0, i)), whole(dgu.shape)],
        out_specs=[tall, tall] + [pair] * 3,
        out_shape=[sds((width, part), F32)] * 2 + [sds((2, width, part), BF)] * 3,
        compiler_params=pltpu.CompilerParams(vmem_limit_bytes=VM),
        cost_estimate=pl.CostEstimate(
            flops=2 * slots * width * dgu.shape[1],
            bytes_accessed=4 * slots * width,
            transcendentals=0,
        ),
        name="in_slopes",
    )(x, dgu)


def out_slope_body(h_ref, dy_ref, gate_ref, *refs):
    wd = refs[0:4]
    y_ref, own_d = refs[4:6]
    part = own_d.shape[0]
    d_y = (gate_ref[:, 0:1] * dy_ref[...].astype(F32)).astype(BF)
    dn = tdot(h_ref[...], d_y)
    own_d[...] = dn[:part]
    for k in (1, 2, 3):
        refs[5 + k][...] = dn[k * part : (k + 1) * part].astype(BF)
    y_ref[...] = dot(h_ref[...], jnp.concatenate([w[...] for w in wd], axis=0)).astype(BF)


def out_slopes(h, dy, gate, wd, tile=256):
    slots, ff = h.shape
    width = wd[0].shape[1]
    part = ff // WS
    col = pl.BlockSpec((slots, tile), lambda i: (0, i))
    flat = pl.BlockSpec((part, tile), lambda i: (0, i))
    return pl.pallas_call(
        out_slope_body,
        grid=(width // tile,),
        in_specs=[whole(h.shape), col, whole(gate.shape)] + [flat] * WS,
        out_specs=[col, flat] + [flat] * 3,
        out_shape=[sds((slots, width), BF), sds((part, width), F32)]
        + [sds((part, width), BF)] * 3,
        compiler_params=pltpu.CompilerParams(vmem_limit_bytes=VM),
        cost_estimate=pl.CostEstimate(
            flops=4 * slots * width * ff, bytes_accessed=4 * slots * width, transcendentals=0
        ),
        name="out_slopes",
    )(h, dy, gate, *wd)


def finish_body(experts, place_ref, a_ref, b_ref, ao_ref, bo_ref, *refs):
    q_ref, k_ref, v_ref, r_ref, g_ref, o_ref, s_ref = refs
    turn = pl.program_id(0)
    second = place_ref[1] == 1
    rows = q_ref.shape[0]
    half = a_ref.shape[3]
    kv = k_ref.shape[1]
    mine = a_ref[:, 0].astype(F32).reshape(rows, half)
    twin = b_ref[:, 0].astype(F32).reshape(rows, half)
    q_ref[...] = jnp.where(second, twin, mine)
    rest = jnp.where(second, mine, twin)
    k_ref[...] = rest[:, :kv]
    v_ref[...] = rest[:, kv : 2 * kv]

    @pl.when(turn == 0)
    def _():
        s_ref[...] = rest[:, 2 * kv :]

    @pl.when(turn > 0)
    def _():
        s_ref[...] += rest[:, 2 * kv :]

    @pl.when(turn == WS - 1)
    def _():
        turned = s_ref[...].T
        r_ref[...] = turned[:experts]
        g_ref[...] = turned[experts : experts + 8]

    mine = ao_ref[:, 0].astype(F32).reshape(rows, half)
    twin = bo_ref[:, 0].astype(F32).reshape(rows, half)
    o_ref[...] = jnp.where(second == (turn < 2), twin, mine)


def finish(experts, place, mine, twin):
    chips, sets, step, half = mine.shape
    rows = chips * step
    first = pl.BlockSpec((chips, 1, step, half), lambda i, p: (0, i, 0, 0))
    later = pl.BlockSpec((chips, 1, step, half), lambda i, p: (0, WS + i % 2, 0, 0))
    turned = lambda i, p: (0, lax.rem(p[0] + i, WS))
    kv = (half - 128) // 2
    S = jax.ShapeDtypeStruct
    return pl.pallas_call(
        functools.partial(finish_body, experts),
        grid_spec=pltpu.PrefetchScalarGridSpec(
            num_scalar_prefetch=1,
            grid=(WS,),
            in_specs=[first, first, later, later],
            out_specs=[
                pl.BlockSpec((rows, half), turned),
                pl.BlockSpec((rows, kv), turned),
                pl.BlockSpec((rows, kv), turned),
                whole((experts, rows)),
                whole((8, rows)),
                pl.BlockSpec((rows, half), lambda i, p: (0, i)),
            ],
            scratch_shapes=[pltpu.VMEM((rows, 128), F32)],
        ),
        out_shape=[
            S((rows, WS * half), F32),
            S((rows, WS * kv), F32),
            S((rows, WS * kv), F32),
            S((experts, rows), F32),
            S((8, rows), F32),
            S((rows, WS * half), F32),
        ],
        compiler_params=pltpu.CompilerParams(vmem_limit_bytes=VM),
        cost_estimate=pl.CostEstimate(flops=0, bytes_accessed=16 * rows * WS * half, transcendentals=0),
        name="finish",
    )(place, mine, twin, mine, twin)


def whole(shape):
    return pl.BlockSpec(shape, lambda *_: (0,) * len(shape))


def sds(shape, kind):
    return jax.ShapeDtypeStruct(shape, kind)


def one_step(body, name, scalars, arrays, outs, scratch, flops):
    moved = sum(a.size * a.dtype.itemsize for a in arrays)
    return pl.pallas_call(
        body,
        in_specs=[pl.BlockSpec(memory_space=pltpu.SMEM)] * len(scalars)
        + [pl.BlockSpec(memory_space=pltpu.VMEM)] * len(arrays),
        out_specs=[pl.BlockSpec(memory_space=pltpu.VMEM)] * len(outs),
        out_shape=outs,
        scratch_shapes=scratch,
        compiler_params=pltpu.CompilerParams(vmem_limit_bytes=VM),
        cost_estimate=pl.CostEstimate(flops=flops, bytes_accessed=moved, transcendentals=0),
        name=name,
    )(*scalars, *arrays)


def other_half(v):
    lanes = v.shape[1]
    low = lax.broadcasted_iota(jnp.int32, v.shape, 1) % HEAD < HEAD // 2
    ahead = pltpu.roll(v, lanes - HEAD // 2, 1)
    behind = pltpu.roll(v, HEAD // 2, 1)
    return jnp.where(low, ahead, behind)


def wide(ref, times):
    return jnp.concatenate([ref[...]] * times, axis=1)


def rms(x):
    return lax.rsqrt(jnp.mean(x * x, axis=1, keepdims=True) + EPS)


def column_sum(m, lane):
    hi, lo = split(m)
    pick = (lax.broadcasted_iota(jnp.int32, (m.shape[0], 128), 1) == lane).astype(F32).astype(BF)
    return tdot(hi, pick) + tdot(lo, pick)


def pack_body(experts, x_ref, wq, wk, wv, wr, na, nm, *outs):
    small = outs[WS + 1]
    me, core = lax.axis_index("ws"), lax.rem(lax.axis_index("exp"), 2)
    rows = x_ref.shape[0]
    strip = wq.shape[0] // 2
    q_w, kv_w = wq.shape[1] // WS, wk.shape[1] // WS
    shard = wq.shape[0]
    norms = [n[...].astype(F32).reshape(1, shard) for n in (na, nm)]
    few = [wr[...].astype(F32), *norms, jnp.zeros((126 - experts, shard), F32)]
    small[...] = jnp.concatenate(few, axis=0).T.astype(BF)

    def place(out, top, left, side, d, start, count):
        part = pl.ds(pl.multiple_of(side * strip + start, 32), count)
        here = slice(top, top + count)
        spot = pl.ds(pl.multiple_of(d * kv_w, 128), kv_w)
        out[here, left : left + q_w] = wq[part, pl.ds(pl.multiple_of(d * q_w, 128), q_w)]
        out[here, left + q_w : left + q_w + kv_w] = wk[part, spot]
        out[here, left + q_w + kv_w : left + q_w + 2 * kv_w] = wv[part, spot]
        out[here, left + q_w + 2 * kv_w : left + q_w + 2 * kv_w + 128] = small[part, :]

    for r in range(WS + 1):
        side = core if r < WS else 1 - core
        d = lax.rem(me + WS - r % WS, WS)
        if r == 2:
            outs[r][:rows, :] = x_ref[...]
            for half in range(2):
                left = half * (q_w + 2 * kv_w + 128)
                place(outs[r], rows, left, side, d, half * strip // 2, strip // 2)
        else:
            place(outs[r], 0, 0, side, d, 0, strip)


def pack(experts, x, wq, wk, wv, wr, na, nm):
    shard = wq.shape[0]
    rows, width = x.shape
    wide_w = (wq.shape[1] + 2 * wk.shape[1]) // WS + 128
    outs = [sds((shard // 2, wide_w), BF)] * (WS + 1)
    outs[2] = sds((rows + shard // 4, 2 * wide_w), BF)
    return one_step(
        functools.partial(pack_body, experts),
        "pack",
        [],
        [x, wq, wk, wv, wr, na, nm],
        outs,
        [pltpu.VMEM((shard, 128), BF)],
        0,
    )


def dispatch_body(experts, routes_ref, cot_ref, send_ref, slot_ref, chosen_ref, spread_ref, both):
    rows, width = cot_ref.shape
    slots = slot_ref.shape[1]
    tile = send_ref.shape[0]
    step = pl.program_id(0)

    @pl.when(step == 0)
    def _():
        name = lax.broadcasted_iota(jnp.int32, (128, rows), 0)
        named = jnp.zeros((128, rows), F32)
        for k in range(routes_ref.shape[0]):
            named = named + (routes_ref[k : k + 1, :] == name).astype(F32)
        chosen = named.T
        chosen_ref[...] = chosen.astype(BF)
        both[:, :width] = cot_ref[...]
        both[:, width:] = chosen.astype(BF)
        this = lax.broadcasted_iota(jnp.int32, (rows, rows), 0)
        that = lax.broadcasted_iota(jnp.int32, (rows, rows), 1)
        rank = dot((that < this).astype(F32).astype(BF), chosen.astype(BF))
        col = lax.broadcasted_iota(jnp.int32, (128, slots), 1)
        first = lax.broadcasted_iota(jnp.int32, (128, slots), 0) * CAP
        spread = jnp.where((col >= first) & (col < first + CAP), 1.0, 0.0)
        spread_ref[...] = spread.astype(BF)
        spot = dot((chosen * (rank + 1.0)).astype(BF), spread.astype(BF))
        want = jnp.sum(spread * (col - first + 1).astype(F32), axis=0, keepdims=True)
        slot_ref[...] = jnp.where(spot == want, 1.0, 0.0).astype(BF)

    part = slot_ref[:, pl.ds(pl.multiple_of(step * tile, tile), tile)]
    send_ref[...] = tdot(part, both[...]).astype(BF)


def dispatch(experts, routes, cot, tile=512):
    rows, width = cot.shape
    slots = experts * CAP
    outs = [
        sds((slots, width + 128), BF),
        sds((rows, slots), BF),
        sds((rows, 128), BF),
        sds((128, slots), BF),
    ]
    return pl.pallas_call(
        functools.partial(dispatch_body, experts),
        grid=(slots // tile,),
        in_specs=[whole((routes.shape[1], rows)), whole((rows, width))],
        out_specs=[pl.BlockSpec((tile, width + 128), lambda i: (i, 0))]
        + [whole(o.shape) for o in outs[1:]],
        out_shape=outs,
        scratch_shapes=[pltpu.VMEM((rows, width + 128), BF)],
        compiler_params=pltpu.CompilerParams(vmem_limit_bytes=VM),
        cost_estimate=pl.CostEstimate(
            flops=2 * rows * width * slots, bytes_accessed=3 * slots * width, transcendentals=0
        ),
        name="dispatch",
    )(routes.T, cot)


def attend_rows(qkv_ref, bias_ref, o_ref, lse_ref, start, q_w, kv_w):
    rows = o_ref.shape[0]
    group = q_w // kv_w
    here = slice(start, start + rows)
    for h in range(q_w // HEAD):
        at = h // group * HEAD
        q = qkv_ref[here, h * HEAD : (h + 1) * HEAD]
        k = qkv_ref[:, q_w + at : q_w + at + HEAD]
        v = qkv_ref[:, q_w + kv_w + at : q_w + kv_w + at + HEAD]
        s = dot_t(q, k) * HEAD ** (-0.5) + bias_ref[here, :]
        peak = jnp.max(s, axis=1, keepdims=True)
        p = jnp.exp(s - peak)
        total = jnp.sum(p, axis=1, keepdims=True)
        lse_ref[:, h : h + 1] = peak + jnp.log(total)
        o_ref[:, h * HEAD : (h + 1) * HEAD] = dot((p / total).astype(BF), v).astype(BF)


def attend_body(experts, place_ref, *refs):
    xs, own, twin = refs[0:4], refs[4:8], refs[8:12]
    cos_ref, sin_ref, bias_ref, wo_ref = refs[12:16]
    h1_ref, qkv_ref, o_ref, lse_ref, w_ref, small_ref, rows_ref = refs[16:23]
    parts = refs[23:26]
    me, core = place_ref[0], place_ref[1]
    rows = xs[0].shape[0]
    strip = own[0].shape[0]
    wide_w = own[0].shape[1]
    q_w = o_ref.shape[1]
    qkv_w = qkv_ref.shape[1]
    kv_w = (qkv_w - q_w) // 2
    for r in range(WS):
        base = lax.rem(me + r, WS) * (2 * strip)
        for source, side in ((own[r], core), (twin[r], 1 - core)):
            folds = source.shape[1] // wide_w
            count = strip // folds
            for f in range(folds):
                left = f * wide_w
                spot = pl.ds(pl.multiple_of(base + side * strip + f * count, 32), count)
                w_ref[spot, :] = source[:, left : left + qkv_w]
                small_ref[spot, :] = source[:, left + qkv_w : left + wide_w]
    turned = small_ref[...].astype(F32).T
    rows_ref[...] = jnp.concatenate(
        [turned[experts : experts + 2], jnp.zeros((6, turned.shape[1]), F32)], axis=0
    )
    gain = turned[experts : experts + 1]
    for r in range(WS):
        x = xs[r][:rows, :].astype(F32)
        h1_ref[r * rows : (r + 1) * rows, :] = (x * rms(x) * gain).astype(BF)
    qkv = dot(h1_ref[...], w_ref[...])
    qk = qkv[:, : q_w + kv_w]
    times = (q_w + kv_w) // 128
    qk = qk * wide(cos_ref, times) + other_half(qk) * wide(sin_ref, times)
    qkv_ref[:, : q_w + kv_w] = qk.astype(BF)
    qkv_ref[:, q_w + kv_w :] = qkv[:, q_w + kv_w :].astype(BF)
    attend_rows(qkv_ref, bias_ref, o_ref, lse_ref, rows, q_w, kv_w)
    for r in range(3):
        part = dot(o_ref[r * rows : (r + 1) * rows, :], wo_ref[...])
        parts[r][...] = part.astype(BF)


def attend(experts, place, xs, own, twin, cos, sin, bias, wo):
    rows, width = xs[0].shape
    tree = rows * WS
    q_w, qkv_w = wo.shape[0], own[0].shape[1] - 128
    outs = [
        sds((tree, width), BF),
        sds((tree, qkv_w), BF),
        sds((tree - rows, q_w), BF),
        sds((tree - rows, 128), F32),
        sds((width, qkv_w), BF),
        sds((width, 128), BF),
        sds((8, width), F32),
    ] + [sds((rows, width), BF)] * 3
    flops = 40 * tree * width * (qkv_w + q_w)
    return one_step(
        functools.partial(attend_body, experts),
        "attend",
        [place],
        [*xs, *own, *twin, cos, sin, bias, wo],
        outs,
        [],
        flops,
    )


def attend_own_body(qkv_ref, bias_ref, wo_ref, o_ref, lse_ref, part_ref):
    q_w = o_ref.shape[1]
    kv_w = (qkv_ref.shape[1] - q_w) // 2
    attend_rows(qkv_ref, bias_ref, o_ref, lse_ref, 0, q_w, kv_w)
    part_ref[...] = dot(o_ref[...], wo_ref[...])


def attend_own(rows, qkv, bias, wo):
    q_w, width = wo.shape
    outs = [sds((rows, q_w), BF), sds((rows, 128), F32), sds((rows, width), F32)]
    flops = 2 * rows * width * q_w + 4 * rows * qkv.shape[0] * q_w
    return one_step(attend_own_body, "attend_own", [], [qkv, bias, wo], outs, [], flops)


def enter_body(x_ref, p0, p1, p2, p3, rows_ref, slot_ref, x2_ref, h2_ref, send_ref):
    @pl.when(pl.program_id(0) == 0)
    def _():
        x2 = x_ref[...].astype(F32) + p0[...]
        for p in (p1, p2, p3):
            x2 = x2 + p[...].astype(F32)
        x2_ref[...] = x2
        h2_ref[...] = (x2 * rms(x2) * rows_ref[1:2, :]).astype(BF)

    send_ref[...] = tdot(slot_ref[...], h2_ref[...]).astype(BF)


def enter(x, parts, rows, to_slot, tile=512):
    n, width = x.shape
    slots = to_slot.shape[1]
    arrays = [x, *parts, rows]
    return pl.pallas_call(
        enter_body,
        grid=(slots // tile,),
        in_specs=[whole(a.shape) for a in arrays] + [pl.BlockSpec((n, tile), lambda i: (0, i))],
        out_specs=[
            whole((n, width)),
            whole((n, width)),
            pl.BlockSpec((tile, width), lambda i: (i, 0)),
        ],
        out_shape=[sds((n, width), F32), sds((n, width), BF), sds((slots, width), BF)],
        compiler_params=pltpu.CompilerParams(vmem_limit_bytes=VM),
        cost_estimate=pl.CostEstimate(
            flops=2 * n * width * slots, bytes_accessed=3 * slots * width, transcendentals=0
        ),
        name="enter",
    )(*arrays, to_slot)


def gate_body(h2_ref, router_ref, slot_ref, chosen_ref, spread_ref, gates_ref, gs_ref):
    logits = dot(h2_ref[...], router_ref[...])
    mask = chosen_ref[...].astype(F32) > 0.5
    logits = jnp.where(mask, logits, MASKED)
    lifted = jnp.where(mask, jnp.exp(logits - jnp.max(logits, axis=1, keepdims=True)), 0.0)
    gates = lifted / jnp.maximum(jnp.sum(lifted, axis=1, keepdims=True), 1e-30)
    gates_ref[...] = gates
    hi, lo = split(gates)
    on_slots = dot(hi, spread_ref[...]) + dot(lo, spread_ref[...])
    hi, lo = split(on_slots * slot_ref[...].astype(F32))
    rows = gates.shape[0]
    gs_ref[:rows, :] = hi
    gs_ref[rows:, :] = lo


def gate_terms(h2, router, to_slot, chosen, spread):
    n, slots = to_slot.shape
    outs = [sds((n, 128), F32), sds((2 * n, slots), BF)]
    arrays = [h2, router, to_slot, chosen, spread]
    return one_step(gate_body, "gate_terms", [], arrays, outs, [], 8 * n * 128 * slots)


def leave_body(experts, back_ref, slot_ref, gates_ref, router_ref, x2_ref, rows_ref, cot_ref, *outs):
    dx2_ref, da_ref, dh2_ref, dl_ref, sum_ref = outs
    width = x2_ref.shape[1]
    step = pl.program_id(0)
    more = dot(slot_ref[...], back_ref[...])

    @pl.when(step == 0)
    def _():
        sum_ref[...] = more

    @pl.when(step > 0)
    def _():
        sum_ref[...] += more

    @pl.when(step == pl.num_programs(0) - 1)
    def _():
        tail = sum_ref[:, width:]
        dgate = tail + pltpu.roll(tail, 128 - experts, 1)
        gates = gates_ref[...]
        dl = gates * (dgate - jnp.sum(gates * dgate, axis=1, keepdims=True))
        dl_ref[...] = dl
        hi, lo = split(dl)
        dh2 = sum_ref[:, :width] + dot_t(hi, router_ref[...]) + dot_t(lo, router_ref[...])
        dh2_ref[...] = dh2
        x2 = x2_ref[...]
        scale, gain = rms(x2), rows_ref[1:2, :]
        inner = jnp.mean(gain * dh2 * x2, axis=1, keepdims=True)
        dx2 = cot_ref[...].astype(F32) + scale * gain * dh2 - x2 * scale * scale * scale * inner
        dx2_ref[...] = dx2
        da_ref[...] = dx2.astype(BF)


def leave(experts, back, to_slot, gates, router, x2, rows, cot, tile=512):
    n, width = x2.shape
    slots = back.shape[0]
    outs = [sds((n, width), F32), sds((n, width), BF), sds((n, width), F32), sds((n, 128), F32)]
    rest = [gates, router, x2, rows, cot]
    return pl.pallas_call(
        functools.partial(leave_body, experts),
        grid=(slots // tile,),
        in_specs=[
            pl.BlockSpec((tile, width + 128), lambda i: (i, 0)),
            pl.BlockSpec((n, tile), lambda i: (0, i)),
        ]
        + [whole(a.shape) for a in rest],
        out_specs=[whole(o.shape) for o in outs],
        out_shape=outs,
        scratch_shapes=[pltpu.VMEM((n, width + 128), F32)],
        compiler_params=pltpu.CompilerParams(vmem_limit_bytes=VM),
        cost_estimate=pl.CostEstimate(
            flops=2 * n * width * slots, bytes_accessed=3 * slots * width, transcendentals=0
        ),
        name="leave",
    )(back, to_slot, *rest)


def small_body(experts, h2_ref, dl_ref, dh2_ref, x2_ref, out_ref):
    hi, lo = split(dl_ref[...])
    h2, x2 = h2_ref[...], x2_ref[...]
    out_ref[...] = tdot(h2, hi) + tdot(h2, lo) + column_sum(dh2_ref[...] * x2 * rms(x2), experts)


def small_slopes(experts, h2, dl, dh2, x2):
    n, width = x2.shape
    return one_step(
        functools.partial(small_body, experts),
        "small_slopes",
        [],
        [h2, dl, dh2, x2],
        [sds((width, 128), F32)],
        [],
        8 * n * width * 128,
    )[0]


def attend_back_body(experts, place_ref, *refs):
    das, xs = refs[0:4], refs[4:8]
    wo_ref, qkv_ref, o_own, o_far, lse_own, lse_far, h1_ref, w_ref = refs[8:16]
    cos_ref, sin_ref, bias_ref, small_ref = refs[16:20]
    keep_ref, give_ref = refs[20:22]
    parts = refs[22:26]
    da, do, dqk, dqkv, o_ref, lse_ref = refs[26:32]
    core = place_ref[1]
    rows = xs[0].shape[0]
    q_w, qkv_w = o_ref.shape[1], qkv_ref.shape[1]
    kv_w = (qkv_w - q_w) // 2
    group = q_w // kv_w
    scale = HEAD ** (-0.5)
    for r in range(WS):
        da[r * rows : (r + 1) * rows, :] = das[r][...]
    o_ref[:rows, :] = o_own[...]
    o_ref[rows:, :] = o_far[...]
    lse_ref[:rows, :] = lse_own[...]
    lse_ref[rows:, :] = lse_far[...]
    do[...] = dot_t(da[...], wo_ref[...]).astype(BF)
    for n in range(kv_w // HEAD):
        at = n * HEAD
        k = qkv_ref[:, q_w + at : q_w + at + HEAD]
        v = qkv_ref[:, q_w + kv_w + at : q_w + kv_w + at + HEAD]
        dk, dv = None, None
        for h in range(n * group, (n + 1) * group):
            q = qkv_ref[:, h * HEAD : (h + 1) * HEAD]
            doh = do[:, h * HEAD : (h + 1) * HEAD]
            p = jnp.exp(dot_t(q, k) * scale + bias_ref[...] - lse_ref[:, h : h + 1])
            dp = dot_t(doh, v)
            delta = jnp.sum(p * dp, axis=1, keepdims=True)
            ds = (p * (dp - delta)).astype(BF)
            dqk[:, h * HEAD : (h + 1) * HEAD] = dot(ds, k) * scale
            more_k, more_v = tdot(ds, q), tdot(p.astype(BF), doh)
            dk = more_k if dk is None else dk + more_k
            dv = more_v if dv is None else dv + more_v
        dqk[:, q_w + at : q_w + at + HEAD] = dk * scale
        dqkv[:, q_w + kv_w + at : q_w + kv_w + at + HEAD] = dv.astype(BF)
    dqkv[:, qkv_w:] = jnp.zeros((da.shape[0], 128), BF)
    d = dqk[...]
    times = (q_w + kv_w) // 128
    d = d * wide(cos_ref, times) - other_half(d) * wide(sin_ref, times)
    dqkv[:, : q_w + kv_w] = d.astype(BF)
    small = small_ref[...]
    for r in range(WS):
        dh1 = dot_t(dqkv[r * rows : (r + 1) * rows, :qkv_w], w_ref[...])
        parts[r][...] = dh1.astype(parts[r].dtype)
        x = xs[r][:rows, :].astype(F32)
        small = small + column_sum(dh1 * x * rms(x), experts + 1)
    half = keep_ref.shape[3]
    chips, step = keep_ref.shape[0], keep_ref.shape[2]
    count = chips * step

    def put(i, first, second):
        kept = jnp.where(core == 0, first, second)
        given = jnp.where(core == 0, second, first)
        keep_ref[:, i] = kept.reshape(chips, step, half)
        give_ref[:, i] = given.reshape(chips, step, half).astype(BF)

    for i in range(WS):
        both = tdot(h1_ref[:, i * count : (i + 1) * count], dqkv[...])
        mine = small[i * count : (i + 1) * count]
        second = jnp.concatenate([both[:, half : 2 * half - 128], both[:, 2 * half - 128 :] + mine], axis=1)
        put(i, both[:, :half], second)
    slope = tdot(o_ref[...], da[...])
    for i in range(2):
        put(WS + i, slope[:, i * half : (i + 1) * half], slope[:, (2 + i) * half : (3 + i) * half])


def attend_back(experts, place, das, xs, wo, qkv, os, lses, h1, w, cos, sin, bias, small):
    rows, width = xs[0].shape
    tree = rows * WS
    q_w, qkv_w = wo.shape[0], qkv.shape[1]
    half = (qkv_w + 128) // 2
    load = (CHIPS, WS + 2, width // WS // CHIPS, half)
    outs = [sds(load, F32), sds(load, BF), sds((rows, width), F32)] + [sds((rows, width), BF)] * 3
    scratch = [
        pltpu.VMEM((tree, width), BF),
        pltpu.VMEM((tree, q_w), BF),
        pltpu.VMEM((tree, (q_w + qkv_w) // 2), F32),
        pltpu.VMEM((tree, qkv_w + 128), BF),
        pltpu.VMEM((tree, q_w), BF),
        pltpu.VMEM((tree, 128), F32),
    ]
    flops = 4 * tree * width * (qkv_w + q_w) + 10 * tree * tree * q_w
    return one_step(
        functools.partial(attend_back_body, experts),
        "attend_back",
        [place],
        [*das, *xs, wo, qkv, *os, *lses, h1, w, cos, sin, bias, small],
        outs,
        scratch,
        flops,
    )


def shards(
    tokens,
    cotangent,
    seg_lengths,
    parents,
    routes,
    norm_attn,
    w_query,
    w_key,
    w_value,
    w_out,
    norm_moe,
    w_router,
    w_gate,
    w_up,
    w_down,
):
    me = lax.axis_index("ws")
    expert = lax.axis_index("exp")
    core = expert % 2
    place = jnp.stack([me, core]).astype(jnp.int32)
    rows, width = tokens.shape
    shard = width // WS
    strip = shard // 2
    experts = 2 * CHIPS
    q_w, kv_w = HEADS // WS * HEAD, KV_HEADS // WS * HEAD
    slots = experts * CAP

    def gathered(v):
        return [v] + [from_peer(v, k) for k in (1, 2, 3)]

    pieces = pack(
        experts, tokens, w_query, w_key, w_value, w_router.T, norm_attn, norm_moe
    )
    came = [None] + [from_peer(pieces[k], k) for k in (1, 2, 3)]
    mine, came[1] = lax.optimization_barrier((tokens, came[1]))
    xs = [tokens, from_peer(mine, 1), came[2], from_peer(mine, 3)]
    own = [pieces[0], came[1], came[2][rows:], came[3]]

    lane = jnp.arange(128, dtype=jnp.int32)
    row_id = jnp.arange(rows, dtype=jnp.int32)
    dy_send, to_slot, chosen, spread = dispatch(experts, routes, cotangent)
    dy_send = dy_send.reshape(experts, CAP, width + 128)
    dy_slots = lax.all_to_all(dy_send, "exp", 0, 0, tiled=True).reshape(slots, width + 128)

    order = (
        ((me + jnp.arange(WS, dtype=jnp.int32)) % WS)[:, None] * rows + row_id[None, :]
    ).reshape(-1)
    visible, position = tree_layout(seg_lengths[0], parents[0], order)
    bias = jnp.where(visible, 0.0, MASKED).astype(F32)
    inverse = THETA ** (-(lane % (HEAD // 2)).astype(F32) * 2.0 / HEAD)
    angles = position.astype(F32)[:, None] * inverse[None, :]
    cosines = jnp.cos(angles)
    sines = jnp.where((lane % HEAD < HEAD // 2)[None, :], -1.0, 1.0) * jnp.sin(angles)
    own[1], bias, cosines, sines = lax.optimization_barrier((own[1], bias, cosines, sines))
    twin = [pieces[WS]] + [other_core(own[k]) for k in (1, 2, 3)]
    h1, qkv, o_far, lse_far, w_qkv, small_full, gains, *parts = attend(
        experts, place, xs, own, twin, cosines, sines, bias, w_out
    )
    o_own, lse_own, part_own = attend_own(rows, qkv, bias, w_out)
    sums = [part_own] + [to_peer(parts[k - 1], k) for k in (1, 2, 3)]
    x2, h2, x_send = enter(tokens, sums, gains, to_slot)
    x_send, wg_own, wu_own, wd_own = lax.optimization_barrier(
        (x_send, w_gate[0], w_up[0], w_down[0])
    )
    x_slots = lax.all_to_all(
        x_send.reshape(experts, CAP, width), "exp", 0, 0, tiled=True
    ).reshape(slots, width)

    sel = jnp.concatenate(
        [
            (lane == expert).astype(F32)[None],
            (lane == expert + experts).astype(F32)[None],
            jnp.zeros((6, 128), F32),
        ],
        axis=0,
    )
    wd = gathered(wd_own)
    gates, gate_slots = gate_terms(h2, small_full, to_slot, chosen, spread)
    wd[1], gates, gate_slots = lax.optimization_barrier((wd[1], gates, gate_slots))
    dx_send, hidden, d_gu, slot_gates = expert_pass(
        x_slots, dy_slots, sel, small_full, gathered(wg_own), gathered(wu_own), wd, 256
    )
    dx_back = lax.all_to_all(
        dx_send.reshape(experts, CAP, width + 128), "exp", 0, 0, tiled=True
    ).reshape(slots, width + 128)

    own_g, own_u, gu1, gu2, gu3 = in_slopes(x_slots, d_gu)
    gu1, gu2, gu3 = to_peer(gu1, 1), to_peer(gu2, 2), to_peer(gu3, 3)
    hidden, gu1 = lax.optimization_barrier((hidden, gu1))
    y, own_d, dn1, dn2, dn3 = out_slopes(hidden, dy_slots, slot_gates, wd)
    dn1, dn2, dn3 = to_peer(dn1, 1), to_peer(dn2, 2), to_peer(dn3, 3)
    dx_back, y, gu1, dn1, gu2, dn2, gu3, dn3 = lax.optimization_barrier(
        (dx_back, y, gu1, dn1, gu2, dn2, gu3, dn3)
    )
    y_back = lax.all_to_all(y.reshape(experts, CAP, width), "exp", 0, 0, tiled=True).reshape(
        slots, width
    )

    dx2, d_a, dh2, dl = leave(
        experts, dx_back, to_slot, gates, small_full, x2, gains, cotangent
    )
    das = gathered(d_a)
    small_terms = small_slopes(experts, h2, dl, dh2, x2)
    grad_gu = jnp.stack([own_g, own_u]) + gu1.astype(F32) + gu2.astype(F32) + gu3.astype(F32)
    grad_wg, grad_wu = grad_gu[0][None], grad_gu[1][None]
    grad_wd = (own_d + dn1.astype(F32) + dn2.astype(F32) + dn3.astype(F32))[None]
    das, grad_wg, grad_wu, grad_wd = lax.optimization_barrier((das, grad_wg, grad_wu, grad_wd))
    keep, give, *slopes = attend_back(
        experts,
        place,
        das,
        xs,
        w_out,
        qkv,
        (o_own, o_far),
        (lse_own, lse_far),
        h1,
        w_qkv,
        cosines,
        sines,
        bias,
        small_terms,
    )
    sent = (keep + other_core(give).astype(F32)).astype(BF)
    sent, y_back = lax.optimization_barrier((sent, y_back))
    step = shard // CHIPS
    both = dot(gate_slots, y_back)
    layer_out = (x2 + both[:rows] + both[rows:]).astype(BF)
    got = same_core(sent)
    slopes = [slopes[0]] + [to_peer(slopes[k], k) for k in (1, 2, 3)]
    got, layer_out, slopes = lax.optimization_barrier((got, layer_out, slopes))
    dh1 = slopes[0]
    for k in (1, 2, 3):
        dh1 = dh1 + slopes[k].astype(F32)
    resid = tokens.astype(F32)
    scale = lax.rsqrt(jnp.mean(resid * resid, axis=-1, keepdims=True) + EPS)
    inner = jnp.mean(gains[0:1] * dh1 * resid, axis=-1, keepdims=True)
    grad_tokens = dx2 + scale * gains[0:1] * dh1 - resid * scale * scale * scale * inner

    total = jnp.sum(got.astype(F32), axis=0).astype(BF)
    final = jnp.stack(
        [lax.dynamic_index_in_dim(total, me, 0, False)]
        + [
            from_peer(lax.dynamic_index_in_dim(total, (me - k) % WS, 0, False), k)
            for k in (1, 2, 3)
        ]
        + [total[WS], total[WS + 1]]
    )
    spread_out = same_core(jnp.broadcast_to(final, (CHIPS,) + final.shape))
    twin_out = other_core(spread_out)
    sum_query, sum_key, sum_value, sum_router, sum_gains, sum_out = finish(
        experts, place, spread_out, twin_out
    )

    return (
        layer_out,
        grad_tokens,
        sum_gains[1],
        sum_query,
        sum_key,
        sum_value,
        sum_out,
        sum_gains[0],
        sum_router.T,
        grad_wg,
        grad_wu,
        grad_wd,
    )


def solution(mesh):
    rows = P(("exp", "ws"), None)
    placed = (
        rows,
        rows,
        P("exp", None),
        P("exp", None),
        rows,
        P("ws"),
        P("ws", None),
        P("ws", None),
        P("ws", None),
        P("ws", None),
        P("ws"),
        P("ws", None),
        P("exp", None, "ws"),
        P("exp", None, "ws"),
        P("exp", "ws", None),
    )
    return jax.shard_map(
        shards,
        mesh=mesh,
        in_specs=placed,
        out_specs=(
            rows,
            rows,
            P("ws"),
            P("ws", None),
            P("ws", None),
            P("ws", None),
            P("ws", None),
            P("ws"),
            P("ws", None),
            P("exp", None, "ws"),
            P("exp", None, "ws"),
            P("exp", "ws", None),
        ),
        check_vma=False,
    )
```
